128 devices in a mesh: seq: 16 (over z, x_lo, core), blk: 8 (over y, x_hi).
Axes of the slice: x: 4 (x_hi: 2, x_lo: 2; x = x_hi * 2 + x_lo), y: 4, z: 4, core: 2. Of those that a mesh axis runs over, the one named last changes fastest.
Arguments:
- tokens: bfloat16 [16384, 1024], P(('seq', 'blk')), may hold values from -6 to 6
- lengths: int32 [16, 6], P('seq'), may hold values from 1 to 768, as said below
- order: int32 [8, 2], replicated, may hold values from 0 to 15, as said below
- w_query: bfloat16 [1024, 1024], replicated, may hold values from -0.1875 to 0.1875
- w_key: bfloat16 [1024, 1024], replicated, may hold values from -0.1875 to 0.1875
- w_value: bfloat16 [1024, 1024], replicated, may hold values from -0.1875 to 0.1875
- w_out: bfloat16 [1024, 1024], replicated, may hold values from -0.1875 to 0.1875
- w_up: bfloat16 [1024, 4096], replicated, may hold values from -0.1875 to 0.1875
- b_up: float32 [4096], replicated, may hold values from -3 to 3
- w_down: bfloat16 [4096, 1024], replicated, may hold values from -0.09375 to 0.09375
- b_down: float32 [1024], replicated, may hold values from -2 to 2
- gain_attn_in: float32 [1024], replicated, may hold values from 0.25 to 1.75
- gain_attn_out: float32 [1024], replicated, may hold values from 0.25 to 1.75
- gain_mlp_in: float32 [1024], replicated, may hold values from 0.25 to 1.75
- gain_mlp_out: float32 [1024], replicated, may hold values from 0.25 to 1.75
- cotangent: bfloat16 [16384, 1024], P(('seq', 'blk')), may hold values from -6 to 6
Outputs:
- output: bfloat16 [16384, 1024], P(('seq', 'blk'))
- grad_tokens: float32 [16384, 1024], P(('seq', 'blk'))
- grad_w_query: float32 [1024, 1024], P(('seq', 'blk'))
- grad_w_key: float32 [1024, 1024], P(('seq', 'blk'))
- grad_w_value: float32 [1024, 1024], P(('seq', 'blk'))
- grad_w_out: float32 [1024, 1024], P(('seq', 'blk'))
- grad_w_up: float32 [1024, 4096], P(('seq', 'blk'))
- grad_b_up: float32 [4096], P(('seq', 'blk'))
- grad_w_down: float32 [4096, 1024], P(('seq', 'blk'))
- grad_b_down: float32 [1024], P(('seq', 'blk'))
- grad_gain_attn_in: float32 [1024], P(('seq', 'blk'))
- grad_gain_attn_out: float32 [1024], P(('seq', 'blk'))
- grad_gain_mlp_in: float32 [1024], P(('seq', 'blk'))
- grad_gain_mlp_out: float32 [1024], P(('seq', 'blk'))
The draws below stay inside these ranges and needn't reach their ends.
Inputs may be any that keep to these rules, and one draw needn't show every extreme that they name: Row s lists the lengths of the sequences packed in order into group s; its first entry is at least 512, the entries sum to less than 1024, and the positions after their sum are padding. One group has a first sequence of exactly the largest length and a sequence of length 1. `order`: row b holds two blocks p and 15 - p of 64 positions; every block of a group is held once.
All inputs are finite; a program needn't handle non-finite values.
Results may differ from the reference program's by a relative error of at most 0.022.
Values may be sent and summed in bfloat16 or wider, within the bound.
No kernel may reach another device: no remote copies, remote signals or barrier semaphores. Data moves between devices by JAX's collectives and lax.ppermute only.
A program may use at most 192 MiB of HBM per device.

```python
import math
import jax
import jax.numpy as jnp
from jax import lax

D = 1024
HEADS = 16
HEAD = 64
FF = 4096
GROUP = 1024
DOCS = 6
SPLIT = 8
GROUPS = 16
SLAB = 64
TOKENS = 16384


def draw_lengths(key, part):
    key = jax.random.fold_in(key, 11)
    key_long, key_weights, key_pick = jax.random.split(key, 3)
    chosen = jax.random.randint(key_pick, (), 0, GROUPS)
    picked = (jnp.arange(GROUPS, dtype=jnp.int32) == chosen)[:, None]
    longest = GROUP // 2 + jax.random.randint(key_long, (GROUPS, 1), 0, GROUP // 4 + 1)
    longest = jnp.where(picked, GROUP // 2 + GROUP // 4, longest)
    remain = GROUP - longest
    powers = jax.random.randint(key_weights, (GROUPS, DOCS), 0, 7)
    weights = jnp.left_shift(jnp.ones_like(powers), powers)
    total_weight = jnp.sum(weights, axis=1, keepdims=True)
    shares = 1 + (remain - DOCS) * weights[:, :DOCS - 1] // total_weight
    last_col = (jnp.arange(DOCS - 1, dtype=jnp.int32) == DOCS - 2)[None, :]
    shares = jnp.where(picked & last_col, 1, shares)
    return jnp.concatenate([longest, shares], axis=1).astype(jnp.int32)


def draw_order(key, part):
    key = jax.random.fold_in(key, 23)
    key_perm, key_flip = jax.random.split(key)
    pairs = jax.random.permutation(key_perm, SPLIT).astype(jnp.int32)
    flips = jax.random.randint(key_flip, (SPLIT,), 0, 2)
    mirror = 2 * SPLIT - 1 - pairs
    first = jnp.where(flips == 1, mirror, pairs)
    second = jnp.where(flips == 1, pairs, mirror)
    return jnp.stack([first, second], axis=1).astype(jnp.int32)


def level_of(own_key, shape, cuts, low, top_value):
    def one(dim, shards_of):
        steps = jax.random.uniform(jax.random.fold_in(jax.random.fold_in(own_key, 6), dim), (shards_of,), jnp.float32, low / len(cuts), top_value / len(cuts))
        return jnp.repeat(jnp.exp(steps), shape[dim] // shards_of).reshape((-1,) + (1,) * (len(shape) - dim - 1))

    level = one(*cuts[0])
    for cut in cuts[1:]:
        level = level * one(*cut)
    return level


def bell_draw(rng, shape, scale, bound, shards=(), held_as=jnp.bfloat16):
    drawn = scale * jax.random.normal(rng, shape, jnp.float32)
    if shards:
        drawn = drawn * level_of(rng, shape, shards, -0.22, 0.18)
    return jnp.clip(drawn, -bound, bound).astype(held_as)


def setup_inputs(seed: int = 0) -> dict:
    arg_keys = jax.random.split(jax.random.key(seed), 17)
    tokens = bell_draw(arg_keys[0], (TOKENS, D), 1.0, 6.0, ((0, 128),))
    lengths = draw_lengths(jax.random.fold_in(arg_keys[16], 71), 0)
    order = draw_order(jax.random.fold_in(arg_keys[16], 71), 0)
    w_query = bell_draw(arg_keys[3], (D, D), D ** -0.5, 0.1875)
    w_key = bell_draw(arg_keys[4], (D, D), D ** -0.5, 0.1875)
    w_value = bell_draw(arg_keys[5], (D, D), D ** -0.5, 0.1875)
    w_out = bell_draw(arg_keys[6], (D, D), D ** -0.5, 0.1875)
    w_up = bell_draw(arg_keys[7], (D, FF), D ** -0.5, 0.1875)
    b_up = bell_draw(arg_keys[8], (FF,), 0.5, 3.0, (), jnp.float32)
    w_down = bell_draw(arg_keys[9], (FF, D), FF ** -0.5, 0.09375)
    b_down = bell_draw(arg_keys[10], (D,), 0.3, 2.0, (), jnp.float32)
    gain_attn_in = jnp.clip(1.0 + 0.15 * jax.random.normal(arg_keys[11], (D,), jnp.float32), 0.25, 1.75)
    gain_attn_out = jnp.clip(1.0 + 0.15 * jax.random.normal(arg_keys[12], (D,), jnp.float32), 0.25, 1.75)
    gain_mlp_in = jnp.clip(1.0 + 0.15 * jax.random.normal(arg_keys[13], (D,), jnp.float32), 0.25, 1.75)
    gain_mlp_out = jnp.clip(1.0 + 0.15 * jax.random.normal(arg_keys[14], (D,), jnp.float32), 0.25, 1.75)
    cotangent = bell_draw(arg_keys[15], (TOKENS, D), 1.0, 6.0, ((0, 128),))
    return {"tokens": tokens, "lengths": lengths, "order": order, "w_query": w_query, "w_key": w_key, "w_value": w_value, "w_out": w_out, "w_up": w_up, "b_up": b_up, "w_down": w_down, "b_down": b_down, "gain_attn_in": gain_attn_in, "gain_attn_out": gain_attn_out, "gain_mlp_in": gain_mlp_in, "gain_mlp_out": gain_mlp_out, "cotangent": cotangent}


@jax.custom_vjp
def low(v):
    return lax.optimization_barrier(v.astype(jnp.bfloat16)).astype(jnp.float32)

@jax.custom_vjp
def low_back(v):
    return v

def low_keep(v):
    return (low(v), None)

def low_pass(kept, grad):
    return (grad,)

def back_keep(v):
    return (v, None)

def back_low(kept, grad):
    return (low(grad),)
low.defvjp(low_keep, low_pass)
low_back.defvjp(back_keep, back_low)
EPSILON = 1e-05
NEGATIVE = -1e+30
HIGHEST = lax.Precision.HIGHEST

def rms_norm(hidden, gain):
    factor = lax.rsqrt(lax.optimization_barrier(jnp.mean(hidden * hidden, axis=-1, keepdims=True)) + EPSILON)
    return hidden * factor * gain

def gelu_tanh(values):
    return jax.nn.gelu(values, approximate=True)

def rotary_tables(relative, half_width):
    freqs = jnp.exp(jnp.arange(half_width, dtype=jnp.float32) * (-math.log(10000.0) / half_width))
    angles = relative.astype(jnp.float32)[:, None] * freqs[None, :]
    return (jnp.cos(angles)[:, None, :], jnp.sin(angles)[:, None, :])

def rotate(values, cosine, sine):
    half_width = values.shape[-1] // 2
    first = values[..., :half_width]
    second = values[..., half_width:]
    return jnp.concatenate([first * cosine - second * sine, second * cosine + first * sine], axis=-1)

def sequence_layout(positions, lengths_row):
    ends = jnp.cumsum(lengths_row)
    passed = positions[:, None] >= ends[None, :]
    docs = lax.optimization_barrier(jnp.sum(passed.astype(jnp.int32), axis=1))
    starts = lax.optimization_barrier(jnp.sum(jnp.where(passed, lengths_row[None, :], 0), axis=1))
    return (docs, starts)

def matmul(left, right):
    return jnp.dot(left, right, precision=HIGHEST, preferred_element_type=jnp.float32)

def attention(query, key, value, positions, docs):
    total = query.shape[0]
    size = math.gcd(total, 512)
    count = total // size
    scale = HEAD ** (-0.5)

    def attend(block_in):
        query_block, pos_block, doc_block = block_in
        raw = jnp.einsum('qhd,khd->hqk', query_block, key, precision=HIGHEST)
        scores = low_back(raw * scale)
        allowed = (doc_block[:, None] == docs[None, :]) & (positions[None, :] <= pos_block[:, None])
        scores = jnp.where(allowed[None], scores, NEGATIVE)
        log_total = jax.nn.logsumexp(scores, axis=-1, keepdims=True)
        probs = low(jnp.exp(scores - log_total))
        return jnp.einsum('hqk,khd->qhd', probs, value, precision=HIGHEST)
    blocks = lax.map(jax.checkpoint(attend), (query.reshape(count, size, HEADS, HEAD), positions.reshape(count, size), docs.reshape(count, size)))
    return blocks.reshape(total, HEADS, HEAD)

def layer(inputs, weights, positions, docs, cosine, sine, valid):
    wq_f, wk_f, wv_f, wo_f, wup_f, bup_f, wdown_f, bdown_f, gain_one, gain_two, gain_three, gain_four = weights
    total = inputs.shape[0]
    attn_low = low(rms_norm(inputs, gain_one))
    q_lin = low_back(matmul(attn_low, wq_f))
    k_lin = low_back(matmul(attn_low, wk_f))
    v_lin = low_back(matmul(attn_low, wv_f))
    query = low(rotate(q_lin.reshape(total, HEADS, HEAD), cosine, sine))
    key = low(rotate(k_lin.reshape(total, HEADS, HEAD), cosine, sine))
    value = low(v_lin).reshape(total, HEADS, HEAD)
    attended = attention(query, key, value, positions, docs)
    out_low = low(low_back(attended.reshape(total, D)))
    projected = low_back(matmul(out_low, wo_f))
    middle = inputs + rms_norm(projected, gain_two)
    mlp_low = low(rms_norm(middle, gain_three))
    pre_act = low_back(matmul(mlp_low, wup_f) + bup_f)
    act_low = low(gelu_tanh(pre_act))
    down = low_back(matmul(act_low, wdown_f) + bdown_f)
    result = middle + rms_norm(down, gain_four)
    return jnp.where(valid[:, None], result, 0.0)

def add_pair(left, right):
    return left + right

def reference(tokens, lengths, order, w_query, w_key, w_value, w_out, w_up, b_up, w_down, b_down, gain_attn_in, gain_attn_out, gain_mlp_in, gain_mlp_out, cotangent):
    rows_all = jnp.arange(GROUP, dtype=jnp.int32)
    positions = order.reshape(-1)[rows_all // SLAB] * SLAB + rows_all % SLAB
    params = tuple((item.astype(jnp.float32) for item in (w_query, w_key, w_value, w_out, w_up, b_up, w_down, b_down, gain_attn_in, gain_attn_out, gain_mlp_in, gain_mlp_out)))

    def per_group(sums, group_in):
        group_tokens, lengths_row, group_cot = group_in
        docs, starts = sequence_layout(positions, lengths_row)
        valid = docs < DOCS
        cosine, sine = rotary_tables(positions - starts, HEAD // 2)

        def forward(inputs, weights):
            return layer(inputs, weights, positions, docs, cosine, sine, valid)
        result, pull = jax.vjp(forward, group_tokens.astype(jnp.float32), params)
        d_inputs, d_weights = pull(group_cot.astype(jnp.float32))
        sums = jax.tree.map(add_pair, sums, d_weights)
        return (sums, (result.astype(jnp.bfloat16), d_inputs))
    zeros = jax.tree.map(jnp.zeros_like, params)
    sums, (outputs, d_inputs) = lax.scan(per_group, zeros, (tokens.reshape(GROUPS, GROUP, D), lengths, cotangent.reshape(GROUPS, GROUP, D)))
    return (outputs.reshape(TOKENS, D), d_inputs.reshape(TOKENS, D), sums[0], sums[1], sums[2], sums[3], sums[4], sums[5], sums[6], sums[7], sums[8], sums[9], sums[10], sums[11])
```

```python
import functools
import math

import jax
import jax.numpy as jnp
import numpy as np
from jax import lax
from jax.experimental import pallas as pl
from jax.experimental.pallas import tpu as pltpu
from jax.sharding import Mesh
from jax.sharding import PartitionSpec as P

HEADS = 16
EPSILON = 1e-05
NEGATIVE = -1e30
ALL = ("z", "xl", "core", "y", "xh")
BLK = ("y", "xh")
BF = jnp.bfloat16
F32 = jnp.float32
TILES = ((0, 0, 256), (256, 0, 512), (512, 0, 768), (768, 512, 1024))


def device_index(z, x, c, y):
    return (((z % 4) * 2 + (x % 4) % 2) * 2 + c) * 8 + (y % 4) * 2 + (x % 4) // 2


def pairs_of(f):
    return [
        (device_index(z, x, c, y), device_index(*f(z, x, c, y)))
        for z in range(4)
        for x in range(4)
        for c in range(2)
        for y in range(4)
    ]


def up(v):
    return v ^ 1


def down_pair(v):
    return ((v + 1) ^ 1) - 1


FLIP = {
    "z+": pairs_of(lambda z, x, c, y: (up(z), x, c, y)),
    "z-": pairs_of(lambda z, x, c, y: (down_pair(z), x, c, y)),
    "y+": pairs_of(lambda z, x, c, y: (z, x, c, up(y))),
    "y-": pairs_of(lambda z, x, c, y: (z, x, c, down_pair(y))),
    "x+": pairs_of(lambda z, x, c, y: (z, up(x), c, y)),
    "x-": pairs_of(lambda z, x, c, y: (z, down_pair(x), c, y)),
    "core": pairs_of(lambda z, x, c, y: (z, x, 1 - c, y)),
}


def swap_with(x, link):
    return lax.ppermute(x, ALL, FLIP[link])


def rms_norm(hidden, gain):
    factor = lax.rsqrt(jnp.mean(hidden * hidden, axis=-1, keepdims=True) + EPSILON)
    return hidden * factor * gain


def gelu_tanh(values):
    return jax.nn.gelu(values, approximate=True)


def half_swap(x):
    n = x.shape[1]
    lane = lax.broadcasted_iota(jnp.int32, x.shape, 1) % 64
    return jnp.where(lane < 32, pltpu.roll(x, n - 32, 1), pltpu.roll(x, 32, 1))


def rotary_tables(relative):
    freqs = jnp.exp(jnp.arange(32, dtype=F32) * (-math.log(10000.0) / 32))
    angles = relative.astype(F32)[:, None] * freqs[None, :]
    c, s = jnp.cos(angles), jnp.sin(angles)
    return jnp.concatenate([c, c, c, c], axis=1), jnp.concatenate([-s, s, -s, s], axis=1)


def dot(a, b):
    return jnp.dot(a, b, preferred_element_type=F32)


def dot_nt(a, b):
    return lax.dot_general(a, b, (((1,), (1,)), ((), ())), preferred_element_type=F32)


def dot_tn(a, b):
    return lax.dot_general(a, b, (((0,), (0,)), ((), ())), preferred_element_type=F32)


def qkv_kernel(x_ref, g_ref, cos_ref, sin_ref, wq_ref, wk_ref, wv_ref, out_ref, a_ref):
    @pl.when(pl.program_id(0) == 0)
    def _():
        x = x_ref[...].astype(F32)
        factor = lax.rsqrt(jnp.mean(x * x, axis=-1, keepdims=True) + EPSILON)
        a_ref[...] = (x * factor * g_ref[...]).astype(BF)

    a = a_ref[...]
    cos = jnp.concatenate([cos_ref[...]] * 2, axis=1)
    sin = jnp.concatenate([sin_ref[...]] * 2, axis=1)
    q = dot(a, wq_ref[...])
    q = (q * cos + half_swap(q) * sin).astype(BF)
    k = dot(a, wk_ref[...])
    k = (k * cos + half_swap(k) * sin).astype(BF)
    v = dot(a, wv_ref[...]).astype(BF)
    for j in range(2):
        at = slice(128 * j, 128 * (j + 1))
        out_ref[j, :, 0:128] = q[:, at]
        out_ref[j, :, 128:256] = k[:, at]
        out_ref[j, :, 256:384] = v[:, at]


def qkv_call(x, gain, cos, sin, wq, wk, wv):
    whole = lambda shape: pl.BlockSpec(shape, lambda j: (0,) * len(shape))
    col = pl.BlockSpec((1024, 256), lambda j: (0, j))
    return pl.pallas_call(
        qkv_kernel,
        grid=(4,),
        in_specs=[whole((128, 1024)), whole((1, 1024)), whole((128, 128)), whole((128, 128)), col, col, col],
        out_specs=[pl.BlockSpec((2, 128, 384), lambda j: (j, 0, 0)), whole((128, 1024))],
        out_shape=[jax.ShapeDtypeStruct((8, 128, 384), BF), jax.ShapeDtypeStruct((128, 1024), BF)],
        compiler_params=pltpu.CompilerParams(vmem_limit_bytes=32 * 2**20),
        cost_estimate=pl.CostEstimate(flops=2 * 128 * 1024 * 3072, bytes_accessed=7 * 2**20, transcendentals=0),
    )(x, gain, cos, sin, wq, wk, wv)


def allowed_mask(len_ref, q0, k0, k1):
    qpos = q0 + lax.broadcasted_iota(jnp.int32, (1, 256), 1)
    start = jnp.zeros((1, 256), jnp.int32)
    end = jnp.int32(0)
    for e in range(6):
        end = end + len_ref[0, e]
        start = jnp.where(qpos >= end, end, start)
    kpos = k0 + lax.broadcasted_iota(jnp.int32, (k1 - k0, 256), 0)
    return (kpos >= start) & (kpos <= qpos)


def attend_kernel(order_ref, len_ref, qkv_ref, out_ref, pos_ref, lse_ref, o_ref):
    for b in range(8):
        for j in range(2):
            at = pl.ds(pl.multiple_of(order_ref[b, j] * 64, 64), 64)
            pos_ref[at, :] = qkv_ref[b, 64 * j : 64 * (j + 1), :]
    first = lax.broadcasted_iota(jnp.int32, (1, 128), 1) < 64
    v_t = pos_ref[:, 256:384].T
    for q0, k0, k1 in TILES:
        q = pos_ref[q0 : q0 + 256, 0:128].astype(F32) * 0.125
        k = pos_ref[k0:k1, 128:256]
        mask = allowed_mask(len_ref, q0, k0, k1)
        outs = []
        for h in range(2):
            q_h = jnp.where(first if h == 0 else ~first, q, 0.0).astype(BF)
            s = jnp.where(mask, dot_nt(k, q_h), NEGATIVE)
            top = jnp.max(s, axis=0, keepdims=True)
            p = jnp.exp(s - top)
            total = jnp.sum(p, axis=0, keepdims=True)
            lse_ref[h : h + 1, q0 : q0 + 256] = top + jnp.log(total)
            p = (p * (1.0 / total)).astype(BF)
            outs.append(dot(v_t[64 * h : 64 * (h + 1), k0:k1], p))
        o_ref[q0 : q0 + 256, :] = jnp.concatenate(outs, axis=0).T.astype(BF)
    for b in range(8):
        for j in range(2):
            at = pl.ds(pl.multiple_of(order_ref[b, j] * 64, 64), 64)
            out_ref[b, 64 * j : 64 * (j + 1), :] = o_ref[at, :]


SMEM = pl.BlockSpec(memory_space=pltpu.SMEM)
VMEM = pl.BlockSpec(memory_space=pltpu.VMEM)


def attend_call(order, lengths, qkv):
    return pl.pallas_call(
        attend_kernel,
        in_specs=[SMEM, SMEM, VMEM],
        out_specs=[VMEM, VMEM, VMEM],
        out_shape=[
            jax.ShapeDtypeStruct((8, 128, 128), BF),
            jax.ShapeDtypeStruct((1024, 384), BF),
            jax.ShapeDtypeStruct((2, 1024), F32),
        ],
        scratch_shapes=[pltpu.VMEM((1024, 128), BF)],
        compiler_params=pltpu.CompilerParams(vmem_limit_bytes=48 * 2**20),
        cost_estimate=pl.CostEstimate(flops=2 * 10**9, bytes_accessed=3 * 2**20, transcendentals=2 * 10**6),
    )(order, lengths, qkv)


def attend_back_kernel(order_ref, len_ref, pos_ref, lse_ref, cos_ref, sin_ref, do_ref, out_ref, d_ref, dk_ref, dv_ref, dq_ref):
    for b in range(8):
        for j in range(2):
            at = pl.ds(pl.multiple_of(order_ref[b, j] * 64, 64), 64)
            d_ref[at, 0:128] = do_ref[b, 64 * j : 64 * (j + 1), :]
    first = lax.broadcasted_iota(jnp.int32, (1, 128), 1) < 64
    k_t = pos_ref[:, 128:256].T
    dk_ref[...] = jnp.zeros_like(dk_ref)
    dv_ref[...] = jnp.zeros_like(dv_ref)
    for q0, k0, k1 in TILES:
        q = pos_ref[q0 : q0 + 256, 0:128].astype(F32) * 0.125
        do = d_ref[q0 : q0 + 256, 0:128]
        k = pos_ref[k0:k1, 128:256]
        v = pos_ref[k0:k1, 256:384]
        mask = allowed_mask(len_ref, q0, k0, k1)
        outs = []
        for h in range(2):
            pick = first if h == 0 else ~first
            q_h = jnp.where(pick, q, 0.0).astype(BF)
            do_h = jnp.where(pick, do.astype(F32), 0.0).astype(BF)
            s = jnp.where(mask, dot_nt(k, q_h), NEGATIVE)
            p = jnp.exp(s - lse_ref[h : h + 1, q0 : q0 + 256])
            dp = dot_nt(v, do_h)
            delta = jnp.sum(p * dp, axis=0, keepdims=True)
            ds = (p * (dp - delta)).astype(BF)
            dv_ref[k0:k1, :] += dot(p.astype(BF), do_h)
            dk_ref[k0:k1, :] += dot(ds, q_h)
            outs.append(dot(k_t[64 * h : 64 * (h + 1), k0:k1], ds))
        dq_ref[q0 : q0 + 256, :] = jnp.concatenate(outs, axis=0).T * 0.125
    cos, sin = cos_ref[...], sin_ref[...]
    dq, dk = dq_ref[...], dk_ref[...]
    d_ref[:, 0:128] = (dq * cos - half_swap(dq) * sin).astype(BF)
    d_ref[:, 128:256] = (dk * cos - half_swap(dk) * sin).astype(BF)
    d_ref[:, 256:384] = dv_ref[...].astype(BF)
    for b in range(8):
        for j in range(2):
            at = pl.ds(pl.multiple_of(order_ref[b, j] * 64, 64), 64)
            out_ref[b, 64 * j : 64 * (j + 1), :] = d_ref[at, :]


def attend_back_call(order, lengths, pos, lse, cos, sin, d_out):
    return pl.pallas_call(
        attend_back_kernel,
        in_specs=[SMEM, SMEM, VMEM, VMEM, VMEM, VMEM, VMEM],
        out_specs=VMEM,
        out_shape=jax.ShapeDtypeStruct((8, 128, 384), BF),
        scratch_shapes=[
            pltpu.VMEM((1024, 384), BF),
            pltpu.VMEM((1024, 128), F32),
            pltpu.VMEM((1024, 128), F32),
            pltpu.VMEM((1024, 128), F32),
        ],
        compiler_params=pltpu.CompilerParams(vmem_limit_bytes=48 * 2**20),
        cost_estimate=pl.CostEstimate(flops=6 * 10**9, bytes_accessed=4 * 2**20, transcendentals=2 * 10**6),
    )(order, lengths, pos, lse, cos, sin, d_out)


def grads_kernel(bits_ref, act_ref, m_ref, o_ref, dpre_ref, dd_ref, dproj_ref,
                 act2_ref, m2_ref, o2_ref, dpre2_ref, dd2_ref, dproj2_ref,
                 p0_ref, p1_ref, p2_ref, p3_ref, p4_ref,
                 m_t, act_t, o_t, dpre, dd, dproj):
    step = pl.program_id(0)

    @pl.when(step == 0)
    def _():
        for dst, one, two in ((m_t, m_ref, m2_ref), (act_t, act_ref, act2_ref), (o_t, o_ref, o2_ref)):
            dst[:, 0:128] = one[...].T
            dst[:, 128:256] = two[...].T
        for dst, one, two in ((dpre, dpre_ref, dpre2_ref), (dd, dd_ref, dd2_ref), (dproj, dproj_ref, dproj2_ref)):
            dst[0:128, :] = one[...]
            dst[128:256, :] = two[...]

    bz, by, bx = bits_ref[0], bits_ref[1], bits_ref[2]
    k_first = step ^ bz
    for k2 in range(2):
        kb = 2 * k_first + k2
        slot = k2 ^ by
        for u, out in ((0, p0_ref), (2, p1_ref)):
            rhs = jnp.concatenate(
                [dpre[:, pl.ds(pl.multiple_of((u + v) * 512 + kb * 128, 128), 128)] for v in range(2)], axis=1
            )
            g = dot(m_t[...], rhs)
            both = [g[:, 0:128].reshape(128, 8, 128), g[:, 128:256].reshape(128, 8, 128)]
            out[0, slot] = jnp.concatenate(both, axis=1).astype(BF).reshape(2048, 128)
    k_first = step ^ by
    rhs = dd[:, pl.ds(pl.multiple_of(k_first * 256, 256), 256)]
    for half in range(2):
        g = dot(act_t[2048 * half : 2048 * (half + 1), :], rhs).astype(BF)
        for k2 in range(2):
            part = g[:, 128 * k2 : 128 * (k2 + 1)].reshape(64, 2, 16, 128)
            slot = k2 ^ bx
            p2_ref[0, slot, 1024 * half : 1024 * (half + 1), :] = part[:, 0].reshape(1024, 128)
            p3_ref[0, slot, 1024 * half : 1024 * (half + 1), :] = part[:, 1].reshape(1024, 128)
    k_first = step ^ bx
    rhs = dproj[:, pl.ds(pl.multiple_of(k_first * 256, 256), 256)]
    g = dot(o_t[...], rhs).astype(BF)
    for k2 in range(2):
        p4_ref[0, k2 ^ bz] = g[:, 128 * k2 : 128 * (k2 + 1)]


def grads_call(bits, mine, theirs):
    out = lambda rows: (
        pl.BlockSpec((1, 2, rows, 128), lambda s, bits: (s, 0, 0, 0)),
        jax.ShapeDtypeStruct((2, 2, rows, 128), BF),
    )
    outs = [out(2048)] * 4 + [out(1024)]
    whole = lambda a: pl.BlockSpec(a.shape, lambda s, bits: (0, 0))
    return pl.pallas_call(
        grads_kernel,
        grid_spec=pltpu.PrefetchScalarGridSpec(
            num_scalar_prefetch=1,
            grid=(2,),
            in_specs=[whole(a) for a in mine + theirs],
            out_specs=[o[0] for o in outs],
            scratch_shapes=[
                pltpu.VMEM((1024, 256), BF),
                pltpu.VMEM((4096, 256), BF),
                pltpu.VMEM((1024, 256), BF),
                pltpu.VMEM((256, 2048), BF),
                pltpu.VMEM((256, 512), BF),
                pltpu.VMEM((256, 512), BF),
            ],
        ),
        out_shape=[o[1] for o in outs],
        compiler_params=pltpu.CompilerParams(vmem_limit_bytes=56 * 2**20),
        cost_estimate=pl.CostEstimate(flops=2 * 256 * 9 * 2**19, bytes_accessed=14 * 2**20, transcendentals=0),
    )(bits, *mine, *theirs)


ROUTES = (("z+", "y+"), ("z-", "y-"), ("y+", "x+"), ("y-", "x-"), ("x+", "z+"))


def halve(parts):
    for turn in range(2):
        got = [swap_with(part[1], route[turn]) for part, route in zip(parts, ROUTES)]
        parts = [(part[0].astype(F32) + other.astype(F32)).astype(BF) for part, other in zip(parts, got)]
    return parts


def local(
    tokens, lengths, order, w_query, w_key, w_value, w_out, w_up, b_up, w_down, b_down,
    gain_attn_in, gain_attn_out, gain_mlp_in, gain_mlp_out, cotangent,
):
    rows, width = tokens.shape
    z, xl, core, y, xh = (lax.axis_index(a) for a in ALL)
    my_blk = y * 2 + xh
    me = ((z * 2 + xl) * 2 + core) * 8 + my_blk
    lengths_row = lengths[0]
    ends = jnp.cumsum(lengths_row)

    def start_of(positions):
        return jnp.sum(jnp.where(positions[:, None] >= ends[None, :], lengths_row[None, :], 0), axis=1)

    within = jnp.arange(rows, dtype=jnp.int32)
    pair = lax.dynamic_index_in_dim(order, my_blk, 0, keepdims=False)
    my_pos = jnp.where(within < 64, pair[0], pair[1]) * 64 + within % 64
    valid = my_pos < ends[-1]
    cos, sin = rotary_tables(my_pos - start_of(my_pos))
    group_pos = jnp.arange(1024, dtype=jnp.int32)
    cos_all, sin_all = rotary_tables(group_pos - start_of(group_pos))

    qkv, attn_low = qkv_call(tokens, gain_attn_in.reshape(1, -1), cos, sin, w_query, w_key, w_value)
    attn_all = lax.all_gather(attn_low, BLK, axis=0, tiled=True)
    qkv_heads = lax.all_to_all(qkv, BLK, 0, 0, tiled=True)
    out_heads, pos_qkv, lse = attend_call(order, lengths, qkv_heads)
    out_mine = lax.all_to_all(out_heads, BLK, 0, 0, tiled=True)
    out_low = out_mine.transpose(1, 0, 2).reshape(rows, width)

    inputs = tokens.astype(F32)
    projected = dot(out_low, w_out)
    branch_one, norm_two_pull = jax.vjp(rms_norm, projected, gain_attn_out)
    middle = inputs + branch_one
    mlp_in, norm_three_pull = jax.vjp(rms_norm, middle, gain_mlp_in)
    mlp_low = mlp_in.astype(BF)
    pre_act = dot(mlp_low, w_up) + b_up
    activated, gelu_pull = jax.vjp(gelu_tanh, pre_act)
    act_low = activated.astype(BF)
    down = dot(act_low, w_down) + b_down
    branch_two, norm_four_pull = jax.vjp(rms_norm, down, gain_mlp_out)
    output = jnp.where(valid[:, None], middle + branch_two, 0.0).astype(BF)
    upstream = jnp.where(valid[:, None], cotangent.astype(F32), 0.0)
    d_down, grad_gain_mlp_out = norm_four_pull(upstream)
    d_down_low = d_down.astype(BF)
    grad_b_down = jnp.sum(d_down_low.astype(F32), axis=0)
    (d_pre,) = gelu_pull(dot_nt(d_down_low, w_down))
    d_pre_low = d_pre.astype(BF)
    grad_b_up = jnp.sum(d_pre_low.astype(F32), axis=0)
    d_middle_norm, grad_gain_mlp_in = norm_three_pull(dot_nt(d_pre_low, w_up))
    d_middle = upstream + d_middle_norm
    d_projected, grad_gain_attn_out = norm_two_pull(d_middle)
    d_proj_low = d_projected.astype(BF)
    d_out_low = dot_nt(d_proj_low, w_out).astype(BF)

    d_out_heads = lax.all_to_all(d_out_low.reshape(rows, 8, 128).transpose(1, 0, 2), BLK, 0, 0, tiled=True)

    half_of = lambda a, which: lax.dynamic_slice_in_dim(a, which * (a.shape[1] // 2), a.shape[1] // 2, 1)
    lefts = [act_low, mlp_low, out_low]
    rights = [d_pre_low, d_down_low, d_proj_low]
    send = jnp.concatenate(lefts + [half_of(a, 1 - core) for a in rights], axis=1)
    got = swap_with(send, "core")
    theirs, at = [], 0
    for n in (4096, 1024, 1024, 2048, 512, 512):
        theirs.append(got[:, at : at + n])
        at += n
    mine = lefts + [half_of(a, core) for a in rights]
    x = xh * 2 + xl
    bits = jnp.stack([z % 2, y % 2, x % 2]).astype(jnp.int32)
    parts = halve(grads_call(bits, mine, theirs))

    d_heads = attend_back_call(order, lengths, pos_qkv, lse, cos_all, sin_all, d_out_heads)
    d_mine = lax.all_to_all(d_heads, BLK, 0, 0, tiled=True)
    dq_low, dk_low, dv_low = (
        d_mine[:, :, 128 * i : 128 * (i + 1)].transpose(1, 0, 2).reshape(rows, width) for i in range(3)
    )
    d_attn = dot_nt(dq_low, w_query) + dot_nt(dk_low, w_key) + dot_nt(dv_low, w_value)
    _, norm_one_pull = jax.vjp(lambda h: rms_norm(h, gain_attn_in), inputs)
    grad_tokens = d_middle + norm_one_pull(d_attn)[0]

    qkv_grads = dot_tn(attn_all, d_heads.reshape(1024, 384)).astype(BF).reshape(128, 8, 384)
    vectors = jnp.concatenate(
        [v.reshape(128, -1) for v in (grad_b_up, grad_b_down, grad_gain_attn_out, grad_gain_mlp_in, grad_gain_mlp_out)]
        + [jnp.zeros((128, 64), F32)],
        axis=1,
    ).astype(BF)
    vectors = jnp.pad(vectors.reshape(128, 1, 128), ((0, 0), (0, 7), (0, 0)))
    payload = jnp.concatenate(
        [p.reshape(128, -1, 128) for p in parts]
        + [vectors]
        + [qkv_grads[:, :, 128 * i : 128 * (i + 1)] for i in range(3)],
        axis=1,
    )
    got = lax.all_to_all(payload, ALL, 0, 0, tiled=True).astype(F32)
    got = got.reshape(2, 2, 2, 2, 2, 2, 2, -1, 128)
    up_sum = jnp.sum(got[..., 0:32, :], axis=(0, 2, 4, 6))
    down_sum = jnp.sum(got[..., 32:64, :], axis=(0, 1, 4, 6))
    out_sum = jnp.sum(got[..., 64:72, :], axis=(0, 4, 5, 6))
    vec_sum = jnp.sum(got[..., 72, :], axis=(0, 1, 2, 3, 4, 5, 6))
    qkv_sum = jnp.sum(got[..., 80:104, :], axis=(0, 1, 2, 3))

    grad_w_up = up_sum.reshape(2, 2, 2, 4, 8, 128).transpose(4, 1, 3, 0, 2, 5).reshape(8, 4096)
    grad_w_down = down_sum.transpose(3, 1, 2, 0, 4).reshape(32, 1024)
    grad_w_out = out_sum.transpose(3, 2, 1, 0, 4).reshape(8, 1024)
    qkv_sum = qkv_sum.reshape(8, 3, 8, 128).transpose(1, 2, 0, 3).reshape(3, 8, 1024)
    grad_b_up, grad_b_down = vec_sum[0:32], vec_sum[32:40]
    grad_gain_attn_out, grad_gain_mlp_in, grad_gain_mlp_out = vec_sum[40:48], vec_sum[48:56], vec_sum[56:64]
    my_rows = lambda w: lax.dynamic_slice_in_dim(w, me * 8, 8, 0).astype(F32)
    weighted = sum(jnp.sum(my_rows(w) * qkv_sum[i], axis=1) for i, w in enumerate((w_query, w_key, w_value)))
    grad_gain_attn_in = weighted / lax.dynamic_slice_in_dim(gain_attn_in, me * 8, 8, 0)
    return (
        output, grad_tokens, qkv_sum[0], qkv_sum[1], qkv_sum[2], grad_w_out, grad_w_up, grad_b_up, grad_w_down,
        grad_b_down, grad_gain_attn_in, grad_gain_attn_out, grad_gain_mlp_in, grad_gain_mlp_out,
    )


def solution(mesh):
    split = Mesh(np.asarray(mesh.devices).reshape(4, 2, 2, 4, 2), ALL)
    every = P(ALL, None)
    flat = P(ALL)
    return jax.shard_map(
        local,
        mesh=split,
        in_specs=(every, P(("z", "xl", "core"), None)) + (P(),) * 13 + (every,),
        out_specs=(every,) * 7 + (flat, every) + (flat,) * 5,
        check_vma=False,
    )
```

```python
import math

import jax
import jax.numpy as jnp
import numpy as np
from jax import lax
from jax.experimental import pallas as pl
from jax.experimental.pallas import tpu as pltpu
from jax.sharding import Mesh
from jax.sharding import PartitionSpec as P

HEADS = 16
EPSILON = 1e-05
NEGATIVE = -1e30
ALL = ("z", "xl", "core", "y", "xh")
BLK = ("y", "xh")
BF = jnp.bfloat16
F32 = jnp.float32
TILES = ((0, 0, 256), (256, 0, 512), (512, 0, 768), (768, 512, 1024))


SMEM = pl.BlockSpec(memory_space=pltpu.SMEM)
VMEM = pl.BlockSpec(memory_space=pltpu.VMEM)
HBM = pl.BlockSpec(memory_space=pltpu.HBM)


def device_index(z, x, c, y):
    return (((z % 4) * 2 + (x % 4) % 2) * 2 + c) * 8 + (y % 4) * 2 + (x % 4) // 2


def pairs_of(f):
    return [
        (device_index(z, x, c, y), device_index(*f(z, x, c, y)))
        for z in range(4)
        for x in range(4)
        for c in range(2)
        for y in range(4)
    ]


def up(v):
    return v ^ 1


def down_pair(v):
    return ((v + 1) ^ 1) - 1


def flip(axis, by_core):
    way = (up, down_pair)

    def there(z, x, c, y):
        move = way[by_core[c]]
        return (
            move(z) if axis == "z" else z,
            move(x) if axis == "x" else x,
            c,
            move(y) if axis == "y" else y,
        )

    return pairs_of(there)


SWAP_CORES = pairs_of(lambda z, x, c, y: (z, x, 1 - c, y))
STEPS = (
    (flip("z", (0, 1)), flip("y", (0, 1)), flip("x", (0, 1))),
    (flip("y", (0, 1)), flip("x", (0, 1)), flip("z", (0, 1))),
)


def half_swap(x):
    n = x.shape[1]
    lane = lax.broadcasted_iota(jnp.int32, x.shape, 1) % 64
    return jnp.where(lane < 32, pltpu.roll(x, n - 32, 1), pltpu.roll(x, 32, 1))


def rotary_tables(relative):
    freqs = jnp.exp(jnp.arange(32, dtype=F32) * (-math.log(10000.0) / 32))
    angles = relative.astype(F32)[:, None] * freqs[None, :]
    c, s = jnp.cos(angles), jnp.sin(angles)
    return jnp.concatenate([c, c, c, c], axis=1), jnp.concatenate([-s, s, -s, s], axis=1)


def dot(a, b):
    return jnp.dot(a, b, preferred_element_type=F32)


def dot_nt(a, b):
    return lax.dot_general(a, b, (((1,), (1,)), ((), ())), preferred_element_type=F32)


def dot_tn(a, b):
    return lax.dot_general(a, b, (((0,), (0,)), ((), ())), preferred_element_type=F32)


def column_positions(info_ref, order_ref, len_ref):
    row = lax.broadcasted_iota(jnp.int32, (128, 1), 0)
    one, two = order_ref[info_ref[1], 0], order_ref[info_ref[1], 1]
    pos = jnp.where(row < 64, one * 64 + row, two * 64 + row - 64)
    start = jnp.zeros((128, 1), jnp.int32)
    end = jnp.int32(0)
    for e in range(6):
        end = end + len_ref[0, e]
        start = jnp.where(pos >= end, end, start)
    return pos, start, end


def qkv_kernel(info_ref, order_ref, len_ref, x_ref, g_ref, wq_hbm, wk_hbm, wv_hbm, out_ref, all_hbm, a_ref, wq, wk, wv, sems):
    copies = [
        pltpu.make_async_copy(hbm.at[:, 512 * h : 512 * (h + 1)], w.at[:, 512 * h : 512 * (h + 1)], sems.at[2 * i + h])
        for i, (hbm, w) in enumerate(((wq_hbm, wq), (wk_hbm, wk), (wv_hbm, wv)))
        for h in range(2)
    ]
    for copy in copies:
        copy.start()
    x = x_ref[...].astype(F32)
    factor = lax.rsqrt(jnp.mean(x * x, axis=-1, keepdims=True) + EPSILON)
    a = (x * factor * g_ref[...]).astype(BF)
    a_ref[...] = a
    spread = [pltpu.make_async_copy(a_ref, all_hbm.at[j], sems.at[6 + j]) for j in range(8)]
    for copy in spread:
        copy.start()
    pos, start, _ = column_positions(info_ref, order_ref, len_ref)
    lane = lax.broadcasted_iota(jnp.int32, (1, 128), 1)
    freqs = jnp.exp((lane % 32).astype(F32) * (-math.log(10000.0) / 32))
    angles = (pos - start).astype(F32) * freqs
    cos = jnp.cos(angles)
    sine = jnp.sin(angles)
    sin = jnp.where(lane % 64 < 32, -sine, sine)
    cos = jnp.concatenate([cos] * 4, axis=1)
    sin = jnp.concatenate([sin] * 4, axis=1)
    for i, w in enumerate((wq, wk, wv)):
        for h in range(2):
            copies[2 * i + h].wait()
            y = dot(a, w[:, 512 * h : 512 * (h + 1)])
            if i < 2:
                y = y * cos + half_swap(y) * sin
            y = y.astype(BF)
            for j in range(4):
                out_ref[4 * h + j, :, 128 * i : 128 * (i + 1)] = y[:, 128 * j : 128 * (j + 1)]
    for copy in spread:
        copy.wait()


def qkv_call(info, order, lengths, x, gain, wq, wk, wv):
    return pl.pallas_call(
        qkv_kernel,
        in_specs=[SMEM, SMEM, SMEM, VMEM, VMEM, HBM, HBM, HBM],
        out_specs=[VMEM, HBM],
        out_shape=[jax.ShapeDtypeStruct((8, 128, 384), BF), jax.ShapeDtypeStruct((8, 128, 1024), BF)],
        scratch_shapes=[pltpu.VMEM((128, 1024), BF)] + [pltpu.VMEM((1024, 1024), BF)] * 3 + [pltpu.SemaphoreType.DMA((14,))],
        compiler_params=pltpu.CompilerParams(vmem_limit_bytes=60 * 2**20),
        cost_estimate=pl.CostEstimate(flops=2 * 128 * 1024 * 3072, bytes_accessed=7 * 2**20, transcendentals=0),
    )(info, order, lengths, x, gain, wq, wk, wv)


def allowed_mask(len_ref, q0, k0, k1):
    qpos = q0 + lax.broadcasted_iota(jnp.int32, (1, 256), 1)
    start = jnp.zeros((1, 256), jnp.int32)
    end = jnp.int32(0)
    for e in range(6):
        end = end + len_ref[0, e]
        start = jnp.where(qpos >= end, end, start)
    kpos = k0 + lax.broadcasted_iota(jnp.int32, (k1 - k0, 256), 0)
    return (kpos >= start) & (kpos <= qpos)


def attend_kernel(order_ref, len_ref, qkv_ref, out_ref, pos_ref, lse_ref, o_ref):
    for b in range(8):
        for j in range(2):
            at = pl.ds(pl.multiple_of(order_ref[b, j] * 64, 64), 64)
            pos_ref[at, :] = qkv_ref[b, 64 * j : 64 * (j + 1), :]
    first = lax.broadcasted_iota(jnp.int32, (1, 128), 1) < 64
    v_t = pos_ref[:, 256:384].T
    for q0, k0, k1 in TILES:
        q = pos_ref[q0 : q0 + 256, 0:128].astype(F32) * 0.125
        k = pos_ref[k0:k1, 128:256]
        mask = allowed_mask(len_ref, q0, k0, k1)
        outs = []
        for h in range(2):
            q_h = jnp.where(first if h == 0 else ~first, q, 0.0).astype(BF)
            s = jnp.where(mask, dot_nt(k, q_h), NEGATIVE)
            top = jnp.max(s, axis=0, keepdims=True)
            p = jnp.exp(s - top)
            total = jnp.sum(p, axis=0, keepdims=True)
            lse_ref[h : h + 1, q0 : q0 + 256] = top + jnp.log(total)
            p = (p * (1.0 / total)).astype(BF)
            outs.append(dot(v_t[64 * h : 64 * (h + 1), k0:k1], p))
        o_ref[q0 : q0 + 256, :] = jnp.concatenate(outs, axis=0).T.astype(BF)
    for b in range(8):
        for j in range(2):
            at = pl.ds(pl.multiple_of(order_ref[b, j] * 64, 64), 64)
            out_ref[b, 64 * j : 64 * (j + 1), :] = o_ref[at, :]


def attend_call(order, lengths, qkv):
    return pl.pallas_call(
        attend_kernel,
        in_specs=[SMEM, SMEM, VMEM],
        out_specs=[VMEM, VMEM, VMEM],
        out_shape=[
            jax.ShapeDtypeStruct((8, 128, 128), BF),
            jax.ShapeDtypeStruct((1024, 384), BF),
            jax.ShapeDtypeStruct((2, 1024), F32),
        ],
        scratch_shapes=[pltpu.VMEM((1024, 128), BF)],
        compiler_params=pltpu.CompilerParams(vmem_limit_bytes=24 * 2**20),
        cost_estimate=pl.CostEstimate(flops=2 * 10**9, bytes_accessed=3 * 2**20, transcendentals=2 * 10**6),
    )(order, lengths, qkv)


def attend_back_kernel(order_ref, len_ref, pos_ref, lse_ref, cos_ref, sin_ref, do_ref, out_ref, d_ref, dk_ref, dv_ref, dq_ref):
    for b in range(8):
        for j in range(2):
            at = pl.ds(pl.multiple_of(order_ref[b, j] * 64, 64), 64)
            d_ref[at, 0:128] = do_ref[b, 64 * j : 64 * (j + 1), :]
    first = lax.broadcasted_iota(jnp.int32, (1, 128), 1) < 64
    k_t = pos_ref[:, 128:256].T
    dk_ref[...] = jnp.zeros_like(dk_ref)
    dv_ref[...] = jnp.zeros_like(dv_ref)
    for q0, k0, k1 in TILES:
        q = pos_ref[q0 : q0 + 256, 0:128].astype(F32) * 0.125
        do = d_ref[q0 : q0 + 256, 0:128]
        k = pos_ref[k0:k1, 128:256]
        v = pos_ref[k0:k1, 256:384]
        mask = allowed_mask(len_ref, q0, k0, k1)
        outs = []
        for h in range(2):
            pick = first if h == 0 else ~first
            q_h = jnp.where(pick, q, 0.0).astype(BF)
            do_h = jnp.where(pick, do.astype(F32), 0.0).astype(BF)
            s = jnp.where(mask, dot_nt(k, q_h), NEGATIVE)
            p = jnp.exp(s - lse_ref[h : h + 1, q0 : q0 + 256])
            dp = dot_nt(v, do_h)
            delta = jnp.sum(p * dp, axis=0, keepdims=True)
            ds = (p * (dp - delta)).astype(BF)
            dv_ref[k0:k1, :] += dot(p.astype(BF), do_h)
            dk_ref[k0:k1, :] += dot(ds, q_h)
            outs.append(dot(k_t[64 * h : 64 * (h + 1), k0:k1], ds))
        dq_ref[q0 : q0 + 256, :] = jnp.concatenate(outs, axis=0).T * 0.125
    cos, sin = cos_ref[...], sin_ref[...]
    dq, dk = dq_ref[...], dk_ref[...]
    d_ref[:, 0:128] = (dq * cos - half_swap(dq) * sin).astype(BF)
    d_ref[:, 128:256] = (dk * cos - half_swap(dk) * sin).astype(BF)
    d_ref[:, 256:384] = dv_ref[...].astype(BF)
    for b in range(8):
        for j in range(2):
            at = pl.ds(pl.multiple_of(order_ref[b, j] * 64, 64), 64)
            out_ref[b, 64 * j : 64 * (j + 1), :] = d_ref[at, :]


def attend_back_call(order, lengths, pos, lse, cos, sin, d_out):
    return pl.pallas_call(
        attend_back_kernel,
        in_specs=[SMEM, SMEM, VMEM, VMEM, VMEM, VMEM, VMEM],
        out_specs=VMEM,
        out_shape=jax.ShapeDtypeStruct((8, 128, 384), BF),
        scratch_shapes=[
            pltpu.VMEM((1024, 384), BF),
            pltpu.VMEM((1024, 128), F32),
            pltpu.VMEM((1024, 128), F32),
            pltpu.VMEM((1024, 128), F32),
        ],
        compiler_params=pltpu.CompilerParams(vmem_limit_bytes=32 * 2**20),
        cost_estimate=pl.CostEstimate(flops=6 * 10**9, bytes_accessed=4 * 2**20, transcendentals=2 * 10**6),
    )(order, lengths, pos, lse, cos, sin, d_out)


ACT, M_AT, O_AT, DPRE, DD, DPROJ, SEND = 0, 4096, 5120, 6144, 8192, 8704, 9216
CHUNK = 512


def mlp_kernel(info_ref, order_ref, len_ref, o_ref, x_ref, ct_ref, wo_hbm, wup_hbm, bup_ref, wdown_hbm, bdown_ref,
               g2_ref, g3_ref, g4_ref,
               out_ref, dmid_ref, do_ref, send_ref, keep_ref, vup_ref, vrow_ref,
               proj_ref, middle_ref, slope_ref, dd_ref, acc_ref, wo_ref, wup_ref, wdown_ref, sems):
    core = info_ref[0]
    count = 4096 // CHUNK
    copy_out = pltpu.make_async_copy(wo_hbm, wo_ref, sems.at[2 * count])
    copy_out.start()
    copies = []
    for i in range(count):
        at = slice(CHUNK * i, CHUNK * (i + 1))
        copies.append((
            pltpu.make_async_copy(wup_hbm.at[:, at], wup_ref.at[:, at], sems.at[2 * i]),
            pltpu.make_async_copy(wdown_hbm.at[at, :], wdown_ref.at[at, :], sems.at[2 * i + 1]),
        ))
        copies[-1][0].start()
        copies[-1][1].start()
    pos, _, end = column_positions(info_ref, order_ref, len_ref)
    valid = pos < end
    o = jnp.concatenate([o_ref[j] for j in range(8)], axis=1)
    send_ref[:, O_AT : O_AT + 1024] = o
    copy_out.wait()
    proj = dot(o, wo_ref[...])
    proj_ref[...] = proj
    r2 = lax.rsqrt(jnp.mean(proj * proj, axis=-1, keepdims=True) + EPSILON)
    middle = x_ref[...].astype(F32) + proj * r2 * g2_ref[...]
    middle_ref[...] = middle
    r3 = lax.rsqrt(jnp.mean(middle * middle, axis=-1, keepdims=True) + EPSILON)
    m = (middle * r3 * g3_ref[...]).astype(BF)
    send_ref[:, M_AT : M_AT + 1024] = m
    acc_ref[...] = jnp.zeros_like(acc_ref)
    root = math.sqrt(2.0 / math.pi)
    for i in range(4096 // CHUNK):
        at = slice(CHUNK * i, CHUNK * (i + 1))
        copies[i][0].wait()
        pre = dot(m, wup_ref[:, at]) + bup_ref[:, at]
        square = pre * pre
        t = jnp.tanh(root * (pre + 0.044715 * (square * pre)))
        half = 0.5 * (1.0 + t)
        act = (pre * half).astype(BF)
        slope_ref[:, at] = half + 0.5 * pre * (1.0 - t * t) * (root + (3.0 * 0.044715 * root) * square)
        send_ref[:, at] = act
        copies[i][1].wait()
        acc_ref[...] += dot(act, wdown_ref[at, :])
    down = acc_ref[...] + bdown_ref[...]
    r4 = lax.rsqrt(jnp.mean(down * down, axis=-1, keepdims=True) + EPSILON)
    out_ref[...] = jnp.where(valid, middle_ref[...] + down * r4 * g4_ref[...], 0.0).astype(BF)
    dy = jnp.where(valid, ct_ref[...].astype(F32), 0.0)
    dz = dy * down
    vrow_ref[0:1, :] = jnp.sum(dz * r4, axis=0, keepdims=True)
    inner = jnp.mean(dz * g4_ref[...], axis=-1, keepdims=True)
    dd = (r4 * g4_ref[...] * dy - down * (r4 * r4 * r4 * inner)).astype(BF)
    dd_ref[...] = dd
    vrow_ref[1:2, :] = jnp.sum(dd.astype(F32), axis=0, keepdims=True)
    send_ref[:, DD : DD + 512] = dd_ref[:, pl.ds(pl.multiple_of((1 - core) * 512, 512), 512)]
    keep_ref[:, 2048:2560] = dd_ref[:, pl.ds(pl.multiple_of(core * 512, 512), 512)]
    acc_ref[...] = jnp.zeros_like(acc_ref)
    for part in range(2):
        which = 1 - core if part == 0 else core
        for i in range(2048 // CHUNK):
            at = pl.ds(pl.multiple_of(which * 2048 + CHUNK * i, CHUNK), CHUNK)
            dact = dot_nt(dd, wdown_ref[at, :])
            dpre = (dact * slope_ref[:, at]).astype(BF)
            vup_ref[:, at] = jnp.sum(dpre.astype(F32), axis=0, keepdims=True)
            if part == 0:
                send_ref[:, DPRE + CHUNK * i : DPRE + CHUNK * (i + 1)] = dpre
            else:
                keep_ref[:, CHUNK * i : CHUNK * (i + 1)] = dpre
            acc_ref[...] += dot_nt(dpre, wup_ref[:, at])
    dm = acc_ref[...]
    middle = middle_ref[...]
    dz = dm * middle
    vrow_ref[2:3, :] = jnp.sum(dz * r3, axis=0, keepdims=True)
    inner = jnp.mean(dz * g3_ref[...], axis=-1, keepdims=True)
    dmid = dy + r3 * g3_ref[...] * dm - middle * (r3 * r3 * r3 * inner)
    dmid_ref[...] = dmid
    proj = proj_ref[...]
    dz = dmid * proj
    vrow_ref[3:4, :] = jnp.sum(dz * r2, axis=0, keepdims=True)
    inner = jnp.mean(dz * g2_ref[...], axis=-1, keepdims=True)
    dproj = (r2 * g2_ref[...] * dmid - proj * (r2 * r2 * r2 * inner)).astype(BF)
    dd_ref[...] = dproj
    send_ref[:, DPROJ : DPROJ + 512] = dd_ref[:, pl.ds(pl.multiple_of((1 - core) * 512, 512), 512)]
    keep_ref[:, 2560:3072] = dd_ref[:, pl.ds(pl.multiple_of(core * 512, 512), 512)]
    d_out = dot_nt(dproj, wo_ref[...]).astype(BF)
    for j in range(8):
        do_ref[j] = d_out[:, 128 * j : 128 * (j + 1)]


def mlp_call(*args):
    shape = jax.ShapeDtypeStruct
    return pl.pallas_call(
        mlp_kernel,
        in_specs=[SMEM] * 3 + [VMEM] * 3 + [HBM, HBM, VMEM, HBM] + [VMEM] * 4,
        out_specs=[VMEM] * 7,
        out_shape=[
            shape((128, 1024), BF), shape((128, 1024), F32), shape((8, 128, 128), BF), shape((128, SEND), BF),
            shape((128, 3072), BF), shape((1, 4096), F32), shape((4, 1024), F32),
        ],
        scratch_shapes=[
            pltpu.VMEM((128, 1024), F32), pltpu.VMEM((128, 1024), F32), pltpu.VMEM((128, 4096), F32),
            pltpu.VMEM((128, 1024), BF), pltpu.VMEM((128, 1024), F32),
            pltpu.VMEM((1024, 1024), BF), pltpu.VMEM((1024, 4096), BF), pltpu.VMEM((4096, 1024), BF),
            pltpu.SemaphoreType.DMA((2 * 4096 // CHUNK + 1,)),
        ],
        compiler_params=pltpu.CompilerParams(vmem_limit_bytes=60 * 2**20),
        cost_estimate=pl.CostEstimate(flops=1, bytes_accessed=1024, transcendentals=0),
    )(*args)


def grad_parts(info_ref, relative, lefts, rights, outs):
    bz, by, bx = info_ref[2], info_ref[3], info_ref[4]

    def left(at, n):
        return lefts[at : at + n, :]

    def cols(at, n):
        return rights[:, pl.ds(pl.multiple_of(at, 128), n)]

    eights = lambda g: [g[:, 128 * i : 128 * (i + 1)].reshape(128, 8, 128) for i in range(g.shape[1] // 128)]
    for k2 in range(2):
        block = 2 * (relative ^ bz) + k2
        rhs = jnp.concatenate([cols(u * 512 + block * 128, 128) for u in range(3)], axis=1)
        rows = eights(dot(left(M_AT, 1024), rhs))
        outs[0][k2 ^ by] = jnp.concatenate(rows, axis=1).reshape(3072, 128).astype(BF)
    rhs = cols(2048 + 256 * (relative ^ by), 256)
    for half in range(2):
        g = dot(left(2048 * half, 2048), rhs)
        for k2 in range(2):
            part = g[:, 128 * k2 : 128 * (k2 + 1)].reshape(64, 32, 128)[:, 0:24]
            outs[1][k2 ^ bx, 1536 * half : 1536 * (half + 1), :] = part.reshape(1536, 128).astype(BF)
    first = 256 * (relative ^ bx)
    g_up = eights(dot(left(M_AT, 1024), cols(3 * 512 + first, 256)))
    g_out = eights(dot(left(O_AT, 1024), cols(2560 + first, 256)))
    for half in range(2):
        g_down = dot(left(2048 * half, 2048), cols(2048 + first, 256))
        d = slice(64 * half, 64 * (half + 1))
        for k2 in range(2):
            tail = g_down[:, 128 * k2 : 128 * (k2 + 1)].reshape(64, 32, 128)[:, 24:32]
            rows = jnp.concatenate([g_up[k2][d], tail, g_out[k2][d]], axis=1)
            outs[2][k2 ^ bz, 1536 * half : 1536 * (half + 1), :] = rows.reshape(1536, 128).astype(BF)


def grads_send_kernel(info_ref, mine_ref, keep_ref, theirs_ref, *refs):
    outs, lefts, rights = refs[0:3], refs[3], refs[4]
    for i in range(6144 // 512):
        at = slice(512 * i, 512 * (i + 1))
        lefts[at, 0:128] = mine_ref[:, at].T
        lefts[at, 128:256] = theirs_ref[:, at].T
    rights[0:128, :] = keep_ref[...]
    rights[128:256, :] = theirs_ref[:, DPRE:SEND]
    grad_parts(info_ref, 1, lefts, rights, outs)


def grads_keep_kernel(info_ref, lefts, rights, *outs):
    grad_parts(info_ref, 0, lefts, rights, outs)


PART_SHAPES = [jax.ShapeDtypeStruct((2, 3072, 128), BF)] * 3
GRAD_COST = pl.CostEstimate(flops=256 * 9 * 2**19, bytes_accessed=8 * 2**20, transcendentals=0)


def grads_send_call(info, send, keep, got):
    return pl.pallas_call(
        grads_send_kernel,
        in_specs=[SMEM, VMEM, VMEM, VMEM],
        out_specs=[VMEM] * 5,
        out_shape=PART_SHAPES + [jax.ShapeDtypeStruct((6144, 256), BF), jax.ShapeDtypeStruct((256, 3072), BF)],
        compiler_params=pltpu.CompilerParams(vmem_limit_bytes=60 * 2**20),
        cost_estimate=GRAD_COST,
    )(info, send, keep, got)


def grads_keep_call(info, lefts, rights):
    return pl.pallas_call(
        grads_keep_kernel,
        in_specs=[SMEM, VMEM, VMEM],
        out_specs=[VMEM] * 3,
        out_shape=PART_SHAPES,
        compiler_params=pltpu.CompilerParams(vmem_limit_bytes=60 * 2**20),
        cost_estimate=GRAD_COST,
    )(info, lefts, rights)


ROWS = 104


def add_kernel(*refs):
    for k, a, out in zip(refs[0:3], refs[3:6], refs[6:9]):
        out[...] = (k[0].astype(F32) + a[0].astype(F32)).astype(BF)


def add_call(kept, one):
    return pl.pallas_call(
        add_kernel,
        grid=(3,),
        in_specs=[pl.BlockSpec((1, 1024, 128), lambda j: (1, j, 0))] * 6,
        out_specs=[pl.BlockSpec((1024, 128), lambda j: (j, 0))] * 3,
        out_shape=[jax.ShapeDtypeStruct((3072, 128), BF)] * 3,
        compiler_params=pltpu.CompilerParams(vmem_limit_bytes=60 * 2**20),
        cost_estimate=pl.CostEstimate(flops=10**6, bytes_accessed=8 * 2**20, transcendentals=0),
    )(*kept, *one)


def pack_kernel(*refs):
    rows = []
    for k, a, b in zip(refs[0:3], refs[3:6], refs[6:9]):
        total = k[0].astype(F32) + a[0].astype(F32) + b[...].astype(F32)
        rows.append(total.reshape(32, 24, 128))
    rows.append(refs[9][...].astype(F32))
    refs[10][...] = jnp.concatenate(rows, axis=1).astype(BF)


def pack_call(kept, one, two, qkv):
    half = pl.BlockSpec((1, 768, 128), lambda j: (0, j, 0))
    return pl.pallas_call(
        pack_kernel,
        grid=(4,),
        in_specs=[half] * 6
        + [pl.BlockSpec((768, 128), lambda j: (j, 0))] * 3
        + [pl.BlockSpec((32, 32, 128), lambda j: (j, 0, 0))],
        out_specs=pl.BlockSpec((32, ROWS, 128), lambda j: (j, 0, 0)),
        out_shape=jax.ShapeDtypeStruct((128, ROWS, 128), BF),
        compiler_params=pltpu.CompilerParams(vmem_limit_bytes=60 * 2**20),
        cost_estimate=pl.CostEstimate(flops=10**7, bytes_accessed=10 * 2**20, transcendentals=0),
    )(*kept, *one, *two, qkv)


def bits_of(s):
    return {n: (s >> i) & 1 for i, n in enumerate(("xh", "yl", "yh", "core", "xl", "zl", "zh"))}


def sum_kernel(got_ref, w_ref, g_ref, up_ref, down_ref, wo_ref, q_ref, k_ref, v_ref, gain_ref, vec_ref):
    def total(keys, at, n):
        sums = {}
        for s in range(128):
            b = bits_of(s)
            k = tuple(b[name] for name in keys)
            v = got_ref[s].astype(F32)[at : at + n]
            sums[k] = sums[k] + v if k in sums else v
        return sums

    for (core, k1, k2), v in total(("core", "zl", "yl"), 0, 24).items():
        for u in range(3):
            at = core * 2048 + u * 512 + (2 * k1 + k2) * 128
            up_ref[:, at : at + 128] = v[8 * u : 8 * (u + 1)]
    for (core, k1, k2), v in total(("core", "yl", "xl"), 24, 24).items():
        at = core * 512 + (2 * k1 + k2) * 128
        down_ref[0:24, at : at + 128] = v
    for (core, k1, k2), v in total(("core", "xl", "zl"), 48, 24).items():
        at = (2 * k1 + k2) * 128
        up_ref[:, core * 2048 + 1536 + at : core * 2048 + 1536 + at + 128] = v[0:8]
        down_ref[24:32, core * 512 + at : core * 512 + at + 128] = v[8:16]
        wo_ref[:, core * 512 + at : core * 512 + at + 128] = v[16:24]
    weighted = jnp.zeros((8, 128), F32)
    vec = jnp.zeros((8, 128), F32)
    for (yh, yl, xh), v in total(("yh", "yl", "xh"), 72, 32).items():
        b = 4 * yh + 2 * yl + xh
        at = slice(128 * b, 128 * (b + 1))
        for i, out in enumerate((q_ref, k_ref, v_ref)):
            part = v[8 * i : 8 * (i + 1)]
            out[:, at] = part
            weighted = weighted + part * w_ref[i, :, at]
        vec = vec + v[24:32]
    gain_ref[...] = jnp.sum(weighted, axis=1, keepdims=True) / g_ref[...]
    vec_ref[...] = vec


def sum_call(got, w_rows, gain_rows):
    shape = jax.ShapeDtypeStruct
    return pl.pallas_call(
        sum_kernel,
        in_specs=[VMEM] * 3,
        out_specs=[VMEM] * 8,
        out_shape=[shape((8, 4096), F32), shape((32, 1024), F32)]
        + [shape((8, 1024), F32)] * 4
        + [shape((8, 1), F32), shape((8, 128), F32)],
        compiler_params=pltpu.CompilerParams(vmem_limit_bytes=32 * 2**20),
        cost_estimate=pl.CostEstimate(flops=10**7, bytes_accessed=3 * 2**20, transcendentals=0),
    )(got, w_rows, gain_rows)


def qkv_grads_kernel(a_ref, d_ref, vec_ref, out_ref):
    d = d_ref[...].reshape(1024, 384)
    g = dot_tn(a_ref[...], d)
    parts = [g[:, 128 * i : 128 * (i + 1)].reshape(32, 8, 128) for i in range(3)]
    first = lax.broadcasted_iota(jnp.int32, (32, 8, 128), 1) == 0
    parts.append(jnp.where(first, vec_ref[...].reshape(32, 1, 128), 0.0))
    out_ref[...] = jnp.concatenate(parts, axis=1).astype(BF)


def qkv_grads_call(a_all, d_heads, vec):
    return pl.pallas_call(
        qkv_grads_kernel,
        grid=(4,),
        in_specs=[
            pl.BlockSpec((1024, 256), lambda j: (0, j)),
            pl.BlockSpec((8, 128, 384), lambda j: (0, 0, 0)),
            pl.BlockSpec((32, 128), lambda j: (j, 0)),
        ],
        out_specs=pl.BlockSpec((32, 32, 128), lambda j: (j, 0, 0)),
        out_shape=jax.ShapeDtypeStruct((128, 32, 128), BF),
        compiler_params=pltpu.CompilerParams(vmem_limit_bytes=60 * 2**20),
        cost_estimate=pl.CostEstimate(flops=8 * 10**8, bytes_accessed=4 * 2**20, transcendentals=0),
    )(a_all, d_heads, vec)


def input_kernel(d_ref, wq_ref, wk_ref, wv_ref, x_ref, g_ref, dmid_ref, out_ref):
    step = pl.program_id(0)
    acc = jnp.where(step == 0, 0.0, out_ref[...])
    for i, w_ref in enumerate((wq_ref, wk_ref, wv_ref)):
        d = jnp.concatenate([d_ref[j, :, 128 * i : 128 * (i + 1)] for j in range(2)], axis=1)
        acc = acc + dot_nt(d, w_ref[...])
    out_ref[...] = acc

    @pl.when(step == 3)
    def _():
        x = x_ref[...].astype(F32)
        r = lax.rsqrt(jnp.mean(x * x, axis=-1, keepdims=True) + EPSILON)
        dz = out_ref[...] * g_ref[...]
        inner = jnp.mean(dz * x, axis=-1, keepdims=True)
        out_ref[...] = dmid_ref[...] + r * dz - x * (r * r * r * inner)


def input_call(d_mine, wq, wk, wv, x, gain, dmid):
    whole = lambda shape: pl.BlockSpec(shape, lambda j: (0,) * len(shape))
    col = pl.BlockSpec((1024, 256), lambda j: (0, j))
    return pl.pallas_call(
        input_kernel,
        grid=(4,),
        in_specs=[pl.BlockSpec((2, 128, 384), lambda j: (j, 0, 0)), col, col, col, whole((128, 1024)), whole((1, 1024)), whole((128, 1024))],
        out_specs=whole((128, 1024)),
        out_shape=jax.ShapeDtypeStruct((128, 1024), F32),
        compiler_params=pltpu.CompilerParams(vmem_limit_bytes=32 * 2**20),
        cost_estimate=pl.CostEstimate(flops=2 * 128 * 1024 * 3072, bytes_accessed=7 * 2**20, transcendentals=0),
    )(d_mine, wq, wk, wv, x, gain, dmid)


def local(
    tokens, lengths, order, w_query, w_key, w_value, w_out, w_up, b_up, w_down, b_down,
    gain_attn_in, gain_attn_out, gain_mlp_in, gain_mlp_out, cotangent,
):
    z, xl, core, y, xh = (lax.axis_index(a) for a in ALL)
    my_blk = y * 2 + xh
    me = ((z * 2 + xl) * 2 + core) * 8 + my_blk
    info = jnp.stack([core, my_blk, z % 2, y % 2, xl]).astype(jnp.int32)
    row = lambda v: v.reshape(1, -1)
    tie = lax.optimization_barrier

    qkv, spread = qkv_call(info, order, lengths, tokens, row(gain_attn_in), w_query, w_key, w_value)
    qkv_heads = lax.all_to_all(qkv, BLK, 0, 0, tiled=True)

    late_lengths, _ = tie((lengths, qkv))
    lengths_row = late_lengths[0]
    group_pos = jnp.arange(1024, dtype=jnp.int32)
    start = jnp.zeros((1024,), jnp.int32)
    end = jnp.int32(0)
    for e in range(6):
        end = end + lengths_row[e]
        start = jnp.where(group_pos >= end, end, start)
    cos_all, sin_all = rotary_tables(group_pos - start)

    qkv_heads, cos_all, sin_all = tie((qkv_heads, cos_all, sin_all))
    out_heads, pos_qkv, lse = attend_call(order, lengths, qkv_heads)
    out_mine = lax.all_to_all(out_heads, BLK, 0, 0, tiled=True)
    out_mine, spread = tie((out_mine, spread))
    attn_all = lax.all_to_all(spread, BLK, 0, 0, tiled=True).reshape(1024, 1024)
    output, d_middle, d_out, send, keep, v_up, v_row = mlp_call(
        info, order, lengths, out_mine, tokens, cotangent, w_out, w_up, row(b_up), w_down, row(b_down),
        row(gain_attn_out), row(gain_mlp_in), row(gain_mlp_out),
    )
    send, keep, d_out, attn_all = tie((send, keep, d_out, attn_all))
    d_out_heads = lax.all_to_all(d_out, BLK, 0, 0, tiled=True)
    got = lax.ppermute(send, ALL, SWAP_CORES)
    *sent, lefts, rights = grads_send_call(info, send, keep, got)
    sent, d_out_heads = tie((sent, d_out_heads))
    one = [lax.ppermute(p, ALL, to) for p, to in zip(sent, STEPS[0])]
    kept = grads_keep_call(info, lefts, rights)
    lse, kept = tie((lse, kept))
    d_heads = attend_back_call(order, lengths, pos_qkv, lse, cos_all, sin_all, d_out_heads)
    d_mine = lax.all_to_all(d_heads, BLK, 0, 0, tiled=True)

    added, d_grads = tie((add_call(kept, one), d_heads))
    two = [lax.ppermute(p, ALL, to) for p, to in zip(added, STEPS[1])]
    v_up, v_row, _ = tie((v_up, v_row, d_heads))
    vectors = jnp.concatenate(
        [v_up.reshape(128, 32)] + [v_row[i].reshape(128, 8) for i in (1, 3, 2, 0)] + [jnp.zeros((128, 64), F32)], axis=1
    )
    packed = pack_call(kept, one, two, qkv_grads_call(attn_all, d_grads, vectors))
    got_all = lax.all_to_all(packed, ALL, 0, 0, tiled=True)

    grad_tokens = input_call(d_mine, w_query, w_key, w_value, tokens, row(gain_attn_in), d_middle)
    my_rows = lambda w: lax.dynamic_slice_in_dim(w, me * 8, 8, 0).astype(F32)
    w_rows = jnp.stack([my_rows(w) for w in (w_query, w_key, w_value)])
    gain_rows = lax.dynamic_slice_in_dim(gain_attn_in, me * 8, 8, 0).reshape(8, 1)
    grad_w_up, grad_w_down, grad_w_out, grad_w_query, grad_w_key, grad_w_value, grad_gain_attn_in, vec = sum_call(
        got_all, w_rows, gain_rows
    )
    vec = vec[0]
    return (
        output, grad_tokens, grad_w_query, grad_w_key, grad_w_value, grad_w_out, grad_w_up, vec[0:32], grad_w_down,
        vec[32:40], grad_gain_attn_in.reshape(8), vec[40:48], vec[48:56], vec[56:64],
    )


def solution(mesh):
    split = Mesh(np.asarray(mesh.devices).reshape(4, 2, 2, 4, 2), ALL)
    every = P(ALL, None)
    flat = P(ALL)
    return jax.shard_map(
        local,
        mesh=split,
        in_specs=(every, P(("z", "xl", "core"), None)) + (P(),) * 13 + (every,),
        out_specs=(every,) * 7 + (flat, every) + (flat,) * 5,
        check_vma=False,
    )
```

```python
import functools
import math

import jax
import jax.numpy as jnp
import numpy as np
from jax import lax
from jax.experimental import pallas as pl
from jax.experimental.pallas import tpu as pltpu
from jax.sharding import Mesh
from jax.sharding import PartitionSpec as P

HEADS = 16
EPSILON = 1e-05
NEGATIVE = -1e30
ALL = ("z", "xl", "core", "y", "xh")
BLK = ("y", "xh")
BF = jnp.bfloat16
F32 = jnp.float32
TILES = ((0, 0, 256), (256, 0, 512), (512, 0, 768), (768, 512, 1024))


SMEM = pl.BlockSpec(memory_space=pltpu.SMEM)
VMEM = pl.BlockSpec(memory_space=pltpu.VMEM)
HBM = pl.BlockSpec(memory_space=pltpu.HBM)


def device_index(z, x, c, y):
    return (((z % 4) * 2 + (x % 4) % 2) * 2 + c) * 8 + (y % 4) * 2 + (x % 4) // 2


def pairs_of(f):
    return [
        (device_index(z, x, c, y), device_index(*f(z, x, c, y)))
        for z in range(4)
        for x in range(4)
        for c in range(2)
        for y in range(4)
    ]


def up(v):
    return v ^ 1


def down_pair(v):
    return ((v + 1) ^ 1) - 1


def flip(axis, by_core):
    way = (up, down_pair)

    def there(z, x, c, y):
        move = way[by_core[c]]
        return (
            move(z) if axis == "z" else z,
            move(x) if axis == "x" else x,
            c,
            move(y) if axis == "y" else y,
        )

    return pairs_of(there)


ACROSS = pairs_of(lambda z, x, c, y: (z, x + 2, c, y))
ALONG = [pairs_of(lambda z, x, c, y, by=by: (z, x, c, y + by)) for by in (1, 2, 3)]
SWAP_CORES = pairs_of(lambda z, x, c, y: (z, x, 1 - c, y))
STEPS = (
    (flip("z", (0, 1)), flip("y", (0, 1)), flip("x", (0, 1))),
    (flip("y", (0, 1)), flip("x", (0, 1)), flip("z", (0, 1))),
)


def half_swap(x):
    n = x.shape[1]
    lane = lax.broadcasted_iota(jnp.int32, x.shape, 1) % 64
    return jnp.where(lane < 32, pltpu.roll(x, n - 32, 1), pltpu.roll(x, 32, 1))


def rotary_tables(relative):
    freqs = jnp.exp(jnp.arange(32, dtype=F32) * (-math.log(10000.0) / 32))
    angles = relative.astype(F32)[:, None] * freqs[None, :]
    c, s = jnp.cos(angles), jnp.sin(angles)
    return jnp.concatenate([c, c, c, c], axis=1), jnp.concatenate([-s, s, -s, s], axis=1)


def dot(a, b):
    return jnp.dot(a, b, preferred_element_type=F32)


def dot_nt(a, b):
    return lax.dot_general(a, b, (((1,), (1,)), ((), ())), preferred_element_type=F32)


def dot_tn(a, b):
    return lax.dot_general(a, b, (((0,), (0,)), ((), ())), preferred_element_type=F32)


def column_positions(info_ref, order_ref, len_ref):
    row = lax.broadcasted_iota(jnp.int32, (128, 1), 0)
    one, two = order_ref[0, info_ref[1]], order_ref[1, info_ref[1]]
    pos = jnp.where(row < 64, one * 64 + row, two * 64 + row - 64)
    start = jnp.zeros((128, 1), jnp.int32)
    end = jnp.int32(0)
    for e in range(6):
        end = end + len_ref[0, e]
        start = jnp.where(pos >= end, end, start)
    return pos, start, end


def qkv_kernel(info_ref, order_ref, len_ref, x_ref, g_ref, wq_hbm, wk_hbm, wv_hbm, out_ref, wq, wk, wv, sems):
    copies = [
        pltpu.make_async_copy(hbm.at[:, 512 * h : 512 * (h + 1)], w.at[:, 512 * h : 512 * (h + 1)], sems.at[2 * i + h])
        for i, (hbm, w) in enumerate(((wq_hbm, wq), (wk_hbm, wk), (wv_hbm, wv)))
        for h in range(2)
    ]
    for copy in copies:
        copy.start()
    x = x_ref[...].astype(F32)
    factor = lax.rsqrt(jnp.mean(x * x, axis=-1, keepdims=True) + EPSILON)
    a = (x * factor * g_ref[...]).astype(BF)
    pos, start, _ = column_positions(info_ref, order_ref, len_ref)
    lane = lax.broadcasted_iota(jnp.int32, (1, 128), 1)
    freqs = jnp.exp((lane % 32).astype(F32) * (-math.log(10000.0) / 32))
    angles = (pos - start).astype(F32) * freqs
    cos = jnp.cos(angles)
    sine = jnp.sin(angles)
    sin = jnp.where(lane % 64 < 32, -sine, sine)
    cos = jnp.concatenate([cos] * 4, axis=1)
    sin = jnp.concatenate([sin] * 4, axis=1)
    for i, w in enumerate((wq, wk, wv)):
        for h in range(2):
            copies[2 * i + h].wait()
            y = dot(a, w[:, 512 * h : 512 * (h + 1)])
            if i < 2:
                y = y * cos + half_swap(y) * sin
            y = y.astype(BF)
            for j in range(4):
                out_ref[4 * h + j, :, 128 * i : 128 * (i + 1)] = y[:, 128 * j : 128 * (j + 1)]


def qkv_call(info, order, lengths, x, gain, wq, wk, wv):
    return pl.pallas_call(
        qkv_kernel,
        in_specs=[SMEM, SMEM, SMEM, VMEM, VMEM, HBM, HBM, HBM],
        out_specs=VMEM,
        out_shape=jax.ShapeDtypeStruct((8, 128, 384), BF),
        scratch_shapes=[pltpu.VMEM((1024, 1024), BF)] * 3 + [pltpu.SemaphoreType.DMA((6,))],
        compiler_params=pltpu.CompilerParams(vmem_limit_bytes=60 * 2**20),
        cost_estimate=pl.CostEstimate(flops=2 * 128 * 1024 * 3072, bytes_accessed=7 * 2**20, transcendentals=0),
    )(info, order, lengths, x, gain, wq, wk, wv)


def allowed_mask(len_ref, q0, k0, k1):
    qpos = q0 + lax.broadcasted_iota(jnp.int32, (1, 256), 1)
    start = jnp.zeros((1, 256), jnp.int32)
    end = jnp.int32(0)
    for e in range(6):
        end = end + len_ref[0, e]
        start = jnp.where(qpos >= end, end, start)
    kpos = k0 + lax.broadcasted_iota(jnp.int32, (k1 - k0, 256), 0)
    return (kpos >= start) & (kpos <= qpos)


def attend_kernel(order_ref, len_ref, qkv_ref, out_ref, pos_ref, lse_ref, o_ref):
    for b in range(8):
        for j in range(2):
            at = pl.ds(pl.multiple_of(order_ref[j, b] * 64, 64), 64)
            pos_ref[at, :] = qkv_ref[b, 64 * j : 64 * (j + 1), :]
    first = lax.broadcasted_iota(jnp.int32, (1, 128), 1) < 64
    v_t = pos_ref[:, 256:384].T
    for q0, k0, k1 in TILES:
        q = pos_ref[q0 : q0 + 256, 0:128].astype(F32) * 0.125
        k = pos_ref[k0:k1, 128:256]
        mask = allowed_mask(len_ref, q0, k0, k1)
        outs = []
        for h in range(2):
            q_h = jnp.where(first if h == 0 else ~first, q, 0.0).astype(BF)
            s = jnp.where(mask, dot_nt(k, q_h), NEGATIVE)
            top = jnp.max(s, axis=0, keepdims=True)
            p = jnp.exp(s - top)
            total = jnp.sum(p, axis=0, keepdims=True)
            lse_ref[h : h + 1, q0 : q0 + 256] = top + jnp.log(total)
            p = (p * (1.0 / total)).astype(BF)
            outs.append(dot(v_t[64 * h : 64 * (h + 1), k0:k1], p))
        o_ref[q0 : q0 + 256, :] = jnp.concatenate(outs, axis=0).T.astype(BF)
    for b in range(8):
        for j in range(2):
            at = pl.ds(pl.multiple_of(order_ref[j, b] * 64, 64), 64)
            out_ref[b, 64 * j : 64 * (j + 1), :] = o_ref[at, :]


def attend_call(order, lengths, qkv):
    return pl.pallas_call(
        attend_kernel,
        in_specs=[SMEM, SMEM, VMEM],
        out_specs=[VMEM] * 3,
        out_shape=[
            jax.ShapeDtypeStruct((8, 128, 128), BF),
            jax.ShapeDtypeStruct((1024, 384), BF),
            jax.ShapeDtypeStruct((2, 1024), F32),
        ],
        scratch_shapes=[pltpu.VMEM((1024, 128), BF)],
        compiler_params=pltpu.CompilerParams(vmem_limit_bytes=24 * 2**20),
        cost_estimate=pl.CostEstimate(flops=2 * 10**9, bytes_accessed=3 * 2**20, transcendentals=2 * 10**6),
    )(order, lengths, qkv)


def attend_back_kernel(order_ref, len_ref, pos_ref, lse_ref, cos_ref, sin_ref, do_ref, out_ref, d_ref, dk_ref, dv_ref, dq_ref):
    for b in range(8):
        for j in range(2):
            at = pl.ds(pl.multiple_of(order_ref[j, b] * 64, 64), 64)
            d_ref[at, 0:128] = do_ref[b, 64 * j : 64 * (j + 1), :]
    first = lax.broadcasted_iota(jnp.int32, (1, 128), 1) < 64
    k_t = pos_ref[:, 128:256].T
    dk_ref[...] = jnp.zeros_like(dk_ref)
    dv_ref[...] = jnp.zeros_like(dv_ref)
    for q0, k0, k1 in TILES:
        q = pos_ref[q0 : q0 + 256, 0:128].astype(F32) * 0.125
        do = d_ref[q0 : q0 + 256, 0:128]
        k = pos_ref[k0:k1, 128:256]
        v = pos_ref[k0:k1, 256:384]
        mask = allowed_mask(len_ref, q0, k0, k1)
        outs = []
        for h in range(2):
            pick = first if h == 0 else ~first
            q_h = jnp.where(pick, q, 0.0).astype(BF)
            do_h = jnp.where(pick, do.astype(F32), 0.0).astype(BF)
            s = jnp.where(mask, dot_nt(k, q_h), NEGATIVE)
            p = jnp.exp(s - lse_ref[h : h + 1, q0 : q0 + 256])
            dp = dot_nt(v, do_h)
            delta = jnp.sum(p * dp, axis=0, keepdims=True)
            ds = (p * (dp - delta)).astype(BF)
            dv_ref[k0:k1, :] += dot(p.astype(BF), do_h)
            dk_ref[k0:k1, :] += dot(ds, q_h)
            outs.append(dot(k_t[64 * h : 64 * (h + 1), k0:k1], ds))
        dq_ref[q0 : q0 + 256, :] = jnp.concatenate(outs, axis=0).T * 0.125
    cos, sin = cos_ref[...], sin_ref[...]
    dq, dk = dq_ref[...], dk_ref[...]
    d_ref[:, 0:128] = (dq * cos - half_swap(dq) * sin).astype(BF)
    d_ref[:, 128:256] = (dk * cos - half_swap(dk) * sin).astype(BF)
    d_ref[:, 256:384] = dv_ref[...].astype(BF)
    for b in range(8):
        for j in range(2):
            at = pl.ds(pl.multiple_of(order_ref[j, b] * 64, 64), 64)
            out_ref[b, 64 * j : 64 * (j + 1), :] = d_ref[at, :]


def attend_back_call(order, lengths, pos, lse, cos, sin, d_out):
    return pl.pallas_call(
        attend_back_kernel,
        in_specs=[SMEM, SMEM, VMEM, VMEM, VMEM, VMEM, VMEM],
        out_specs=VMEM,
        out_shape=jax.ShapeDtypeStruct((8, 128, 384), BF),
        scratch_shapes=[
            pltpu.VMEM((1024, 384), BF),
            pltpu.VMEM((1024, 128), F32),
            pltpu.VMEM((1024, 128), F32),
            pltpu.VMEM((1024, 128), F32),
        ],
        compiler_params=pltpu.CompilerParams(vmem_limit_bytes=32 * 2**20),
        cost_estimate=pl.CostEstimate(flops=1, bytes_accessed=1024, transcendentals=0),
    )(order, lengths, pos, lse, cos, sin, d_out)


ACT, M_AT, O_AT, DPRE, DD, DPROJ, SEND = 0, 4096, 5120, 6144, 8192, 8704, 9216
CHUNK = 1024


def mlp_kernel(info_ref, order_ref, len_ref, o_ref, x_ref, ct_ref, wo_hbm, wup_hbm, bup_ref, wdown_hbm, bdown_ref,
               g2_ref, g3_ref, g4_ref,
               out_ref, dmid_ref, do_ref, send_ref, keep_ref, vup_ref, vrow_ref,
               proj_ref, middle_ref, slope_ref, dd_ref, acc_ref, wo_ref, wup_ref, wdown_ref, sems):
    core = info_ref[0]
    count = 4096 // CHUNK
    copy_out = pltpu.make_async_copy(wo_hbm, wo_ref, sems.at[2 * count])
    copy_out.start()
    copies = []
    for i in range(count):
        at = slice(CHUNK * i, CHUNK * (i + 1))
        copies.append((
            pltpu.make_async_copy(wup_hbm.at[:, at], wup_ref.at[:, at], sems.at[2 * i]),
            pltpu.make_async_copy(wdown_hbm.at[at, :], wdown_ref.at[at, :], sems.at[2 * i + 1]),
        ))
        copies[-1][0].start()
        copies[-1][1].start()
    pos, _, end = column_positions(info_ref, order_ref, len_ref)
    valid = pos < end
    o = jnp.concatenate([o_ref[j] for j in range(8)], axis=1)
    send_ref[:, O_AT : O_AT + 1024] = o
    copy_out.wait()
    proj = dot(o, wo_ref[...])
    proj_ref[...] = proj
    r2 = lax.rsqrt(jnp.mean(proj * proj, axis=-1, keepdims=True) + EPSILON)
    middle = x_ref[...].astype(F32) + proj * r2 * g2_ref[...]
    middle_ref[...] = middle
    r3 = lax.rsqrt(jnp.mean(middle * middle, axis=-1, keepdims=True) + EPSILON)
    m = (middle * r3 * g3_ref[...]).astype(BF)
    send_ref[:, M_AT : M_AT + 1024] = m
    acc_ref[...] = jnp.zeros_like(acc_ref)
    root = math.sqrt(2.0 / math.pi)
    for i in range(4096 // CHUNK):
        at = slice(CHUNK * i, CHUNK * (i + 1))
        copies[i][0].wait()
        pre = dot(m, wup_ref[:, at]) + bup_ref[:, at]
        square = pre * pre
        t = jnp.tanh(root * (pre + 0.044715 * (square * pre)))
        half = 0.5 * (1.0 + t)
        act = (pre * half).astype(BF)
        slope_ref[:, at] = half + 0.5 * pre * (1.0 - t * t) * (root + (3.0 * 0.044715 * root) * square)
        send_ref[:, at] = act
        copies[i][1].wait()
        acc_ref[...] += dot(act, wdown_ref[at, :])
    down = acc_ref[...] + bdown_ref[...]
    r4 = lax.rsqrt(jnp.mean(down * down, axis=-1, keepdims=True) + EPSILON)
    out_ref[...] = jnp.where(valid, middle_ref[...] + down * r4 * g4_ref[...], 0.0).astype(BF)
    dy = jnp.where(valid, ct_ref[...].astype(F32), 0.0)
    dz = dy * down
    vrow_ref[0:1, :] = jnp.sum(dz * r4, axis=0, keepdims=True)
    inner = jnp.mean(dz * g4_ref[...], axis=-1, keepdims=True)
    dd = (r4 * g4_ref[...] * dy - down * (r4 * r4 * r4 * inner)).astype(BF)
    dd_ref[...] = dd
    vrow_ref[1:2, :] = jnp.sum(dd.astype(F32), axis=0, keepdims=True)
    send_ref[:, DD : DD + 512] = dd_ref[:, pl.ds(pl.multiple_of((1 - core) * 512, 512), 512)]
    keep_ref[:, 2048:2560] = dd_ref[:, pl.ds(pl.multiple_of(core * 512, 512), 512)]
    acc_ref[...] = jnp.zeros_like(acc_ref)
    for part in range(2):
        which = 1 - core if part == 0 else core
        for i in range(2048 // CHUNK):
            at = pl.ds(pl.multiple_of(which * 2048 + CHUNK * i, CHUNK), CHUNK)
            dact = dot_nt(dd, wdown_ref[at, :])
            dpre = (dact * slope_ref[:, at]).astype(BF)
            vup_ref[:, at] = jnp.sum(dpre.astype(F32), axis=0, keepdims=True)
            if part == 0:
                send_ref[:, DPRE + CHUNK * i : DPRE + CHUNK * (i + 1)] = dpre
            else:
                keep_ref[:, CHUNK * i : CHUNK * (i + 1)] = dpre
            acc_ref[...] += dot_nt(dpre, wup_ref[:, at])
    dm = acc_ref[...]
    middle = middle_ref[...]
    dz = dm * middle
    vrow_ref[2:3, :] = jnp.sum(dz * r3, axis=0, keepdims=True)
    inner = jnp.mean(dz * g3_ref[...], axis=-1, keepdims=True)
    dmid = dy + r3 * g3_ref[...] * dm - middle * (r3 * r3 * r3 * inner)
    dmid_ref[...] = dmid
    proj = proj_ref[...]
    dz = dmid * proj
    vrow_ref[3:4, :] = jnp.sum(dz * r2, axis=0, keepdims=True)
    inner = jnp.mean(dz * g2_ref[...], axis=-1, keepdims=True)
    dproj = (r2 * g2_ref[...] * dmid - proj * (r2 * r2 * r2 * inner)).astype(BF)
    dd_ref[...] = dproj
    send_ref[:, DPROJ : DPROJ + 512] = dd_ref[:, pl.ds(pl.multiple_of((1 - core) * 512, 512), 512)]
    keep_ref[:, 2560:3072] = dd_ref[:, pl.ds(pl.multiple_of(core * 512, 512), 512)]
    d_out = dot_nt(dproj, wo_ref[...]).astype(BF)
    for j in range(8):
        do_ref[j] = d_out[:, 128 * j : 128 * (j + 1)]


def mlp_call(*args):
    shape = jax.ShapeDtypeStruct
    return pl.pallas_call(
        mlp_kernel,
        in_specs=[SMEM] * 3 + [VMEM] * 3 + [HBM, HBM, VMEM, HBM] + [VMEM] * 4,
        out_specs=[VMEM] * 7,
        out_shape=[
            shape((128, 1024), BF), shape((128, 1024), F32), shape((8, 128, 128), BF), shape((128, SEND), BF),
            shape((128, 3072), BF), shape((1, 4096), F32), shape((4, 1024), F32),
        ],
        scratch_shapes=[
            pltpu.VMEM((128, 1024), F32), pltpu.VMEM((128, 1024), F32), pltpu.VMEM((128, 4096), F32),
            pltpu.VMEM((128, 1024), BF), pltpu.VMEM((128, 1024), F32),
            pltpu.VMEM((1024, 1024), BF), pltpu.VMEM((1024, 4096), BF), pltpu.VMEM((4096, 1024), BF),
            pltpu.SemaphoreType.DMA((2 * 4096 // CHUNK + 1,)),
        ],
        compiler_params=pltpu.CompilerParams(vmem_limit_bytes=60 * 2**20),
        cost_estimate=pl.CostEstimate(flops=4 * 128 * 9 * 2**20, bytes_accessed=20 * 2**20, transcendentals=2**19),
    )(*args)


def grad_parts(info_ref, relative, lefts, rights, outs, copies):
    bz, by, bx = info_ref[2], info_ref[3], info_ref[4]

    def left(at, n):
        return lefts[at : at + n, :]

    def cols(at, n):
        return rights[:, pl.ds(pl.multiple_of(at, 128), n)]

    eights = lambda g: [g[:, 128 * i : 128 * (i + 1)].reshape(128, 8, 128) for i in range(g.shape[1] // 128)]
    for k2 in range(2):
        block = 2 * (relative ^ bz) + k2
        rhs = jnp.concatenate([cols(u * 512 + block * 128, 128) for u in range(3)], axis=1)
        rows = eights(dot(left(M_AT, 1024), rhs))
        outs[0][k2 ^ by] = jnp.concatenate(rows, axis=1).reshape(3072, 128).astype(BF)
    copies[0].start()
    rhs = cols(2048 + 256 * (relative ^ by), 256)
    for half in range(2):
        g = dot(left(2048 * half, 2048), rhs)
        for k2 in range(2):
            part = g[:, 128 * k2 : 128 * (k2 + 1)].reshape(64, 32, 128)[:, 0:24]
            outs[1][k2 ^ bx, 1536 * half : 1536 * (half + 1), :] = part.reshape(1536, 128).astype(BF)
    copies[1].start()
    first = 256 * (relative ^ bx)
    g_up = eights(dot(left(M_AT, 1024), cols(3 * 512 + first, 256)))
    g_out = eights(dot(left(O_AT, 1024), cols(2560 + first, 256)))
    for half in range(2):
        g_down = dot(left(2048 * half, 2048), cols(2048 + first, 256))
        d = slice(64 * half, 64 * (half + 1))
        for k2 in range(2):
            tail = g_down[:, 128 * k2 : 128 * (k2 + 1)].reshape(64, 32, 128)[:, 24:32]
            rows = jnp.concatenate([g_up[k2][d], tail, g_out[k2][d]], axis=1)
            outs[2][k2 ^ bz, 1536 * half : 1536 * (half + 1), :] = rows.reshape(1536, 128).astype(BF)
    copies[2].start()


def turn(mine, theirs, lefts):
    for i in range(6144 // 512):
        at = slice(512 * i, 512 * (i + 1))
        lefts[at, 0:128] = mine[:, at].T
        lefts[at, 128:256] = theirs[:, at].T


def grads_kernel(relative, info_ref, mine_ref, keep_ref, theirs_ref, p_hbm, q_hbm, r_hbm, lefts, rights, p_ref, q_ref, r_ref, sems):
    turn(mine_ref, theirs_ref, lefts)
    rights[0:128, :] = keep_ref[...]
    rights[128:256, :] = theirs_ref[:, DPRE:SEND]
    copies = [
        pltpu.make_async_copy(ref, hbm, sems.at[i])
        for i, (ref, hbm) in enumerate(((p_ref, p_hbm), (q_ref, q_hbm), (r_ref, r_hbm)))
    ]
    grad_parts(info_ref, relative, lefts, rights, (p_ref, q_ref, r_ref), copies)
    for copy in copies:
        copy.wait()


PART_SHAPES = [jax.ShapeDtypeStruct((2, 3072, 128), BF)] * 3


def grads_call(relative, info, send, keep, got):
    return pl.pallas_call(
        functools.partial(grads_kernel, relative),
        in_specs=[SMEM, VMEM, VMEM, VMEM],
        out_specs=[HBM] * 3,
        out_shape=PART_SHAPES,
        scratch_shapes=[pltpu.VMEM((6144, 256), BF), pltpu.VMEM((256, 3072), BF)]
        + [pltpu.VMEM((2, 3072, 128), BF)] * 3
        + [pltpu.SemaphoreType.DMA((3,))],
        compiler_params=pltpu.CompilerParams(vmem_limit_bytes=60 * 2**20),
        cost_estimate=pl.CostEstimate(flops=1, bytes_accessed=1024, transcendentals=0),
    )(info, send, keep, got)


ROWS = 104


def add_kernel(*refs):
    for k, a, out in zip(refs[0:3], refs[3:6], refs[6:9]):
        out[...] = k[0] + a[0]


def add_call(kept, one):
    return pl.pallas_call(
        add_kernel,
        grid=(2,),
        in_specs=[pl.BlockSpec((1, 1536, 128), lambda j: (1, j, 0))] * 6,
        out_specs=[pl.BlockSpec((1536, 128), lambda j: (j, 0))] * 3,
        out_shape=[jax.ShapeDtypeStruct((3072, 128), BF)] * 3,
        compiler_params=pltpu.CompilerParams(vmem_limit_bytes=60 * 2**20),
        cost_estimate=pl.CostEstimate(flops=1, bytes_accessed=1024, transcendentals=0),
    )(*kept, *one)


def pack_kernel(*refs):
    rows = []
    for k, a, b in zip(refs[0:3], refs[3:6], refs[6:9]):
        total = k[0].astype(F32) + a[0].astype(F32) + b[...].astype(F32)
        rows.append(total.reshape(32, 24, 128))
    rows.append(refs[9][...].astype(F32))
    refs[10][...] = jnp.concatenate(rows, axis=1).astype(BF)


def pack_call(kept, one, two, qkv):
    half = pl.BlockSpec((1, 768, 128), lambda j: (0, j, 0))
    return pl.pallas_call(
        pack_kernel,
        grid=(4,),
        in_specs=[half] * 6
        + [pl.BlockSpec((768, 128), lambda j: (j, 0))] * 3
        + [pl.BlockSpec((32, 32, 128), lambda j: (j, 0, 0))],
        out_specs=pl.BlockSpec((32, ROWS, 128), lambda j: (j, 0, 0)),
        out_shape=jax.ShapeDtypeStruct((128, ROWS, 128), BF),
        compiler_params=pltpu.CompilerParams(vmem_limit_bytes=60 * 2**20),
        cost_estimate=pl.CostEstimate(flops=1, bytes_accessed=1024, transcendentals=0),
    )(*kept, *one, *two, qkv)


def bits_of(s):
    return {n: (s >> i) & 1 for i, n in enumerate(("xh", "yl", "yh", "core", "xl", "zl", "zh"))}


def sum_kernel(got_ref, w_ref, g_ref, up_ref, down_ref, wo_ref, q_ref, k_ref, v_ref, gain_ref, vec_ref):
    def total(keys, at, n):
        sums = {}
        for s in range(128):
            b = bits_of(s)
            k = tuple(b[name] for name in keys)
            v = got_ref[s].astype(F32)[at : at + n]
            sums[k] = sums[k] + v if k in sums else v
        return sums

    for (core, k1, k2), v in total(("core", "zl", "yl"), 0, 24).items():
        for u in range(3):
            at = core * 2048 + u * 512 + (2 * k1 + k2) * 128
            up_ref[:, at : at + 128] = v[8 * u : 8 * (u + 1)]
    for (core, k1, k2), v in total(("core", "yl", "xl"), 24, 24).items():
        at = core * 512 + (2 * k1 + k2) * 128
        down_ref[0:24, at : at + 128] = v
    for (core, k1, k2), v in total(("core", "xl", "zl"), 48, 24).items():
        at = (2 * k1 + k2) * 128
        up_ref[:, core * 2048 + 1536 + at : core * 2048 + 1536 + at + 128] = v[0:8]
        down_ref[24:32, core * 512 + at : core * 512 + at + 128] = v[8:16]
        wo_ref[:, core * 512 + at : core * 512 + at + 128] = v[16:24]
    weighted = jnp.zeros((8, 128), F32)
    vec = jnp.zeros((8, 128), F32)
    for (yh, yl, xh), v in total(("yh", "yl", "xh"), 72, 32).items():
        b = 4 * yh + 2 * yl + xh
        at = slice(128 * b, 128 * (b + 1))
        for i, out in enumerate((q_ref, k_ref, v_ref)):
            part = v[8 * i : 8 * (i + 1)]
            out[:, at] = part
            weighted = weighted + part * w_ref[i, :, at]
        vec = vec + v[24:32]
    gain_ref[...] = jnp.sum(weighted, axis=1, keepdims=True) / g_ref[...]
    vec_ref[...] = vec


def sum_call(got, w_rows, gain_rows):
    shape = jax.ShapeDtypeStruct
    return pl.pallas_call(
        sum_kernel,
        in_specs=[VMEM] * 3,
        out_specs=[VMEM] * 8,
        out_shape=[shape((8, 4096), F32), shape((32, 1024), F32)]
        + [shape((8, 1024), F32)] * 4
        + [shape((8, 1), F32), shape((8, 128), F32)],
        compiler_params=pltpu.CompilerParams(vmem_limit_bytes=16 * 2**20),
        cost_estimate=pl.CostEstimate(flops=10**7, bytes_accessed=3 * 2**20, transcendentals=0),
    )(got, w_rows, gain_rows)


def qkv_grads_kernel(info_ref, x0_ref, x1_ref, x2_ref, x3_ref, gain_ref, d_ref, vec_ref, out_ref, a_ref, dd_ref):
    step = pl.program_id(0)

    @pl.when(step == 0)
    def _():
        y, xh = info_ref[1] // 2, info_ref[1] % 2
        for back, ref in enumerate((x0_ref, x1_ref, x2_ref, x3_ref)):
            source = ((y + 4 - back) % 4) * 2
            for i in range(2):
                at = slice(256 * back + 128 * i, 256 * back + 128 * (i + 1))
                x = ref[i].astype(F32)
                factor = lax.rsqrt(jnp.mean(x * x, axis=-1, keepdims=True) + EPSILON)
                a = (x * factor * gain_ref[...]).astype(BF)
                for j in range(4):
                    a_ref[j, at, :] = a[:, 256 * j : 256 * (j + 1)]
                dd_ref[at, :] = d_ref[source + (xh if i == 0 else 1 - xh)]

    g = dot_tn(a_ref[step], dd_ref[...])
    parts = [g[:, 128 * i : 128 * (i + 1)].reshape(32, 8, 128) for i in range(3)]
    first = lax.broadcasted_iota(jnp.int32, (32, 8, 128), 1) == 0
    parts.append(jnp.where(first, vec_ref[...].reshape(32, 1, 128), 0.0))
    out_ref[...] = jnp.concatenate(parts, axis=1).astype(BF)


def qkv_grads_call(info, pairs, gain, d_heads, vec):
    whole = lambda *shape: pl.BlockSpec(shape, lambda j: (0,) * len(shape))
    return pl.pallas_call(
        qkv_grads_kernel,
        grid=(4,),
        in_specs=[SMEM]
        + [whole(2, 128, 1024)] * 4
        + [whole(1, 1024), whole(8, 128, 384), pl.BlockSpec((32, 128), lambda j: (j, 0))],
        out_specs=pl.BlockSpec((32, 32, 128), lambda j: (j, 0, 0)),
        out_shape=jax.ShapeDtypeStruct((128, 32, 128), BF),
        scratch_shapes=[pltpu.VMEM((4, 1024, 256), BF), pltpu.VMEM((1024, 384), BF)],
        compiler_params=pltpu.CompilerParams(vmem_limit_bytes=60 * 2**20),
        cost_estimate=pl.CostEstimate(flops=1, bytes_accessed=1024, transcendentals=0),
    )(info, *pairs, gain, d_heads, vec)


def input_kernel(d_ref, wq_ref, wk_ref, wv_ref, x_ref, g_ref, dmid_ref, out_ref):
    step = pl.program_id(0)
    acc = jnp.where(step == 0, 0.0, out_ref[...])
    for i, w_ref in enumerate((wq_ref, wk_ref, wv_ref)):
        d = jnp.concatenate([d_ref[j, :, 128 * i : 128 * (i + 1)] for j in range(2)], axis=1)
        acc = acc + dot_nt(d, w_ref[...])
    out_ref[...] = acc

    @pl.when(step == 3)
    def _():
        x = x_ref[...].astype(F32)
        r = lax.rsqrt(jnp.mean(x * x, axis=-1, keepdims=True) + EPSILON)
        dz = out_ref[...] * g_ref[...]
        inner = jnp.mean(dz * x, axis=-1, keepdims=True)
        out_ref[...] = dmid_ref[...] + r * dz - x * (r * r * r * inner)


def input_call(d_mine, wq, wk, wv, x, gain, dmid):
    whole = lambda shape: pl.BlockSpec(shape, lambda j: (0,) * len(shape))
    col = pl.BlockSpec((1024, 256), lambda j: (0, j))
    return pl.pallas_call(
        input_kernel,
        grid=(4,),
        in_specs=[pl.BlockSpec((2, 128, 384), lambda j: (j, 0, 0)), col, col, col, whole((128, 1024)), whole((1, 1024)), whole((128, 1024))],
        out_specs=whole((128, 1024)),
        out_shape=jax.ShapeDtypeStruct((128, 1024), F32),
        compiler_params=pltpu.CompilerParams(vmem_limit_bytes=16 * 2**20),
        cost_estimate=pl.CostEstimate(flops=2 * 128 * 1024 * 3072, bytes_accessed=7 * 2**20, transcendentals=0),
    )(d_mine, wq, wk, wv, x, gain, dmid)


def local(
    tokens, lengths, order, w_query, w_key, w_value, w_out, w_up, b_up, w_down, b_down,
    gain_attn_in, gain_attn_out, gain_mlp_in, gain_mlp_out, cotangent,
):
    z, xl, core, y, xh = (lax.axis_index(a) for a in ALL)
    my_blk = y * 2 + xh
    me = ((z * 2 + xl) * 2 + core) * 8 + my_blk
    info = jnp.stack([core, my_blk, z % 2, y % 2, xl]).astype(jnp.int32)
    row = lambda v: v.reshape(1, -1)
    order = order.T
    tie = lax.optimization_barrier

    across = lax.ppermute(tokens, ALL, ACROSS)
    qkv = qkv_call(info, order, lengths, tokens, row(gain_attn_in), w_query, w_key, w_value)
    qkv_heads = lax.all_to_all(qkv, BLK, 0, 0, tiled=True)

    late_lengths, _ = tie((lengths, qkv))
    lengths_row = late_lengths[0]
    group_pos = jnp.arange(1024, dtype=jnp.int32)
    start = jnp.zeros((1024,), jnp.int32)
    end = jnp.int32(0)
    for e in range(6):
        end = end + lengths_row[e]
        start = jnp.where(group_pos >= end, end, start)
    cos_all, sin_all = rotary_tables(group_pos - start)

    qkv_heads, cos_all, sin_all, pair = tie((qkv_heads, cos_all, sin_all, jnp.stack([tokens, across])))

    pairs = [pair] + [lax.ppermute(pair, ALL, to) for to in ALONG]
    out_heads, pos_qkv, lse = attend_call(order, lengths, qkv_heads)
    out_mine = lax.all_to_all(out_heads, BLK, 0, 0, tiled=True)
    out_mine, pairs[2] = tie((out_mine, pairs[2]))
    output, d_middle, d_out, send, keep, v_up, v_row = mlp_call(
        info, order, lengths, out_mine, tokens, cotangent, w_out, w_up, row(b_up), w_down, row(b_down),
        row(gain_attn_out), row(gain_mlp_in), row(gain_mlp_out),
    )
    send, keep, d_out, pairs = tie((send, keep, d_out, pairs))
    d_out_heads = lax.all_to_all(d_out, BLK, 0, 0, tiled=True)
    got = lax.ppermute(send, ALL, SWAP_CORES)
    sent = grads_call(1, info, send, keep, got)
    sent, d_out_heads = tie((sent, d_out_heads))
    one = [lax.ppermute(p, ALL, to) for p, to in zip(sent, STEPS[0])]
    d_heads = attend_back_call(order, lengths, pos_qkv, lse, cos_all, sin_all, d_out_heads)
    d_mine = lax.all_to_all(d_heads, BLK, 0, 0, tiled=True)
    keep, _ = tie((keep, d_heads))
    kept = grads_call(0, info, send, keep, got)
    added, d_mine = tie((add_call(kept, one), d_mine))
    two = [lax.ppermute(p, ALL, to) for p, to in zip(added, STEPS[1])]
    d_grads, v_up, v_row, _ = tie((d_heads, v_up, v_row, added))
    vectors = jnp.concatenate(
        [v_up.reshape(128, 32)] + [v_row[i].reshape(128, 8) for i in (1, 3, 2, 0)] + [jnp.zeros((128, 64), F32)], axis=1
    )
    packed = pack_call(kept, one, two, qkv_grads_call(info, pairs, row(gain_attn_in), d_grads, vectors))
    got_all = lax.all_to_all(packed, ALL, 0, 0, tiled=True)

    grad_tokens = input_call(d_mine, w_query, w_key, w_value, tokens, row(gain_attn_in), d_middle)
    my_rows = lambda w: lax.dynamic_slice_in_dim(w, me * 8, 8, 0).astype(F32)
    w_rows = jnp.stack([my_rows(w) for w in (w_query, w_key, w_value)])
    gain_rows = lax.dynamic_slice_in_dim(gain_attn_in, me * 8, 8, 0).reshape(8, 1)
    grad_w_up, grad_w_down, grad_w_out, grad_w_query, grad_w_key, grad_w_value, grad_gain_attn_in, vec = sum_call(
        got_all, w_rows, gain_rows
    )
    vec = vec[0]
    return (
        output, grad_tokens, grad_w_query, grad_w_key, grad_w_value, grad_w_out, grad_w_up, vec[0:32], grad_w_down,
        vec[32:40], grad_gain_attn_in.reshape(8), vec[40:48], vec[48:56], vec[56:64],
    )


def solution(mesh):
    split = Mesh(np.asarray(mesh.devices).reshape(4, 2, 2, 4, 2), ALL)
    every = P(ALL, None)
    flat = P(ALL)
    return jax.shard_map(
        local,
        mesh=split,
        in_specs=(every, P(("z", "xl", "core"), None)) + (P(),) * 13 + (every,),
        out_specs=(every,) * 7 + (flat, every) + (flat,) * 5,
        check_vma=False,
    )
```

```python
import functools
import math

import jax
import jax.numpy as jnp
import numpy as np
from jax import lax
from jax.experimental import pallas as pl
from jax.experimental.pallas import tpu as pltpu
from jax.sharding import Mesh
from jax.sharding import PartitionSpec as P

HEADS = 16
EPSILON = 1e-05
NEGATIVE = -1e30
ALL = ("z", "xl", "core", "y", "xh")
BLK = ("y", "xh")
BF = jnp.bfloat16
F32 = jnp.float32
TILES = ((0, 0, 256), (256, 0, 512), (512, 0, 768), (768, 512, 1024))


SMEM = pl.BlockSpec(memory_space=pltpu.SMEM)
VMEM = pl.BlockSpec(memory_space=pltpu.VMEM)
HBM = pl.BlockSpec(memory_space=pltpu.HBM)


def device_index(z, x, c, y):
    return (((z % 4) * 2 + (x % 4) % 2) * 2 + c) * 8 + (y % 4) * 2 + (x % 4) // 2


def pairs_of(f):
    return [
        (device_index(z, x, c, y), device_index(*f(z, x, c, y)))
        for z in range(4)
        for x in range(4)
        for c in range(2)
        for y in range(4)
    ]


def up(v):
    return v ^ 1


def down_pair(v):
    return ((v + 1) ^ 1) - 1


def flip(axis, by_core):
    way = (up, down_pair)

    def there(z, x, c, y):
        move = way[by_core[c]]
        return (
            move(z) if axis == "z" else z,
            move(x) if axis == "x" else x,
            c,
            move(y) if axis == "y" else y,
        )

    return pairs_of(there)


ACROSS = pairs_of(lambda z, x, c, y: (z, x + 2, c, y))
ALONG = [pairs_of(lambda z, x, c, y, by=by: (z, x, c, y + by)) for by in (1, 2, 3)]
SWAP_CORES = pairs_of(lambda z, x, c, y: (z, x, 1 - c, y))
PARTS = (32, 24, 16)
STEPS = (
    (flip("z", (0, 1)), flip("y", (0, 1)), flip("x", (0, 1))),
    (flip("y", (0, 1)), flip("x", (0, 1)), flip("z", (0, 1))),
)


def half_swap(x):
    n = x.shape[1]
    lane = lax.broadcasted_iota(jnp.int32, x.shape, 1) % 64
    return jnp.where(lane < 32, pltpu.roll(x, n - 32, 1), pltpu.roll(x, 32, 1))


def rotary_tables(relative):
    freqs = jnp.exp(jnp.arange(32, dtype=F32) * (-math.log(10000.0) / 32))
    angles = relative.astype(F32)[:, None] * freqs[None, :]
    c, s = jnp.cos(angles), jnp.sin(angles)
    return jnp.concatenate([c, c, c, c], axis=1), jnp.concatenate([-s, s, -s, s], axis=1)


def dot(a, b):
    return jnp.dot(a, b, preferred_element_type=F32)


def dot_nt(a, b):
    return lax.dot_general(a, b, (((1,), (1,)), ((), ())), preferred_element_type=F32)


def dot_tn(a, b):
    return lax.dot_general(a, b, (((0,), (0,)), ((), ())), preferred_element_type=F32)


def column_positions(info_ref, order_ref, len_ref):
    row = lax.broadcasted_iota(jnp.int32, (128, 1), 0)
    one, two = order_ref[0, info_ref[1]], order_ref[1, info_ref[1]]
    pos = jnp.where(row < 64, one * 64 + row, two * 64 + row - 64)
    start = jnp.zeros((128, 1), jnp.int32)
    end = jnp.int32(0)
    for e in range(6):
        end = end + len_ref[0, e]
        start = jnp.where(pos >= end, end, start)
    return pos, start, end


def qkv_kernel(info_ref, order_ref, len_ref, x_ref, g_ref, wq_hbm, wk_hbm, wv_hbm, out_ref, a_ref, wq, wk, wv, sems):
    copies = [
        pltpu.make_async_copy(hbm.at[:, 512 * h : 512 * (h + 1)], w.at[:, 512 * h : 512 * (h + 1)], sems.at[2 * i + h])
        for i, (hbm, w) in enumerate(((wq_hbm, wq), (wk_hbm, wk), (wv_hbm, wv)))
        for h in range(2)
    ]
    for copy in copies:
        copy.start()
    x = x_ref[...].astype(F32)
    factor = lax.rsqrt(jnp.mean(x * x, axis=-1, keepdims=True) + EPSILON)
    a = (x * factor * g_ref[...]).astype(BF)
    a_ref[...] = a
    pos, start, _ = column_positions(info_ref, order_ref, len_ref)
    lane = lax.broadcasted_iota(jnp.int32, (1, 128), 1)
    freqs = jnp.exp((lane % 32).astype(F32) * (-math.log(10000.0) / 32))
    angles = (pos - start).astype(F32) * freqs
    cos = jnp.cos(angles)
    sine = jnp.sin(angles)
    sin = jnp.where(lane % 64 < 32, -sine, sine)
    cos = jnp.concatenate([cos] * 4, axis=1)
    sin = jnp.concatenate([sin] * 4, axis=1)
    for i, w in enumerate((wq, wk, wv)):
        for h in range(2):
            copies[2 * i + h].wait()
            y = dot(a, w[:, 512 * h : 512 * (h + 1)])
            if i < 2:
                y = y * cos + half_swap(y) * sin
            y = y.astype(BF)
            for j in range(4):
                out_ref[4 * h + j, :, 128 * i : 128 * (i + 1)] = y[:, 128 * j : 128 * (j + 1)]


def qkv_call(info, order, lengths, x, gain, wq, wk, wv):
    return pl.pallas_call(
        qkv_kernel,
        in_specs=[SMEM, SMEM, SMEM, VMEM, VMEM, HBM, HBM, HBM],
        out_specs=[VMEM, VMEM],
        out_shape=[jax.ShapeDtypeStruct((8, 128, 384), BF), jax.ShapeDtypeStruct((128, 1024), BF)],
        scratch_shapes=[pltpu.VMEM((1024, 1024), BF)] * 3 + [pltpu.SemaphoreType.DMA((6,))],
        compiler_params=pltpu.CompilerParams(vmem_limit_bytes=60 * 2**20),
        cost_estimate=pl.CostEstimate(flops=2 * 128 * 1024 * 3072, bytes_accessed=7 * 2**20, transcendentals=0),
    )(info, order, lengths, x, gain, wq, wk, wv)


def allowed_mask(len_ref, q0, k0, k1):
    qpos = q0 + lax.broadcasted_iota(jnp.int32, (1, 256), 1)
    start = jnp.zeros((1, 256), jnp.int32)
    end = jnp.int32(0)
    for e in range(6):
        end = end + len_ref[0, e]
        start = jnp.where(qpos >= end, end, start)
    kpos = k0 + lax.broadcasted_iota(jnp.int32, (k1 - k0, 256), 0)
    return (kpos >= start) & (kpos <= qpos)


def attend_kernel(order_ref, len_ref, qkv_ref, out_ref, pos_ref, lse_ref, o_ref):
    for b in range(8):
        for j in range(2):
            at = pl.ds(pl.multiple_of(order_ref[j, b] * 64, 64), 64)
            pos_ref[at, :] = qkv_ref[b, 64 * j : 64 * (j + 1), :]
    first = lax.broadcasted_iota(jnp.int32, (1, 128), 1) < 64
    v_t = pos_ref[:, 256:384].T
    for q0, k0, k1 in TILES:
        q = pos_ref[q0 : q0 + 256, 0:128].astype(F32) * 0.125
        k = pos_ref[k0:k1, 128:256]
        mask = allowed_mask(len_ref, q0, k0, k1)
        outs = []
        for h in range(2):
            q_h = jnp.where(first if h == 0 else ~first, q, 0.0).astype(BF)
            s = jnp.where(mask, dot_nt(k, q_h), NEGATIVE)
            top = jnp.max(s, axis=0, keepdims=True)
            p = jnp.exp(s - top)
            total = jnp.sum(p, axis=0, keepdims=True)
            lse_ref[h : h + 1, q0 : q0 + 256] = top + jnp.log(total)
            p = (p * (1.0 / total)).astype(BF)
            outs.append(dot(v_t[64 * h : 64 * (h + 1), k0:k1], p))
        o_ref[q0 : q0 + 256, :] = jnp.concatenate(outs, axis=0).T.astype(BF)
    for b in range(8):
        for j in range(2):
            at = pl.ds(pl.multiple_of(order_ref[j, b] * 64, 64), 64)
            out_ref[b, 64 * j : 64 * (j + 1), :] = o_ref[at, :]


def attend_call(order, lengths, qkv):
    return pl.pallas_call(
        attend_kernel,
        in_specs=[SMEM, SMEM, VMEM],
        out_specs=[VMEM] * 3,
        out_shape=[
            jax.ShapeDtypeStruct((8, 128, 128), BF),
            jax.ShapeDtypeStruct((1024, 384), BF),
            jax.ShapeDtypeStruct((2, 1024), F32),
        ],
        scratch_shapes=[pltpu.VMEM((1024, 128), BF)],
        compiler_params=pltpu.CompilerParams(vmem_limit_bytes=24 * 2**20),
        cost_estimate=pl.CostEstimate(flops=2 * 10**9, bytes_accessed=3 * 2**20, transcendentals=2 * 10**6),
    )(order, lengths, qkv)


def attend_back_kernel(order_ref, len_ref, pos_ref, lse_ref, cos_ref, sin_ref, do_ref, out_ref, d_ref, dk_ref, dv_ref, dq_ref):
    for b in range(8):
        for j in range(2):
            at = pl.ds(pl.multiple_of(order_ref[j, b] * 64, 64), 64)
            d_ref[at, 0:128] = do_ref[b, 64 * j : 64 * (j + 1), :]
    first = lax.broadcasted_iota(jnp.int32, (1, 128), 1) < 64
    k_t = pos_ref[:, 128:256].T
    dk_ref[...] = jnp.zeros_like(dk_ref)
    dv_ref[...] = jnp.zeros_like(dv_ref)
    for q0, k0, k1 in TILES:
        q = pos_ref[q0 : q0 + 256, 0:128].astype(F32) * 0.125
        do = d_ref[q0 : q0 + 256, 0:128]
        k = pos_ref[k0:k1, 128:256]
        v = pos_ref[k0:k1, 256:384]
        mask = allowed_mask(len_ref, q0, k0, k1)
        outs = []
        for h in range(2):
            pick = first if h == 0 else ~first
            q_h = jnp.where(pick, q, 0.0).astype(BF)
            do_h = jnp.where(pick, do.astype(F32), 0.0).astype(BF)
            s = jnp.where(mask, dot_nt(k, q_h), NEGATIVE)
            p = jnp.exp(s - lse_ref[h : h + 1, q0 : q0 + 256])
            dp = dot_nt(v, do_h)
            delta = jnp.sum(p * dp, axis=0, keepdims=True)
            ds = (p * (dp - delta)).astype(BF)
            dv_ref[k0:k1, :] += dot(p.astype(BF), do_h)
            dk_ref[k0:k1, :] += dot(ds, q_h)
            outs.append(dot(k_t[64 * h : 64 * (h + 1), k0:k1], ds))
        dq_ref[q0 : q0 + 256, :] = jnp.concatenate(outs, axis=0).T * 0.125
    cos, sin = cos_ref[...], sin_ref[...]
    dq, dk = dq_ref[...], dk_ref[...]
    d_ref[:, 0:128] = (dq * cos - half_swap(dq) * sin).astype(BF)
    d_ref[:, 128:256] = (dk * cos - half_swap(dk) * sin).astype(BF)
    d_ref[:, 256:384] = dv_ref[...].astype(BF)
    for b in range(8):
        for j in range(2):
            at = pl.ds(pl.multiple_of(order_ref[j, b] * 64, 64), 64)
            out_ref[b, 64 * j : 64 * (j + 1), :] = d_ref[at, :]


def attend_back_call(order, lengths, pos, lse, cos, sin, d_out):
    return pl.pallas_call(
        attend_back_kernel,
        in_specs=[SMEM, SMEM, VMEM, VMEM, VMEM, VMEM, VMEM],
        out_specs=VMEM,
        out_shape=jax.ShapeDtypeStruct((8, 128, 384), BF),
        scratch_shapes=[
            pltpu.VMEM((1024, 384), BF),
            pltpu.VMEM((1024, 128), F32),
            pltpu.VMEM((1024, 128), F32),
            pltpu.VMEM((1024, 128), F32),
        ],
        compiler_params=pltpu.CompilerParams(vmem_limit_bytes=32 * 2**20),
        cost_estimate=pl.CostEstimate(flops=1, bytes_accessed=1024, transcendentals=0),
    )(order, lengths, pos, lse, cos, sin, d_out)


ACT, M_AT, O_AT, DPRE, DD, DPROJ, SEND = 0, 4096, 5120, 6144, 8192, 8704, 9216
CHUNK = 1024


def mlp_kernel(info_ref, order_ref, len_ref, o_ref, x_ref, ct_ref, wo_hbm, wup_hbm, bup_ref, wdown_hbm, bdown_ref,
               g2_ref, g3_ref, g4_ref,
               out_ref, dmid_ref, do_ref, send_ref, keep_ref, vup_ref, vrow_ref,
               proj_ref, middle_ref, slope_ref, dd_ref, acc_ref, wo_ref, wup_ref, wdown_ref, sems):
    core = info_ref[0]
    count = 4096 // CHUNK
    copy_out = pltpu.make_async_copy(wo_hbm, wo_ref, sems.at[2 * count])
    copy_out.start()
    copies = []
    for i in range(count):
        at = slice(CHUNK * i, CHUNK * (i + 1))
        copies.append((
            pltpu.make_async_copy(wup_hbm.at[:, at], wup_ref.at[:, at], sems.at[2 * i]),
            pltpu.make_async_copy(wdown_hbm.at[at, :], wdown_ref.at[at, :], sems.at[2 * i + 1]),
        ))
        copies[-1][0].start()
        copies[-1][1].start()
    pos, _, end = column_positions(info_ref, order_ref, len_ref)
    valid = pos < end
    o = jnp.concatenate([o_ref[j] for j in range(8)], axis=1)
    send_ref[:, O_AT : O_AT + 1024] = o
    copy_out.wait()
    proj = dot(o, wo_ref[...])
    proj_ref[...] = proj
    r2 = lax.rsqrt(jnp.mean(proj * proj, axis=-1, keepdims=True) + EPSILON)
    middle = x_ref[...].astype(F32) + proj * r2 * g2_ref[...]
    middle_ref[...] = middle
    r3 = lax.rsqrt(jnp.mean(middle * middle, axis=-1, keepdims=True) + EPSILON)
    m = (middle * r3 * g3_ref[...]).astype(BF)
    send_ref[:, M_AT : M_AT + 1024] = m
    acc_ref[...] = jnp.zeros_like(acc_ref)
    root = math.sqrt(2.0 / math.pi)
    for i in range(4096 // CHUNK):
        at = slice(CHUNK * i, CHUNK * (i + 1))
        copies[i][0].wait()
        pre = dot(m, wup_ref[:, at]) + bup_ref[:, at]
        square = pre * pre
        t = jnp.tanh(root * (pre + 0.044715 * (square * pre)))
        half = 0.5 * (1.0 + t)
        act = (pre * half).astype(BF)
        slope_ref[:, at] = half + 0.5 * pre * (1.0 - t * t) * (root + (3.0 * 0.044715 * root) * square)
        send_ref[:, at] = act
        copies[i][1].wait()
        acc_ref[...] += dot(act, wdown_ref[at, :])
    down = acc_ref[...] + bdown_ref[...]
    r4 = lax.rsqrt(jnp.mean(down * down, axis=-1, keepdims=True) + EPSILON)
    out_ref[...] = jnp.where(valid, middle_ref[...] + down * r4 * g4_ref[...], 0.0).astype(BF)
    dy = jnp.where(valid, ct_ref[...].astype(F32), 0.0)
    dz = dy * down
    vrow_ref[0:1, :] = jnp.sum(dz * r4, axis=0, keepdims=True)
    inner = jnp.mean(dz * g4_ref[...], axis=-1, keepdims=True)
    dd = (r4 * g4_ref[...] * dy - down * (r4 * r4 * r4 * inner)).astype(BF)
    dd_ref[...] = dd
    vrow_ref[1:2, :] = jnp.sum(dd.astype(F32), axis=0, keepdims=True)
    send_ref[:, DD : DD + 512] = dd_ref[:, pl.ds(pl.multiple_of((1 - core) * 512, 512), 512)]
    keep_ref[:, 2048:2560] = dd_ref[:, pl.ds(pl.multiple_of(core * 512, 512), 512)]
    acc_ref[...] = jnp.zeros_like(acc_ref)
    for part in range(2):
        which = 1 - core if part == 0 else core
        for i in range(2048 // CHUNK):
            at = pl.ds(pl.multiple_of(which * 2048 + CHUNK * i, CHUNK), CHUNK)
            dact = dot_nt(dd, wdown_ref[at, :])
            dpre = (dact * slope_ref[:, at]).astype(BF)
            vup_ref[:, at] = jnp.sum(dpre.astype(F32), axis=0, keepdims=True)
            if part == 0:
                send_ref[:, DPRE + CHUNK * i : DPRE + CHUNK * (i + 1)] = dpre
            else:
                keep_ref[:, CHUNK * i : CHUNK * (i + 1)] = dpre
            acc_ref[...] += dot_nt(dpre, wup_ref[:, at])
    dm = acc_ref[...]
    middle = middle_ref[...]
    dz = dm * middle
    vrow_ref[2:3, :] = jnp.sum(dz * r3, axis=0, keepdims=True)
    inner = jnp.mean(dz * g3_ref[...], axis=-1, keepdims=True)
    dmid = dy + r3 * g3_ref[...] * dm - middle * (r3 * r3 * r3 * inner)
    dmid_ref[...] = dmid
    proj = proj_ref[...]
    dz = dmid * proj
    vrow_ref[3:4, :] = jnp.sum(dz * r2, axis=0, keepdims=True)
    inner = jnp.mean(dz * g2_ref[...], axis=-1, keepdims=True)
    dproj = (r2 * g2_ref[...] * dmid - proj * (r2 * r2 * r2 * inner)).astype(BF)
    dd_ref[...] = dproj
    send_ref[:, DPROJ : DPROJ + 512] = dd_ref[:, pl.ds(pl.multiple_of((1 - core) * 512, 512), 512)]
    keep_ref[:, 2560:3072] = dd_ref[:, pl.ds(pl.multiple_of(core * 512, 512), 512)]
    d_out = dot_nt(dproj, wo_ref[...]).astype(BF)
    for j in range(8):
        do_ref[j] = d_out[:, 128 * j : 128 * (j + 1)]


def mlp_call(*args):
    shape = jax.ShapeDtypeStruct
    return pl.pallas_call(
        mlp_kernel,
        in_specs=[SMEM] * 3 + [VMEM] * 3 + [HBM, HBM, VMEM, HBM] + [VMEM] * 4,
        out_specs=[VMEM] * 7,
        out_shape=[
            shape((128, 1024), BF), shape((128, 1024), F32), shape((8, 128, 128), BF), shape((128, SEND), BF),
            shape((128, 3072), BF), shape((1, 4096), F32), shape((4, 1024), F32),
        ],
        scratch_shapes=[
            pltpu.VMEM((128, 1024), F32), pltpu.VMEM((128, 1024), F32), pltpu.VMEM((128, 4096), F32),
            pltpu.VMEM((128, 1024), BF), pltpu.VMEM((128, 1024), F32),
            pltpu.VMEM((1024, 1024), BF), pltpu.VMEM((1024, 4096), BF), pltpu.VMEM((4096, 1024), BF),
            pltpu.SemaphoreType.DMA((2 * 4096 // CHUNK + 1,)),
        ],
        compiler_params=pltpu.CompilerParams(vmem_limit_bytes=60 * 2**20),
        cost_estimate=pl.CostEstimate(flops=4 * 128 * 9 * 2**20, bytes_accessed=20 * 2**20, transcendentals=2**19),
    )(*args)


def grad_parts(info_ref, relative, lefts, rights, outs, copies):
    bz, by, bx = info_ref[2], info_ref[3], info_ref[4]

    def left(at, n):
        return lefts[at : at + n, :]

    def cols(at, n):
        return rights[:, pl.ds(pl.multiple_of(at, 128), n)]

    eights = lambda g: [g[:, 128 * i : 128 * (i + 1)].reshape(128, 8, 128) for i in range(g.shape[1] // 128)]
    for k2 in range(2):
        block = 2 * (relative ^ bz) + k2
        rhs = jnp.concatenate([cols(u * 512 + block * 128, 128) for u in range(4)], axis=1)
        rows = eights(dot(left(M_AT, 1024), rhs))
        outs[0][k2 ^ by] = jnp.concatenate(rows, axis=1).reshape(4096, 128).astype(BF)
    copies[0].start()
    rhs = cols(2048 + 256 * (relative ^ by), 256)
    for half in range(2):
        g = dot(left(2048 * half, 2048), rhs)
        for k2 in range(2):
            part = g[:, 128 * k2 : 128 * (k2 + 1)].reshape(64, 32, 128)[:, 0:24]
            outs[1][k2 ^ bx, 1536 * half : 1536 * (half + 1), :] = part.reshape(1536, 128).astype(BF)
    copies[1].start()
    first = 256 * (relative ^ bx)
    g_out = eights(dot(left(O_AT, 1024), cols(2560 + first, 256)))
    for half in range(2):
        g_down = dot(left(2048 * half, 2048), cols(2048 + first, 256))
        d = slice(64 * half, 64 * (half + 1))
        for k2 in range(2):
            tail = g_down[:, 128 * k2 : 128 * (k2 + 1)].reshape(64, 32, 128)[:, 24:32]
            rows = jnp.concatenate([tail, g_out[k2][d]], axis=1)
            outs[2][k2 ^ bz, 1024 * half : 1024 * (half + 1), :] = rows.reshape(1024, 128).astype(BF)
    copies[2].start()


def turn(mine, theirs, lefts):
    for i in range(6144 // 512):
        at = slice(512 * i, 512 * (i + 1))
        lefts[at, 0:128] = mine[:, at].T
        lefts[at, 128:256] = theirs[:, at].T


def grads_kernel(relative, info_ref, mine_ref, keep_ref, theirs_ref, p_hbm, q_hbm, r_hbm, lefts, rights, p_ref, q_ref, r_ref, sems):
    turn(mine_ref, theirs_ref, lefts)
    rights[0:128, :] = keep_ref[...]
    rights[128:256, :] = theirs_ref[:, DPRE:SEND]
    copies = [
        pltpu.make_async_copy(ref, hbm, sems.at[i])
        for i, (ref, hbm) in enumerate(((p_ref, p_hbm), (q_ref, q_hbm), (r_ref, r_hbm)))
    ]
    grad_parts(info_ref, relative, lefts, rights, (p_ref, q_ref, r_ref), copies)
    for copy in copies:
        copy.wait()


PART_SHAPES = [jax.ShapeDtypeStruct((2, 128 * n, 128), BF) for n in PARTS]


def grads_call(relative, info, send, keep, got):
    return pl.pallas_call(
        functools.partial(grads_kernel, relative),
        in_specs=[SMEM, VMEM, VMEM, VMEM],
        out_specs=[HBM] * 3,
        out_shape=PART_SHAPES,
        scratch_shapes=[pltpu.VMEM((6144, 256), BF), pltpu.VMEM((256, 3072), BF)]
        + [pltpu.VMEM((2, 128 * n, 128), BF) for n in PARTS]
        + [pltpu.SemaphoreType.DMA((3,))],
        compiler_params=pltpu.CompilerParams(vmem_limit_bytes=60 * 2**20),
        cost_estimate=pl.CostEstimate(flops=1, bytes_accessed=1024, transcendentals=0),
    )(info, send, keep, got)


ROWS = 88


def add_kernel(*refs):
    for k, a, out in zip(refs[0:3], refs[3:6], refs[6:9]):
        out[...] = k[0] + a[0]


def add_call(kept, one):
    return pl.pallas_call(
        add_kernel,
        grid=(2,),
        in_specs=[pl.BlockSpec((1, 64 * n, 128), lambda j: (1, j, 0)) for n in PARTS] * 2,
        out_specs=[pl.BlockSpec((64 * n, 128), lambda j: (j, 0)) for n in PARTS],
        out_shape=[jax.ShapeDtypeStruct((128 * n, 128), BF) for n in PARTS],
        compiler_params=pltpu.CompilerParams(vmem_limit_bytes=60 * 2**20),
        cost_estimate=pl.CostEstimate(flops=1, bytes_accessed=1024, transcendentals=0),
    )(*kept, *one)


def pack_kernel(*refs):
    rows = []
    for k, a, b, n in zip(refs[0:3], refs[3:6], refs[6:9], PARTS):
        total = k[0].astype(F32) + a[0].astype(F32) + b[...].astype(F32)
        rows.append(total.reshape(64, n, 128))
    rows.append(refs[9][...].astype(F32) + refs[10][...].astype(F32))
    refs[11][...] = jnp.concatenate(rows, axis=1).astype(BF)


def pack_call(kept, one, two, qkv, qkv_two):
    half = [pl.BlockSpec((1, 64 * n, 128), lambda j: (0, j, 0)) for n in PARTS]
    tail = pl.BlockSpec((64, 16, 128), lambda j: (j, 0, 0))
    return pl.pallas_call(
        pack_kernel,
        grid=(2,),
        in_specs=half * 2 + [pl.BlockSpec((64 * n, 128), lambda j: (j, 0)) for n in PARTS] + [tail] * 2,
        out_specs=pl.BlockSpec((64, ROWS, 128), lambda j: (j, 0, 0)),
        out_shape=jax.ShapeDtypeStruct((128, ROWS, 128), BF),
        compiler_params=pltpu.CompilerParams(vmem_limit_bytes=60 * 2**20),
        cost_estimate=pl.CostEstimate(flops=1, bytes_accessed=1024, transcendentals=0),
    )(*kept, *one, *two, qkv, qkv_two)


def bits_of(s):
    return {n: (s >> i) & 1 for i, n in enumerate(("xh", "yl", "yh", "core", "xl", "zl", "zh"))}


def sum_kernel(got_ref, w_ref, g_ref, up_ref, down_ref, wo_ref, q_ref, k_ref, v_ref, gain_ref, *vec_refs):
    def total(keys, at, n):
        sums = {}
        for s in range(128):
            b = bits_of(s)
            k = tuple(b[name] for name in keys)
            v = got_ref[s].astype(F32)[at : at + n]
            sums[k] = sums[k] + v if k in sums else v
        return sums

    for (core, k1, k2), v in total(("core", "zl", "yl"), 0, 32).items():
        for u in range(4):
            at = core * 2048 + u * 512 + (2 * k1 + k2) * 128
            up_ref[:, at : at + 128] = v[8 * u : 8 * (u + 1)]
    for (core, k1, k2), v in total(("core", "yl", "xl"), 32, 24).items():
        at = core * 512 + (2 * k1 + k2) * 128
        down_ref[0:24, at : at + 128] = v
    for (core, k1, k2), v in total(("core", "xl", "zl"), 56, 16).items():
        at = core * 512 + (2 * k1 + k2) * 128
        down_ref[24:32, at : at + 128] = v[0:8]
        wo_ref[:, at : at + 128] = v[8:16]
    weighted = jnp.zeros((8, 128), F32)
    vec = jnp.zeros((8, 128), F32)
    for (core, yh, yl, xh), v in total(("core", "yh", "yl", "xh"), 72, 16).items():
        b = 4 * yh + 2 * yl + xh
        at = slice(128 * b, 128 * (b + 1))
        for i, out in ((2, v_ref),) if core else ((0, q_ref), (1, k_ref)):
            part = v[8 * (i % 2) : 8 * (i % 2) + 8]
            out[:, at] = part
            weighted = weighted + part * w_ref[i, :, at]
        if core:
            vec = vec + v[8:16]
    gain_ref[...] = jnp.sum(weighted.T, axis=0, keepdims=True) / g_ref[...]
    at = 0
    for ref in vec_refs:
        n = ref.shape[1]
        ref[...] = vec[0:1, at : at + n]
        at += n


def sum_call(got, w_rows, gain_rows):
    shape = jax.ShapeDtypeStruct
    return pl.pallas_call(
        sum_kernel,
        in_specs=[VMEM] * 3,
        out_specs=[VMEM] * 12,
        out_shape=[shape((8, 4096), F32), shape((32, 1024), F32)]
        + [shape((8, 1024), F32)] * 4
        + [shape((1, n), F32) for n in (8, 32, 8, 8, 8, 8)],
        compiler_params=pltpu.CompilerParams(vmem_limit_bytes=16 * 2**20),
        cost_estimate=pl.CostEstimate(flops=10**7, bytes_accessed=3 * 2**20, transcendentals=0),
    )(got, w_rows, gain_rows)


def qkv_grads_kernel(info_ref, a0_ref, a1_ref, a2_ref, a3_ref, d_ref, vec_ref, keep_ref, send_ref):
    y, xh = info_ref[1] // 2, info_ref[1] % 2
    g = jnp.zeros((512, 384), F32)
    for back, ref in enumerate((a0_ref, a1_ref, a2_ref, a3_ref)):
        source = ((y + 4 - back) % 4) * 2
        d = jnp.concatenate([d_ref[source + xh], d_ref[source + 1 - xh]], axis=0)
        g = g + dot_tn(ref[...].reshape(256, 512), d)
    parts = [g[:, 128 * i : 128 * (i + 1)].reshape(64, 8, 128) for i in range(3)]
    first = lax.broadcasted_iota(jnp.int32, (64, 8, 128), 1) == 0
    parts.append(jnp.where(first, vec_ref[...].reshape(64, 1, 128), 0.0))
    one, two = (jnp.concatenate(parts[i : i + 2], axis=1) for i in (0, 2))
    mine = info_ref[0] == 0
    keep_ref[...] = jnp.where(mine, one, two).astype(BF)
    send_ref[...] = jnp.where(mine, two, one).astype(BF)


def qkv_grads_call(info, pairs, d_heads, vec):
    return pl.pallas_call(
        qkv_grads_kernel,
        grid=(2,),
        in_specs=[SMEM]
        + [pl.BlockSpec((2, 128, 512), lambda j: (0, 0, j))] * 4
        + [pl.BlockSpec((8, 128, 384), lambda j: (0, 0, 0)), pl.BlockSpec((64, 128), lambda j: (j, 0))],
        out_specs=[pl.BlockSpec((64, 16, 128), lambda j: (j, 0, 0))] * 2,
        out_shape=[jax.ShapeDtypeStruct((128, 16, 128), BF)] * 2,
        compiler_params=pltpu.CompilerParams(vmem_limit_bytes=60 * 2**20),
        cost_estimate=pl.CostEstimate(flops=1, bytes_accessed=1024, transcendentals=0),
    )(info, *pairs, d_heads, vec)


def input_kernel(d_ref, wq_ref, wk_ref, wv_ref, x_ref, g_ref, dmid_ref, out_ref):
    step = pl.program_id(0)
    acc = jnp.where(step == 0, 0.0, out_ref[...])
    for i, w_ref in enumerate((wq_ref, wk_ref, wv_ref)):
        d = jnp.concatenate([d_ref[j, :, 128 * i : 128 * (i + 1)] for j in range(2)], axis=1)
        acc = acc + dot_nt(d, w_ref[...])
    out_ref[...] = acc

    @pl.when(step == 3)
    def _():
        x = x_ref[...].astype(F32)
        r = lax.rsqrt(jnp.mean(x * x, axis=-1, keepdims=True) + EPSILON)
        dz = out_ref[...] * g_ref[...]
        inner = jnp.mean(dz * x, axis=-1, keepdims=True)
        out_ref[...] = dmid_ref[...] + r * dz - x * (r * r * r * inner)


def input_call(d_mine, wq, wk, wv, x, gain, dmid):
    whole = lambda shape: pl.BlockSpec(shape, lambda j: (0,) * len(shape))
    col = pl.BlockSpec((1024, 256), lambda j: (0, j))
    return pl.pallas_call(
        input_kernel,
        grid=(4,),
        in_specs=[pl.BlockSpec((2, 128, 384), lambda j: (j, 0, 0)), col, col, col, whole((128, 1024)), whole((1, 1024)), whole((128, 1024))],
        out_specs=whole((128, 1024)),
        out_shape=jax.ShapeDtypeStruct((128, 1024), F32),
        compiler_params=pltpu.CompilerParams(vmem_limit_bytes=16 * 2**20),
        cost_estimate=pl.CostEstimate(flops=2 * 128 * 1024 * 3072, bytes_accessed=7 * 2**20, transcendentals=0),
    )(d_mine, wq, wk, wv, x, gain, dmid)


def local(
    tokens, lengths, order, w_query, w_key, w_value, w_out, w_up, b_up, w_down, b_down,
    gain_attn_in, gain_attn_out, gain_mlp_in, gain_mlp_out, cotangent,
):
    z, xl, core, y, xh = (lax.axis_index(a) for a in ALL)
    my_blk = y * 2 + xh
    me = ((z * 2 + xl) * 2 + core) * 8 + my_blk
    info = jnp.stack([core, my_blk, z % 2, y % 2, xl]).astype(jnp.int32)
    row = lambda v: v.reshape(1, -1)
    order = order.T
    tie = lax.optimization_barrier

    qkv, attn_low = qkv_call(info, order, lengths, tokens, row(gain_attn_in), w_query, w_key, w_value)
    across = lax.ppermute(attn_low, ALL, ACROSS)
    qkv_heads = lax.all_to_all(qkv, BLK, 0, 0, tiled=True)

    late_lengths, _ = tie((lengths, qkv))
    lengths_row = late_lengths[0]
    group_pos = jnp.arange(1024, dtype=jnp.int32)
    start = jnp.zeros((1024,), jnp.int32)
    end = jnp.int32(0)
    for e in range(6):
        end = end + lengths_row[e]
        start = jnp.where(group_pos >= end, end, start)
    cos_all, sin_all = rotary_tables(group_pos - start)

    qkv_heads, cos_all, sin_all, pair = tie((qkv_heads, cos_all, sin_all, jnp.stack([attn_low, across])))

    pairs = [pair] + [lax.ppermute(pair, ALL, to) for to in ALONG]
    out_heads, pos_qkv, lse = attend_call(order, lengths, qkv_heads)
    out_mine = lax.all_to_all(out_heads, BLK, 0, 0, tiled=True)
    out_mine, pairs[2] = tie((out_mine, pairs[2]))
    output, d_middle, d_out, send, keep, v_up, v_row = mlp_call(
        info, order, lengths, out_mine, tokens, cotangent, w_out, w_up, row(b_up), w_down, row(b_down),
        row(gain_attn_out), row(gain_mlp_in), row(gain_mlp_out),
    )
    send, keep, d_out, pairs = tie((send, keep, d_out, pairs))
    d_out_heads = lax.all_to_all(d_out, BLK, 0, 0, tiled=True)
    got = lax.ppermute(send, ALL, SWAP_CORES)
    sent = grads_call(1, info, send, keep, got)
    sent, d_out_heads = tie((sent, d_out_heads))
    one = [lax.ppermute(p, ALL, to) for p, to in zip(sent, STEPS[0])]
    d_heads = attend_back_call(order, lengths, pos_qkv, lse, cos_all, sin_all, d_out_heads)
    d_mine = lax.all_to_all(d_heads, BLK, 0, 0, tiled=True)
    keep, _ = tie((keep, d_heads))
    kept = grads_call(0, info, send, keep, got)
    v_up, v_row, _ = tie((v_up, v_row, d_heads))
    vectors = jnp.concatenate(
        [v_up.reshape(128, 32)] + [v_row[i].reshape(128, 8) for i in (1, 3, 2, 0)] + [jnp.zeros((128, 64), F32)], axis=1
    )
    one, vectors = tie((one, vectors))
    added = add_call(kept, one)
    two = [lax.ppermute(p, ALL, to) for p, to in zip(added, STEPS[1])]
    d_grads, d_mine, _ = tie((d_heads, d_mine, added))
    qkv_keep, qkv_send = qkv_grads_call(info, pairs, d_grads, vectors)
    qkv_send, two[2] = tie((qkv_send, two[2]))
    packed = pack_call(kept, one, two, qkv_keep, lax.ppermute(qkv_send, ALL, SWAP_CORES))
    got_all = lax.all_to_all(packed, ALL, 0, 0, tiled=True)

    grad_tokens = input_call(d_mine, w_query, w_key, w_value, tokens, row(gain_attn_in), d_middle)
    my_rows = lambda w: lax.dynamic_slice_in_dim(w, me * 8, 8, 0).astype(F32)
    w_rows = jnp.stack([my_rows(w) for w in (w_query, w_key, w_value)])
    gain_rows = lax.dynamic_slice_in_dim(gain_attn_in, me * 8, 8, 0).reshape(1, 8)
    grad_w_up, grad_w_down, grad_w_out, grad_w_query, grad_w_key, grad_w_value, *vec = sum_call(got_all, w_rows, gain_rows)
    grad_gain_attn_in, grad_b_up, grad_b_down, grad_gain_attn_out, grad_gain_mlp_in, grad_gain_mlp_out = (
        v.reshape(-1) for v in vec
    )
    return (
        output, grad_tokens, grad_w_query, grad_w_key, grad_w_value, grad_w_out, grad_w_up, grad_b_up, grad_w_down,
        grad_b_down, grad_gain_attn_in, grad_gain_attn_out, grad_gain_mlp_in, grad_gain_mlp_out,
    )


def solution(mesh):
    split = Mesh(np.asarray(mesh.devices).reshape(4, 2, 2, 4, 2), ALL)
    every = P(ALL, None)
    flat = P(ALL)
    return jax.shard_map(
        local,
        mesh=split,
        in_specs=(every, P(("z", "xl", "core"), None)) + (P(),) * 13 + (every,),
        out_specs=(every,) * 7 + (flat, every) + (flat,) * 5,
        check_vma=False,
    )
```

```python
import functools
import math

import jax
import jax.numpy as jnp
import numpy as np
from jax import lax
from jax.experimental import pallas as pl
from jax.experimental.pallas import tpu as pltpu
from jax.sharding import Mesh
from jax.sharding import PartitionSpec as P

HEADS = 16
EPSILON = 1e-05
NEGATIVE = -1e30
ALL = ("z", "xl", "core", "y", "xh")
BLK = ("y", "xh")
BF = jnp.bfloat16
F32 = jnp.float32
TILES = ((0, 0, 256), (256, 0, 512), (512, 0, 768), (768, 512, 1024))


SMEM = pl.BlockSpec(memory_space=pltpu.SMEM)
VMEM = pl.BlockSpec(memory_space=pltpu.VMEM)
HBM = pl.BlockSpec(memory_space=pltpu.HBM)


def device_index(z, x, c, y):
    return (((z % 4) * 2 + (x % 4) % 2) * 2 + c) * 8 + (y % 4) * 2 + (x % 4) // 2


def pairs_of(f):
    return [
        (device_index(z, x, c, y), device_index(*f(z, x, c, y)))
        for z in range(4)
        for x in range(4)
        for c in range(2)
        for y in range(4)
    ]


def up(v):
    return v ^ 1


def down_pair(v):
    return ((v + 1) ^ 1) - 1


def flip(axis, by_core):
    way = (up, down_pair)

    def there(z, x, c, y):
        move = way[by_core[c]]
        return (
            move(z) if axis == "z" else z,
            move(x) if axis == "x" else x,
            c,
            move(y) if axis == "y" else y,
        )

    return pairs_of(there)


ACROSS = pairs_of(lambda z, x, c, y: (z, x + 2, c, y))
ALONG = [pairs_of(lambda z, x, c, y, by=by: (z, x, c, y + by)) for by in (1, 2, 3)]
SWAP_CORES = pairs_of(lambda z, x, c, y: (z, x, 1 - c, y))
PARTS = (32, 24, 16)
STEPS = (
    (flip("z", (0, 1)), flip("y", (0, 1)), flip("x", (0, 1))),
    (flip("y", (0, 1)), flip("x", (0, 1)), flip("z", (0, 1))),
)


def half_swap(x):
    n = x.shape[1]
    lane = lax.broadcasted_iota(jnp.int32, x.shape, 1) % 64
    return jnp.where(lane < 32, pltpu.roll(x, n - 32, 1), pltpu.roll(x, 32, 1))


def rotary_tables(relative):
    freqs = jnp.exp(jnp.arange(32, dtype=F32) * (-math.log(10000.0) / 32))
    angles = relative.astype(F32)[:, None] * freqs[None, :]
    c, s = jnp.cos(angles), jnp.sin(angles)
    return jnp.concatenate([c, c, c, c], axis=1), jnp.concatenate([-s, s, -s, s], axis=1)


def dot(a, b):
    return jnp.dot(a, b, preferred_element_type=F32)


def dot_nt(a, b):
    return lax.dot_general(a, b, (((1,), (1,)), ((), ())), preferred_element_type=F32)


def dot_tn(a, b):
    return lax.dot_general(a, b, (((0,), (0,)), ((), ())), preferred_element_type=F32)


def column_positions(info_ref, order_ref, len_ref):
    row = lax.broadcasted_iota(jnp.int32, (128, 1), 0)
    one, two = order_ref[0, info_ref[1]], order_ref[1, info_ref[1]]
    pos = jnp.where(row < 64, one * 64 + row, two * 64 + row - 64)
    start = jnp.zeros((128, 1), jnp.int32)
    end = jnp.int32(0)
    for e in range(6):
        end = end + len_ref[0, e]
        start = jnp.where(pos >= end, end, start)
    return pos, start, end


def qkv_kernel(info_ref, order_ref, len_ref, x_ref, g_ref, wq_hbm, wk_hbm, wv_hbm, out_ref, a_ref, wq, wk, wv, sems):
    copies = [
        pltpu.make_async_copy(hbm.at[:, 512 * h : 512 * (h + 1)], w.at[:, 512 * h : 512 * (h + 1)], sems.at[2 * i + h])
        for i, (hbm, w) in enumerate(((wq_hbm, wq), (wk_hbm, wk), (wv_hbm, wv)))
        for h in range(2)
    ]
    for copy in copies:
        copy.start()
    x = x_ref[...].astype(F32)
    factor = lax.rsqrt(jnp.mean(x * x, axis=-1, keepdims=True) + EPSILON)
    a = (x * factor * g_ref[...]).astype(BF)
    a_ref[...] = a
    pos, start, _ = column_positions(info_ref, order_ref, len_ref)
    lane = lax.broadcasted_iota(jnp.int32, (1, 128), 1)
    freqs = jnp.exp((lane % 32).astype(F32) * (-math.log(10000.0) / 32))
    angles = (pos - start).astype(F32) * freqs
    cos = jnp.cos(angles)
    sine = jnp.sin(angles)
    sin = jnp.where(lane % 64 < 32, -sine, sine)
    cos = jnp.concatenate([cos] * 4, axis=1)
    sin = jnp.concatenate([sin] * 4, axis=1)
    for i, w in enumerate((wq, wk, wv)):
        for h in range(2):
            copies[2 * i + h].wait()
            y = dot(a, w[:, 512 * h : 512 * (h + 1)])
            if i < 2:
                y = y * cos + half_swap(y) * sin
            y = y.astype(BF)
            for j in range(4):
                out_ref[4 * h + j, :, 128 * i : 128 * (i + 1)] = y[:, 128 * j : 128 * (j + 1)]


def qkv_call(info, order, lengths, x, gain, wq, wk, wv):
    return pl.pallas_call(
        qkv_kernel,
        in_specs=[SMEM, SMEM, SMEM, VMEM, VMEM, HBM, HBM, HBM],
        out_specs=[VMEM, VMEM],
        out_shape=[jax.ShapeDtypeStruct((8, 128, 384), BF), jax.ShapeDtypeStruct((128, 1024), BF)],
        scratch_shapes=[pltpu.VMEM((1024, 1024), BF)] * 3 + [pltpu.SemaphoreType.DMA((6,))],
        compiler_params=pltpu.CompilerParams(vmem_limit_bytes=60 * 2**20),
        cost_estimate=pl.CostEstimate(flops=2 * 128 * 1024 * 3072, bytes_accessed=7 * 2**20, transcendentals=0),
    )(info, order, lengths, x, gain, wq, wk, wv)


def allowed_mask(len_ref, q0, k0, k1):
    qpos = q0 + lax.broadcasted_iota(jnp.int32, (1, 256), 1)
    start = jnp.zeros((1, 256), jnp.int32)
    end = jnp.int32(0)
    for e in range(6):
        end = end + len_ref[0, e]
        start = jnp.where(qpos >= end, end, start)
    kpos = k0 + lax.broadcasted_iota(jnp.int32, (k1 - k0, 256), 0)
    return (kpos >= start) & (kpos <= qpos)


def attend_kernel(order_ref, len_ref, qkv_ref, out_ref, pos_ref, lse_ref, o_ref):
    for b in range(8):
        for j in range(2):
            at = pl.ds(pl.multiple_of(order_ref[j, b] * 64, 64), 64)
            pos_ref[at, :] = qkv_ref[b, 64 * j : 64 * (j + 1), :]
    first = lax.broadcasted_iota(jnp.int32, (1, 128), 1) < 64
    v_t = pos_ref[:, 256:384].T
    for q0, k0, k1 in TILES:
        q = pos_ref[q0 : q0 + 256, 0:128].astype(F32) * 0.125
        k = pos_ref[k0:k1, 128:256]
        mask = allowed_mask(len_ref, q0, k0, k1)
        outs = []
        for h in range(2):
            q_h = jnp.where(first if h == 0 else ~first, q, 0.0).astype(BF)
            s = jnp.where(mask, dot_nt(k, q_h), NEGATIVE)
            top = jnp.max(s, axis=0, keepdims=True)
            p = jnp.exp(s - top)
            total = jnp.sum(p, axis=0, keepdims=True)
            lse_ref[h : h + 1, q0 : q0 + 256] = top + jnp.log(total)
            p = (p * (1.0 / total)).astype(BF)
            outs.append(dot(v_t[64 * h : 64 * (h + 1), k0:k1], p))
        o_ref[q0 : q0 + 256, :] = jnp.concatenate(outs, axis=0).T.astype(BF)
    for b in range(8):
        for j in range(2):
            at = pl.ds(pl.multiple_of(order_ref[j, b] * 64, 64), 64)
            out_ref[b, 64 * j : 64 * (j + 1), :] = o_ref[at, :]


def attend_call(order, lengths, qkv):
    return pl.pallas_call(
        attend_kernel,
        in_specs=[SMEM, SMEM, VMEM],
        out_specs=[VMEM] * 3,
        out_shape=[
            jax.ShapeDtypeStruct((8, 128, 128), BF),
            jax.ShapeDtypeStruct((1024, 384), BF),
            jax.ShapeDtypeStruct((2, 1024), F32),
        ],
        scratch_shapes=[pltpu.VMEM((1024, 128), BF)],
        compiler_params=pltpu.CompilerParams(vmem_limit_bytes=24 * 2**20),
        cost_estimate=pl.CostEstimate(flops=2 * 10**9, bytes_accessed=3 * 2**20, transcendentals=2 * 10**6),
    )(order, lengths, qkv)


def attend_back_kernel(order_ref, len_ref, pos_ref, lse_ref, cos_ref, sin_ref, do_ref, out_ref, d_ref, dk_ref, dv_ref, dq_ref):
    for b in range(8):
        for j in range(2):
            at = pl.ds(pl.multiple_of(order_ref[j, b] * 64, 64), 64)
            d_ref[at, 0:128] = do_ref[b, 64 * j : 64 * (j + 1), :]
    first = lax.broadcasted_iota(jnp.int32, (1, 128), 1) < 64
    k_t = pos_ref[:, 128:256].T
    dk_ref[...] = jnp.zeros_like(dk_ref)
    dv_ref[...] = jnp.zeros_like(dv_ref)
    for q0, k0, k1 in TILES:
        q = pos_ref[q0 : q0 + 256, 0:128].astype(F32) * 0.125
        do = d_ref[q0 : q0 + 256, 0:128]
        k = pos_ref[k0:k1, 128:256]
        v = pos_ref[k0:k1, 256:384]
        mask = allowed_mask(len_ref, q0, k0, k1)
        outs = []
        for h in range(2):
            pick = first if h == 0 else ~first
            q_h = jnp.where(pick, q, 0.0).astype(BF)
            do_h = jnp.where(pick, do.astype(F32), 0.0).astype(BF)
            s = jnp.where(mask, dot_nt(k, q_h), NEGATIVE)
            p = jnp.exp(s - lse_ref[h : h + 1, q0 : q0 + 256])
            dp = dot_nt(v, do_h)
            delta = jnp.sum(p * dp, axis=0, keepdims=True)
            ds = (p * (dp - delta)).astype(BF)
            dv_ref[k0:k1, :] += dot(p.astype(BF), do_h)
            dk_ref[k0:k1, :] += dot(ds, q_h)
            outs.append(dot(k_t[64 * h : 64 * (h + 1), k0:k1], ds))
        dq_ref[q0 : q0 + 256, :] = jnp.concatenate(outs, axis=0).T * 0.125
    cos, sin = cos_ref[...], sin_ref[...]
    dq, dk = dq_ref[...], dk_ref[...]
    d_ref[:, 0:128] = (dq * cos - half_swap(dq) * sin).astype(BF)
    d_ref[:, 128:256] = (dk * cos - half_swap(dk) * sin).astype(BF)
    d_ref[:, 256:384] = dv_ref[...].astype(BF)
    for b in range(8):
        for j in range(2):
            at = pl.ds(pl.multiple_of(order_ref[j, b] * 64, 64), 64)
            out_ref[b, 64 * j : 64 * (j + 1), :] = d_ref[at, :]


def attend_back_call(order, lengths, pos, lse, cos, sin, d_out):
    return pl.pallas_call(
        attend_back_kernel,
        in_specs=[SMEM, SMEM, VMEM, VMEM, VMEM, VMEM, VMEM],
        out_specs=VMEM,
        out_shape=jax.ShapeDtypeStruct((8, 128, 384), BF),
        scratch_shapes=[
            pltpu.VMEM((1024, 384), BF),
            pltpu.VMEM((1024, 128), F32),
            pltpu.VMEM((1024, 128), F32),
            pltpu.VMEM((1024, 128), F32),
        ],
        compiler_params=pltpu.CompilerParams(vmem_limit_bytes=32 * 2**20),
        cost_estimate=pl.CostEstimate(flops=20000000000, bytes_accessed=1024, transcendentals=0),
    )(order, lengths, pos, lse, cos, sin, d_out)


ACT, M_AT, O_AT, DPRE, DD, DPROJ, SEND = 0, 4096, 5120, 6144, 8192, 8704, 9216
CHUNK = 1024


def mlp_kernel(info_ref, order_ref, len_ref, o_ref, x_ref, ct_ref, wo_hbm, wup_hbm, bup_ref, wdown_hbm, bdown_ref,
               g2_ref, g3_ref, g4_ref,
               out_ref, dmid_ref, do_ref, send_ref, keep_ref, vup_ref, vrow_ref,
               proj_ref, middle_ref, slope_ref, dd_ref, acc_ref, wo_ref, wup_ref, wdown_ref, sems):
    core = info_ref[0]
    count = 4096 // CHUNK
    copy_out = pltpu.make_async_copy(wo_hbm, wo_ref, sems.at[2 * count])
    copy_out.start()
    copies = []
    for i in range(count):
        at = slice(CHUNK * i, CHUNK * (i + 1))
        copies.append((
            pltpu.make_async_copy(wup_hbm.at[:, at], wup_ref.at[:, at], sems.at[2 * i]),
            pltpu.make_async_copy(wdown_hbm.at[at, :], wdown_ref.at[at, :], sems.at[2 * i + 1]),
        ))
        copies[-1][0].start()
        copies[-1][1].start()
    pos, _, end = column_positions(info_ref, order_ref, len_ref)
    valid = pos < end
    o = jnp.concatenate([o_ref[j] for j in range(8)], axis=1)
    send_ref[:, O_AT : O_AT + 1024] = o
    copy_out.wait()
    proj = dot(o, wo_ref[...])
    proj_ref[...] = proj
    r2 = lax.rsqrt(jnp.mean(proj * proj, axis=-1, keepdims=True) + EPSILON)
    middle = x_ref[...].astype(F32) + proj * r2 * g2_ref[...]
    middle_ref[...] = middle
    r3 = lax.rsqrt(jnp.mean(middle * middle, axis=-1, keepdims=True) + EPSILON)
    m = (middle * r3 * g3_ref[...]).astype(BF)
    send_ref[:, M_AT : M_AT + 1024] = m
    acc_ref[...] = jnp.zeros_like(acc_ref)
    root = math.sqrt(2.0 / math.pi)
    for i in range(4096 // CHUNK):
        at = slice(CHUNK * i, CHUNK * (i + 1))
        copies[i][0].wait()
        pre = dot(m, wup_ref[:, at]) + bup_ref[:, at]
        square = pre * pre
        t = jnp.tanh(root * (pre + 0.044715 * (square * pre)))
        half = 0.5 * (1.0 + t)
        act = (pre * half).astype(BF)
        slope_ref[:, at] = half + 0.5 * pre * (1.0 - t * t) * (root + (3.0 * 0.044715 * root) * square)
        send_ref[:, at] = act
        copies[i][1].wait()
        acc_ref[...] += dot(act, wdown_ref[at, :])
    down = acc_ref[...] + bdown_ref[...]
    r4 = lax.rsqrt(jnp.mean(down * down, axis=-1, keepdims=True) + EPSILON)
    out_ref[...] = jnp.where(valid, middle_ref[...] + down * r4 * g4_ref[...], 0.0).astype(BF)
    dy = jnp.where(valid, ct_ref[...].astype(F32), 0.0)
    dz = dy * down
    vrow_ref[0:1, :] = jnp.sum(dz * r4, axis=0, keepdims=True)
    inner = jnp.mean(dz * g4_ref[...], axis=-1, keepdims=True)
    dd = (r4 * g4_ref[...] * dy - down * (r4 * r4 * r4 * inner)).astype(BF)
    dd_ref[...] = dd
    vrow_ref[1:2, :] = jnp.sum(dd.astype(F32), axis=0, keepdims=True)
    send_ref[:, DD : DD + 512] = dd_ref[:, pl.ds(pl.multiple_of((1 - core) * 512, 512), 512)]
    keep_ref[:, 2048:2560] = dd_ref[:, pl.ds(pl.multiple_of(core * 512, 512), 512)]
    acc_ref[...] = jnp.zeros_like(acc_ref)
    for part in range(2):
        which = 1 - core if part == 0 else core
        for i in range(2048 // CHUNK):
            at = pl.ds(pl.multiple_of(which * 2048 + CHUNK * i, CHUNK), CHUNK)
            dact = dot_nt(dd, wdown_ref[at, :])
            dpre = (dact * slope_ref[:, at]).astype(BF)
            vup_ref[:, at] = jnp.sum(dpre.astype(F32), axis=0, keepdims=True)
            if part == 0:
                send_ref[:, DPRE + CHUNK * i : DPRE + CHUNK * (i + 1)] = dpre
            else:
                keep_ref[:, CHUNK * i : CHUNK * (i + 1)] = dpre
            acc_ref[...] += dot_nt(dpre, wup_ref[:, at])
    dm = acc_ref[...]
    middle = middle_ref[...]
    dz = dm * middle
    vrow_ref[2:3, :] = jnp.sum(dz * r3, axis=0, keepdims=True)
    inner = jnp.mean(dz * g3_ref[...], axis=-1, keepdims=True)
    dmid = dy + r3 * g3_ref[...] * dm - middle * (r3 * r3 * r3 * inner)
    dmid_ref[...] = dmid
    proj = proj_ref[...]
    dz = dmid * proj
    vrow_ref[3:4, :] = jnp.sum(dz * r2, axis=0, keepdims=True)
    inner = jnp.mean(dz * g2_ref[...], axis=-1, keepdims=True)
    dproj = (r2 * g2_ref[...] * dmid - proj * (r2 * r2 * r2 * inner)).astype(BF)
    dd_ref[...] = dproj
    send_ref[:, DPROJ : DPROJ + 512] = dd_ref[:, pl.ds(pl.multiple_of((1 - core) * 512, 512), 512)]
    keep_ref[:, 2560:3072] = dd_ref[:, pl.ds(pl.multiple_of(core * 512, 512), 512)]
    d_out = dot_nt(dproj, wo_ref[...]).astype(BF)
    for j in range(8):
        do_ref[j] = d_out[:, 128 * j : 128 * (j + 1)]


def mlp_call(*args):
    shape = jax.ShapeDtypeStruct
    return pl.pallas_call(
        mlp_kernel,
        in_specs=[SMEM] * 3 + [VMEM] * 3 + [HBM, HBM, VMEM, HBM] + [VMEM] * 4,
        out_specs=[VMEM] * 7,
        out_shape=[
            shape((128, 1024), BF), shape((128, 1024), F32), shape((8, 128, 128), BF), shape((128, SEND), BF),
            shape((128, 3072), BF), shape((1, 4096), F32), shape((4, 1024), F32),
        ],
        scratch_shapes=[
            pltpu.VMEM((128, 1024), F32), pltpu.VMEM((128, 1024), F32), pltpu.VMEM((128, 4096), F32),
            pltpu.VMEM((128, 1024), BF), pltpu.VMEM((128, 1024), F32),
            pltpu.VMEM((1024, 1024), BF), pltpu.VMEM((1024, 4096), BF), pltpu.VMEM((4096, 1024), BF),
            pltpu.SemaphoreType.DMA((2 * 4096 // CHUNK + 1,)),
        ],
        compiler_params=pltpu.CompilerParams(vmem_limit_bytes=60 * 2**20),
        cost_estimate=pl.CostEstimate(flops=4 * 128 * 9 * 2**20, bytes_accessed=20 * 2**20, transcendentals=2**19),
    )(*args)


def grad_parts(info_ref, relative, lefts, rights, outs, copies):
    bz, by, bx = info_ref[2], info_ref[3], info_ref[4]

    def left(at, n):
        return lefts[at : at + n, :]

    def cols(at, n):
        return rights[:, pl.ds(pl.multiple_of(at, 128), n)]

    eights = lambda g: [g[:, 128 * i : 128 * (i + 1)].reshape(128, 8, 128) for i in range(g.shape[1] // 128)]
    for k2 in range(2):
        block = 2 * (relative ^ bz) + k2
        rhs = jnp.concatenate([cols(u * 512 + block * 128, 128) for u in range(4)], axis=1)
        rows = eights(dot(left(M_AT, 1024), rhs))
        outs[0][k2 ^ by] = jnp.concatenate(rows, axis=1).reshape(4096, 128).astype(BF)
    copies[0].start()
    rhs = cols(2048 + 256 * (relative ^ by), 256)
    for half in range(2):
        g = dot(left(2048 * half, 2048), rhs)
        for k2 in range(2):
            part = g[:, 128 * k2 : 128 * (k2 + 1)].reshape(64, 32, 128)[:, 0:24]
            outs[1][k2 ^ bx, 1536 * half : 1536 * (half + 1), :] = part.reshape(1536, 128).astype(BF)
    copies[1].start()
    first = 256 * (relative ^ bx)
    g_out = eights(dot(left(O_AT, 1024), cols(2560 + first, 256)))
    for half in range(2):
        g_down = dot(left(2048 * half, 2048), cols(2048 + first, 256))
        d = slice(64 * half, 64 * (half + 1))
        for k2 in range(2):
            tail = g_down[:, 128 * k2 : 128 * (k2 + 1)].reshape(64, 32, 128)[:, 24:32]
            rows = jnp.concatenate([tail, g_out[k2][d]], axis=1)
            outs[2][k2 ^ bz, 1024 * half : 1024 * (half + 1), :] = rows.reshape(1024, 128).astype(BF)
    copies[2].start()


def turn(mine, theirs, lefts):
    for i in range(6144 // 512):
        at = slice(512 * i, 512 * (i + 1))
        lefts[at, 0:128] = mine[:, at].T
        lefts[at, 128:256] = theirs[:, at].T


def grads_kernel(relative, info_ref, mine_ref, keep_ref, theirs_ref, p_hbm, q_hbm, r_hbm, lefts, rights, p_ref, q_ref, r_ref, sems):
    turn(mine_ref, theirs_ref, lefts)
    rights[0:128, :] = keep_ref[...]
    rights[128:256, :] = theirs_ref[:, DPRE:SEND]
    copies = [
        pltpu.make_async_copy(ref, hbm, sems.at[i])
        for i, (ref, hbm) in enumerate(((p_ref, p_hbm), (q_ref, q_hbm), (r_ref, r_hbm)))
    ]
    grad_parts(info_ref, relative, lefts, rights, (p_ref, q_ref, r_ref), copies)
    for copy in copies:
        copy.wait()


PART_SHAPES = [jax.ShapeDtypeStruct((2, 128 * n, 128), BF) for n in PARTS]


def grads_call(relative, info, send, keep, got):
    return pl.pallas_call(
        functools.partial(grads_kernel, relative),
        in_specs=[SMEM, VMEM, VMEM, VMEM],
        out_specs=[HBM] * 3,
        out_shape=PART_SHAPES,
        scratch_shapes=[pltpu.VMEM((6144, 256), BF), pltpu.VMEM((256, 3072), BF)]
        + [pltpu.VMEM((2, 128 * n, 128), BF) for n in PARTS]
        + [pltpu.SemaphoreType.DMA((3,))],
        compiler_params=pltpu.CompilerParams(vmem_limit_bytes=60 * 2**20),
        cost_estimate=pl.CostEstimate(flops=1, bytes_accessed=1024, transcendentals=0),
    )(info, send, keep, got)


ROWS = 88


def add_kernel(*refs):
    for k, a, out in zip(refs[0:3], refs[3:6], refs[6:9]):
        out[...] = k[0] + a[0]


def add_call(kept, one):
    return pl.pallas_call(
        add_kernel,
        grid=(2,),
        in_specs=[pl.BlockSpec((1, 64 * n, 128), lambda j: (1, j, 0)) for n in PARTS] * 2,
        out_specs=[pl.BlockSpec((64 * n, 128), lambda j: (j, 0)) for n in PARTS],
        out_shape=[jax.ShapeDtypeStruct((128 * n, 128), BF) for n in PARTS],
        compiler_params=pltpu.CompilerParams(vmem_limit_bytes=60 * 2**20),
        cost_estimate=pl.CostEstimate(flops=1, bytes_accessed=1024, transcendentals=0),
    )(*kept, *one)


def pack_kernel(*refs):
    rows = []
    for k, a, b, n in zip(refs[0:3], refs[3:6], refs[6:9], PARTS):
        total = k[0].astype(F32) + a[0].astype(F32) + b[...].astype(F32)
        rows.append(total.reshape(64, n, 128))
    rows.append(refs[9][...].astype(F32) + refs[10][...].astype(F32))
    refs[11][...] = jnp.concatenate(rows, axis=1).astype(BF)


def pack_call(kept, one, two, qkv, qkv_two):
    half = [pl.BlockSpec((1, 64 * n, 128), lambda j: (0, j, 0)) for n in PARTS]
    tail = pl.BlockSpec((64, 16, 128), lambda j: (j, 0, 0))
    return pl.pallas_call(
        pack_kernel,
        grid=(2,),
        in_specs=half * 2 + [pl.BlockSpec((64 * n, 128), lambda j: (j, 0)) for n in PARTS] + [tail] * 2,
        out_specs=pl.BlockSpec((64, ROWS, 128), lambda j: (j, 0, 0)),
        out_shape=jax.ShapeDtypeStruct((128, ROWS, 128), BF),
        compiler_params=pltpu.CompilerParams(vmem_limit_bytes=60 * 2**20),
        cost_estimate=pl.CostEstimate(flops=1, bytes_accessed=1024, transcendentals=0),
    )(*kept, *one, *two, qkv, qkv_two)


def bits_of(s):
    return {n: (s >> i) & 1 for i, n in enumerate(("xh", "yl", "yh", "core", "xl", "zl", "zh"))}


def sum_kernel(got_ref, w_ref, g_ref, up_ref, down_ref, wo_ref, q_ref, k_ref, v_ref, gain_ref, *vec_refs):
    def total(keys, at, n):
        sums = {}
        for s in range(128):
            b = bits_of(s)
            k = tuple(b[name] for name in keys)
            v = got_ref[s].astype(F32)[at : at + n]
            sums[k] = sums[k] + v if k in sums else v
        return sums

    for (core, k1, k2), v in total(("core", "zl", "yl"), 0, 32).items():
        for u in range(4):
            at = core * 2048 + u * 512 + (2 * k1 + k2) * 128
            up_ref[:, at : at + 128] = v[8 * u : 8 * (u + 1)]
    for (core, k1, k2), v in total(("core", "yl", "xl"), 32, 24).items():
        at = core * 512 + (2 * k1 + k2) * 128
        down_ref[0:24, at : at + 128] = v
    for (core, k1, k2), v in total(("core", "xl", "zl"), 56, 16).items():
        at = core * 512 + (2 * k1 + k2) * 128
        down_ref[24:32, at : at + 128] = v[0:8]
        wo_ref[:, at : at + 128] = v[8:16]
    weighted = jnp.zeros((8, 128), F32)
    vec = jnp.zeros((8, 128), F32)
    for (core, yh, yl, xh), v in total(("core", "yh", "yl", "xh"), 72, 16).items():
        b = 4 * yh + 2 * yl + xh
        at = slice(128 * b, 128 * (b + 1))
        for i, out in ((2, v_ref),) if core else ((0, q_ref), (1, k_ref)):
            part = v[8 * (i % 2) : 8 * (i % 2) + 8]
            out[:, at] = part
            weighted = weighted + part * w_ref[i, :, at]
        if core:
            vec = vec + v[8:16]
    gain_ref[...] = jnp.sum(weighted.T, axis=0, keepdims=True) / g_ref[...]
    at = 0
    for ref in vec_refs:
        n = ref.shape[1]
        ref[...] = vec[0:1, at : at + n]
        at += n


def sum_call(got, w_rows, gain_rows):
    shape = jax.ShapeDtypeStruct
    return pl.pallas_call(
        sum_kernel,
        in_specs=[VMEM] * 3,
        out_specs=[VMEM] * 12,
        out_shape=[shape((8, 4096), F32), shape((32, 1024), F32)]
        + [shape((8, 1024), F32)] * 4
        + [shape((1, n), F32) for n in (8, 32, 8, 8, 8, 8)],
        compiler_params=pltpu.CompilerParams(vmem_limit_bytes=16 * 2**20),
        cost_estimate=pl.CostEstimate(flops=10**7, bytes_accessed=3 * 2**20, transcendentals=0),
    )(got, w_rows, gain_rows)


def qkv_grads_kernel(info_ref, a0_ref, a1_ref, a2_ref, a3_ref, d_ref, vec_ref, keep_ref, send_ref):
    y, xh = info_ref[1] // 2, info_ref[1] % 2
    g = jnp.zeros((512, 384), F32)
    for back, ref in enumerate((a0_ref, a1_ref, a2_ref, a3_ref)):
        source = ((y + 4 - back) % 4) * 2
        d = jnp.concatenate([d_ref[source + xh], d_ref[source + 1 - xh]], axis=0)
        g = g + dot_tn(ref[...].reshape(256, 512), d)
    parts = [g[:, 128 * i : 128 * (i + 1)].reshape(64, 8, 128) for i in range(3)]
    first = lax.broadcasted_iota(jnp.int32, (64, 8, 128), 1) == 0
    parts.append(jnp.where(first, vec_ref[...].reshape(64, 1, 128), 0.0))
    one, two = (jnp.concatenate(parts[i : i + 2], axis=1) for i in (0, 2))
    mine = info_ref[0] == 0
    keep_ref[...] = jnp.where(mine, one, two).astype(BF)
    send_ref[...] = jnp.where(mine, two, one).astype(BF)


def qkv_grads_call(info, pairs, d_heads, vec):
    return pl.pallas_call(
        qkv_grads_kernel,
        grid=(2,),
        in_specs=[SMEM]
        + [pl.BlockSpec((2, 128, 512), lambda j: (0, 0, j))] * 4
        + [pl.BlockSpec((8, 128, 384), lambda j: (0, 0, 0)), pl.BlockSpec((64, 128), lambda j: (j, 0))],
        out_specs=[pl.BlockSpec((64, 16, 128), lambda j: (j, 0, 0))] * 2,
        out_shape=[jax.ShapeDtypeStruct((128, 16, 128), BF)] * 2,
        compiler_params=pltpu.CompilerParams(vmem_limit_bytes=63 * 2**20),
        cost_estimate=pl.CostEstimate(flops=1, bytes_accessed=1024, transcendentals=0),
    )(info, *pairs, d_heads, vec)


def input_kernel(d_ref, wq_ref, wk_ref, wv_ref, x_ref, g_ref, dmid_ref, out_ref):
    step = pl.program_id(0)
    acc = jnp.where(step == 0, 0.0, out_ref[...])
    for i, w_ref in enumerate((wq_ref, wk_ref, wv_ref)):
        d = jnp.concatenate([d_ref[j, :, 128 * i : 128 * (i + 1)] for j in range(2)], axis=1)
        acc = acc + dot_nt(d, w_ref[...])
    out_ref[...] = acc

    @pl.when(step == 3)
    def _():
        x = x_ref[...].astype(F32)
        r = lax.rsqrt(jnp.mean(x * x, axis=-1, keepdims=True) + EPSILON)
        dz = out_ref[...] * g_ref[...]
        inner = jnp.mean(dz * x, axis=-1, keepdims=True)
        out_ref[...] = dmid_ref[...] + r * dz - x * (r * r * r * inner)


def input_call(d_mine, wq, wk, wv, x, gain, dmid):
    whole = lambda shape: pl.BlockSpec(shape, lambda j: (0,) * len(shape))
    col = pl.BlockSpec((1024, 256), lambda j: (0, j))
    return pl.pallas_call(
        input_kernel,
        grid=(4,),
        in_specs=[pl.BlockSpec((2, 128, 384), lambda j: (j, 0, 0)), col, col, col, whole((128, 1024)), whole((1, 1024)), whole((128, 1024))],
        out_specs=whole((128, 1024)),
        out_shape=jax.ShapeDtypeStruct((128, 1024), F32),
        compiler_params=pltpu.CompilerParams(vmem_limit_bytes=16 * 2**20),
        cost_estimate=pl.CostEstimate(flops=2 * 128 * 1024 * 3072, bytes_accessed=7 * 2**20, transcendentals=0),
    )(d_mine, wq, wk, wv, x, gain, dmid)


def local(
    tokens, lengths, order, w_query, w_key, w_value, w_out, w_up, b_up, w_down, b_down,
    gain_attn_in, gain_attn_out, gain_mlp_in, gain_mlp_out, cotangent,
):
    z, xl, core, y, xh = (lax.axis_index(a) for a in ALL)
    my_blk = y * 2 + xh
    me = ((z * 2 + xl) * 2 + core) * 8 + my_blk
    info = jnp.stack([core, my_blk, z % 2, y % 2, xl]).astype(jnp.int32)
    row = lambda v: v.reshape(1, -1)
    order = order.T
    tie = lax.optimization_barrier

    qkv, attn_low = qkv_call(info, order, lengths, tokens, row(gain_attn_in), w_query, w_key, w_value)
    across = lax.ppermute(attn_low, ALL, ACROSS)
    qkv_heads = lax.all_to_all(qkv, BLK, 0, 0, tiled=True)

    late_lengths, _ = tie((lengths, qkv))
    lengths_row = late_lengths[0]
    group_pos = jnp.arange(1024, dtype=jnp.int32)
    start = jnp.zeros((1024,), jnp.int32)
    end = jnp.int32(0)
    for e in range(6):
        end = end + lengths_row[e]
        start = jnp.where(group_pos >= end, end, start)
    cos_all, sin_all = rotary_tables(group_pos - start)

    qkv_heads, cos_all, sin_all, pair = tie((qkv_heads, cos_all, sin_all, jnp.stack([attn_low, across])))

    pairs = [pair] + [lax.ppermute(pair, ALL, to) for to in ALONG]
    out_heads, pos_qkv, lse = attend_call(order, lengths, qkv_heads)
    out_mine = lax.all_to_all(out_heads, BLK, 0, 0, tiled=True)
    out_mine, pairs[2] = tie((out_mine, pairs[2]))
    output, d_middle, d_out, send, keep, v_up, v_row = mlp_call(
        info, order, lengths, out_mine, tokens, cotangent, w_out, w_up, row(b_up), w_down, row(b_down),
        row(gain_attn_out), row(gain_mlp_in), row(gain_mlp_out),
    )
    send, keep, d_out, pairs = tie((send, keep, d_out, pairs))
    d_out_heads = lax.all_to_all(d_out, BLK, 0, 0, tiled=True)
    got = lax.ppermute(send, ALL, SWAP_CORES)
    sent = grads_call(1, info, send, keep, got)
    lse, _ = tie((lse, sent))
    one = [lax.ppermute(p, ALL, to) for p, to in zip(sent, STEPS[0])]
    d_heads = attend_back_call(order, lengths, pos_qkv, lse, cos_all, sin_all, d_out_heads)
    d_mine = lax.all_to_all(d_heads, BLK, 0, 0, tiled=True)
    keep, _ = tie((keep, d_heads))
    kept = grads_call(0, info, send, keep, got)
    v_up, v_row, _ = tie((v_up, v_row, d_heads))
    vectors = jnp.concatenate(
        [v_up.reshape(128, 32)] + [v_row[i].reshape(128, 8) for i in (1, 3, 2, 0)] + [jnp.zeros((128, 64), F32)], axis=1
    )
    one, vectors = tie((one, vectors))
    added = add_call(kept, one)
    two = [lax.ppermute(p, ALL, to) for p, to in zip(added, STEPS[1])]
    d_grads, d_mine, _ = tie((d_heads, d_mine, added))
    qkv_keep, qkv_send = qkv_grads_call(info, pairs, d_grads, vectors)
    qkv_send, two[2] = tie((qkv_send, two[2]))
    packed = pack_call(kept, one, two, qkv_keep, lax.ppermute(qkv_send, ALL, SWAP_CORES))
    got_all = lax.all_to_all(packed, ALL, 0, 0, tiled=True)

    grad_tokens = input_call(d_mine, w_query, w_key, w_value, tokens, row(gain_attn_in), d_middle)
    my_rows = lambda w: lax.dynamic_slice_in_dim(w, me * 8, 8, 0).astype(F32)
    w_rows = jnp.stack([my_rows(w) for w in (w_query, w_key, w_value)])
    gain_rows = lax.dynamic_slice_in_dim(gain_attn_in, me * 8, 8, 0).reshape(1, 8)
    grad_w_up, grad_w_down, grad_w_out, grad_w_query, grad_w_key, grad_w_value, *vec = sum_call(got_all, w_rows, gain_rows)
    grad_gain_attn_in, grad_b_up, grad_b_down, grad_gain_attn_out, grad_gain_mlp_in, grad_gain_mlp_out = (
        v.reshape(-1) for v in vec
    )
    return (
        output, grad_tokens, grad_w_query, grad_w_key, grad_w_value, grad_w_out, grad_w_up, grad_b_up, grad_w_down,
        grad_b_down, grad_gain_attn_in, grad_gain_attn_out, grad_gain_mlp_in, grad_gain_mlp_out,
    )


def solution(mesh):
    split = Mesh(np.asarray(mesh.devices).reshape(4, 2, 2, 4, 2), ALL)
    every = P(ALL, None)
    flat = P(ALL)
    return jax.shard_map(
        local,
        mesh=split,
        in_specs=(every, P(("z", "xl", "core"), None)) + (P(),) * 13 + (every,),
        out_specs=(every,) * 7 + (flat, every) + (flat,) * 5,
        check_vma=False,
    )
```

```python
import functools
import math

import jax
import jax.numpy as jnp
import numpy as np
from jax import lax
from jax.experimental import pallas as pl
from jax.experimental.pallas import tpu as pltpu
from jax.sharding import Mesh
from jax.sharding import PartitionSpec as P

HEADS = 16
EPSILON = 1e-05
NEGATIVE = -1e30
ALL = ("z", "xl", "core", "y", "xh")
BLK = ("y", "xh")
BF = jnp.bfloat16
F32 = jnp.float32
TILES = ((0, 0, 256), (256, 0, 512), (512, 0, 768), (768, 512, 1024))


SMEM = pl.BlockSpec(memory_space=pltpu.SMEM)
VMEM = pl.BlockSpec(memory_space=pltpu.VMEM)
HBM = pl.BlockSpec(memory_space=pltpu.HBM)


def device_index(z, x, c, y):
    return (((z % 4) * 2 + (x % 4) % 2) * 2 + c) * 8 + (y % 4) * 2 + (x % 4) // 2


def pairs_of(f):
    return [
        (device_index(z, x, c, y), device_index(*f(z, x, c, y)))
        for z in range(4)
        for x in range(4)
        for c in range(2)
        for y in range(4)
    ]


def up(v):
    return v ^ 1


def down_pair(v):
    return ((v + 1) ^ 1) - 1


def flip(axis, by_core):
    way = (up, down_pair)

    def there(z, x, c, y):
        move = way[by_core[c]]
        return (
            move(z) if axis == "z" else z,
            move(x) if axis == "x" else x,
            c,
            move(y) if axis == "y" else y,
        )

    return pairs_of(there)


ACROSS = pairs_of(lambda z, x, c, y: (z, x + 2, c, y))
ALONG = [pairs_of(lambda z, x, c, y, by=by: (z, x, c, y + by)) for by in (1, 2, 3)]
SWAP_CORES = pairs_of(lambda z, x, c, y: (z, x, 1 - c, y))
PARTS = (24, 24, 24)
STEPS = (
    (flip("x", (0, 1)), flip("z", (0, 1)), flip("y", (0, 1))),
    (flip("z", (0, 1)), flip("y", (0, 1)), flip("x", (0, 1))),
)


def half_swap(x):
    n = x.shape[1]
    lane = lax.broadcasted_iota(jnp.int32, x.shape, 1) % 64
    return jnp.where(lane < 32, pltpu.roll(x, n - 32, 1), pltpu.roll(x, 32, 1))


def rotary_tables(relative):
    freqs = jnp.exp(jnp.arange(32, dtype=F32) * (-math.log(10000.0) / 32))
    angles = relative.astype(F32)[:, None] * freqs[None, :]
    c, s = jnp.cos(angles), jnp.sin(angles)
    return jnp.concatenate([c, c, c, c], axis=1), jnp.concatenate([-s, s, -s, s], axis=1)


def dot(a, b):
    return jnp.dot(a, b, preferred_element_type=F32)


def dot_nt(a, b):
    return lax.dot_general(a, b, (((1,), (1,)), ((), ())), preferred_element_type=F32)


def dot_tn(a, b):
    return lax.dot_general(a, b, (((0,), (0,)), ((), ())), preferred_element_type=F32)


def column_positions(info_ref, order_ref, len_ref):
    row = lax.broadcasted_iota(jnp.int32, (128, 1), 0)
    one, two = order_ref[0, info_ref[1]], order_ref[1, info_ref[1]]
    pos = jnp.where(row < 64, one * 64 + row, two * 64 + row - 64)
    start = jnp.zeros((128, 1), jnp.int32)
    end = jnp.int32(0)
    for e in range(6):
        end = end + len_ref[0, e]
        start = jnp.where(pos >= end, end, start)
    return pos, start, end


def qkv_kernel(info_ref, order_ref, len_ref, x_ref, g_ref, wq_hbm, wk_hbm, wv_hbm, out_ref, a_ref, wq, wk, wv, sems):
    copies = [
        pltpu.make_async_copy(hbm.at[:, 512 * h : 512 * (h + 1)], w.at[:, 512 * h : 512 * (h + 1)], sems.at[2 * i + h])
        for i, (hbm, w) in enumerate(((wq_hbm, wq), (wk_hbm, wk), (wv_hbm, wv)))
        for h in range(2)
    ]
    for copy in copies:
        copy.start()
    x = x_ref[...].astype(F32)
    factor = lax.rsqrt(jnp.mean(x * x, axis=-1, keepdims=True) + EPSILON)
    a = (x * factor * g_ref[...]).astype(BF)
    a_ref[...] = a
    pos, start, _ = column_positions(info_ref, order_ref, len_ref)
    lane = lax.broadcasted_iota(jnp.int32, (1, 128), 1)
    freqs = jnp.exp((lane % 32).astype(F32) * (-math.log(10000.0) / 32))
    angles = (pos - start).astype(F32) * freqs
    cos = jnp.cos(angles)
    sine = jnp.sin(angles)
    sin = jnp.where(lane % 64 < 32, -sine, sine)
    cos = jnp.concatenate([cos] * 4, axis=1)
    sin = jnp.concatenate([sin] * 4, axis=1)
    for i, w in enumerate((wq, wk, wv)):
        for h in range(2):
            copies[2 * i + h].wait()
            y = dot(a, w[:, 512 * h : 512 * (h + 1)])
            if i < 2:
                y = y * cos + half_swap(y) * sin
            y = y.astype(BF)
            for j in range(4):
                out_ref[4 * h + j, :, 128 * i : 128 * (i + 1)] = y[:, 128 * j : 128 * (j + 1)]


def qkv_call(info, order, lengths, x, gain, wq, wk, wv):
    return pl.pallas_call(
        qkv_kernel,
        in_specs=[SMEM, SMEM, SMEM, VMEM, VMEM, HBM, HBM, HBM],
        out_specs=[VMEM, VMEM],
        out_shape=[jax.ShapeDtypeStruct((8, 128, 384), BF), jax.ShapeDtypeStruct((128, 1024), BF)],
        scratch_shapes=[pltpu.VMEM((1024, 1024), BF)] * 3 + [pltpu.SemaphoreType.DMA((6,))],
        compiler_params=pltpu.CompilerParams(vmem_limit_bytes=60 * 2**20),
        cost_estimate=pl.CostEstimate(flops=2 * 128 * 1024 * 3072, bytes_accessed=7 * 2**20, transcendentals=0),
    )(info, order, lengths, x, gain, wq, wk, wv)


def allowed_mask(len_ref, q0, k0, k1):
    qpos = q0 + lax.broadcasted_iota(jnp.int32, (1, 256), 1)
    start = jnp.zeros((1, 256), jnp.int32)
    end = jnp.int32(0)
    for e in range(6):
        end = end + len_ref[0, e]
        start = jnp.where(qpos >= end, end, start)
    kpos = k0 + lax.broadcasted_iota(jnp.int32, (k1 - k0, 256), 0)
    return (kpos >= start) & (kpos <= qpos)


def attend_kernel(order_ref, len_ref, qkv_ref, out_ref, pos_ref, lse_ref, o_ref):
    for b in range(8):
        for j in range(2):
            at = pl.ds(pl.multiple_of(order_ref[j, b] * 64, 64), 64)
            pos_ref[at, :] = qkv_ref[b, 64 * j : 64 * (j + 1), :]
    first = lax.broadcasted_iota(jnp.int32, (1, 128), 1) < 64
    v_t = pos_ref[:, 256:384].T
    for q0, k0, k1 in TILES:
        q = pos_ref[q0 : q0 + 256, 0:128].astype(F32) * 0.125
        k = pos_ref[k0:k1, 128:256]
        mask = allowed_mask(len_ref, q0, k0, k1)
        outs = []
        for h in range(2):
            q_h = jnp.where(first if h == 0 else ~first, q, 0.0).astype(BF)
            s = jnp.where(mask, dot_nt(k, q_h), NEGATIVE)
            top = jnp.max(s, axis=0, keepdims=True)
            p = jnp.exp(s - top)
            total = jnp.sum(p, axis=0, keepdims=True)
            lse_ref[h : h + 1, q0 : q0 + 256] = top + jnp.log(total)
            p = (p * (1.0 / total)).astype(BF)
            outs.append(dot(v_t[64 * h : 64 * (h + 1), k0:k1], p))
        o_ref[q0 : q0 + 256, :] = jnp.concatenate(outs, axis=0).T.astype(BF)
    for b in range(8):
        for j in range(2):
            at = pl.ds(pl.multiple_of(order_ref[j, b] * 64, 64), 64)
            out_ref[b, 64 * j : 64 * (j + 1), :] = o_ref[at, :]


def attend_call(order, lengths, qkv):
    return pl.pallas_call(
        attend_kernel,
        in_specs=[SMEM, SMEM, VMEM],
        out_specs=[VMEM] * 3,
        out_shape=[
            jax.ShapeDtypeStruct((8, 128, 128), BF),
            jax.ShapeDtypeStruct((1024, 384), BF),
            jax.ShapeDtypeStruct((2, 1024), F32),
        ],
        scratch_shapes=[pltpu.VMEM((1024, 128), BF)],
        compiler_params=pltpu.CompilerParams(vmem_limit_bytes=24 * 2**20),
        cost_estimate=pl.CostEstimate(flops=2 * 10**9, bytes_accessed=3 * 2**20, transcendentals=2 * 10**6),
    )(order, lengths, qkv)


def attend_back_kernel(order_ref, len_ref, pos_ref, lse_ref, cos_ref, sin_ref, do_ref, out_ref, d_ref, dk_ref, dv_ref, dq_ref):
    for b in range(8):
        for j in range(2):
            at = pl.ds(pl.multiple_of(order_ref[j, b] * 64, 64), 64)
            d_ref[at, 0:128] = do_ref[b, 64 * j : 64 * (j + 1), :]
    first = lax.broadcasted_iota(jnp.int32, (1, 128), 1) < 64
    k_t = pos_ref[:, 128:256].T
    dk_ref[...] = jnp.zeros_like(dk_ref)
    dv_ref[...] = jnp.zeros_like(dv_ref)
    for q0, k0, k1 in TILES:
        q = pos_ref[q0 : q0 + 256, 0:128].astype(F32) * 0.125
        do = d_ref[q0 : q0 + 256, 0:128]
        k = pos_ref[k0:k1, 128:256]
        v = pos_ref[k0:k1, 256:384]
        mask = allowed_mask(len_ref, q0, k0, k1)
        outs = []
        for h in range(2):
            pick = first if h == 0 else ~first
            q_h = jnp.where(pick, q, 0.0).astype(BF)
            do_h = jnp.where(pick, do.astype(F32), 0.0).astype(BF)
            s = jnp.where(mask, dot_nt(k, q_h), NEGATIVE)
            p = jnp.exp(s - lse_ref[h : h + 1, q0 : q0 + 256])
            dp = dot_nt(v, do_h)
            delta = jnp.sum(p * dp, axis=0, keepdims=True)
            ds = (p * (dp - delta)).astype(BF)
            dv_ref[k0:k1, :] += dot(p.astype(BF), do_h)
            dk_ref[k0:k1, :] += dot(ds, q_h)
            outs.append(dot(k_t[64 * h : 64 * (h + 1), k0:k1], ds))
        dq_ref[q0 : q0 + 256, :] = jnp.concatenate(outs, axis=0).T * 0.125
    cos, sin = cos_ref[...], sin_ref[...]
    dq, dk = dq_ref[...], dk_ref[...]
    d_ref[:, 0:128] = (dq * cos - half_swap(dq) * sin).astype(BF)
    d_ref[:, 128:256] = (dk * cos - half_swap(dk) * sin).astype(BF)
    d_ref[:, 256:384] = dv_ref[...].astype(BF)
    for b in range(8):
        for j in range(2):
            at = pl.ds(pl.multiple_of(order_ref[j, b] * 64, 64), 64)
            out_ref[b, 64 * j : 64 * (j + 1), :] = d_ref[at, :]


def attend_back_call(order, lengths, pos, lse, cos, sin, d_out):
    return pl.pallas_call(
        attend_back_kernel,
        in_specs=[SMEM, SMEM, VMEM, VMEM, VMEM, VMEM, VMEM],
        out_specs=VMEM,
        out_shape=jax.ShapeDtypeStruct((8, 128, 384), BF),
        scratch_shapes=[
            pltpu.VMEM((1024, 384), BF),
            pltpu.VMEM((1024, 128), F32),
            pltpu.VMEM((1024, 128), F32),
            pltpu.VMEM((1024, 128), F32),
        ],
        compiler_params=pltpu.CompilerParams(vmem_limit_bytes=32 * 2**20),
        cost_estimate=pl.CostEstimate(flops=20000000000, bytes_accessed=1024, transcendentals=0),
    )(order, lengths, pos, lse, cos, sin, d_out)


ACT, M_AT, O_AT, DPRE, DD, DPROJ, SEND = 0, 4096, 5120, 6144, 8192, 8704, 9216
CHUNK = 1024


def mlp_kernel(info_ref, order_ref, len_ref, o_ref, x_ref, ct_ref, wo_hbm, wup_hbm, bup_ref, wdown_hbm, bdown_ref,
               g2_ref, g3_ref, g4_ref,
               out_ref, dmid_ref, do_ref, send_ref, keep_ref, vup_ref, vrow_ref,
               proj_ref, middle_ref, slope_ref, dd_ref, acc_ref, wo_ref, wup_ref, wdown_ref, sems):
    core = info_ref[0]
    count = 4096 // CHUNK
    copy_out = pltpu.make_async_copy(wo_hbm, wo_ref, sems.at[2 * count])
    copy_out.start()
    copies = []
    for i in range(count):
        at = slice(CHUNK * i, CHUNK * (i + 1))
        copies.append((
            pltpu.make_async_copy(wup_hbm.at[:, at], wup_ref.at[:, at], sems.at[2 * i]),
            pltpu.make_async_copy(wdown_hbm.at[at, :], wdown_ref.at[at, :], sems.at[2 * i + 1]),
        ))
        copies[-1][0].start()
        copies[-1][1].start()
    pos, _, end = column_positions(info_ref, order_ref, len_ref)
    valid = pos < end
    o = jnp.concatenate([o_ref[j] for j in range(8)], axis=1)
    send_ref[:, O_AT : O_AT + 1024] = o
    copy_out.wait()
    proj = dot(o, wo_ref[...])
    proj_ref[...] = proj
    r2 = lax.rsqrt(jnp.mean(proj * proj, axis=-1, keepdims=True) + EPSILON)
    middle = x_ref[...].astype(F32) + proj * r2 * g2_ref[...]
    middle_ref[...] = middle
    r3 = lax.rsqrt(jnp.mean(middle * middle, axis=-1, keepdims=True) + EPSILON)
    m = (middle * r3 * g3_ref[...]).astype(BF)
    send_ref[:, M_AT : M_AT + 1024] = m
    acc_ref[...] = jnp.zeros_like(acc_ref)
    root = math.sqrt(2.0 / math.pi)
    for i in range(4096 // CHUNK):
        at = slice(CHUNK * i, CHUNK * (i + 1))
        copies[i][0].wait()
        pre = dot(m, wup_ref[:, at]) + bup_ref[:, at]
        square = pre * pre
        t = jnp.tanh(root * (pre + 0.044715 * (square * pre)))
        half = 0.5 * (1.0 + t)
        act = (pre * half).astype(BF)
        slope_ref[:, at] = half + 0.5 * pre * (1.0 - t * t) * (root + (3.0 * 0.044715 * root) * square)
        send_ref[:, at] = act
        copies[i][1].wait()
        acc_ref[...] += dot(act, wdown_ref[at, :])
    down = acc_ref[...] + bdown_ref[...]
    r4 = lax.rsqrt(jnp.mean(down * down, axis=-1, keepdims=True) + EPSILON)
    out_ref[...] = jnp.where(valid, middle_ref[...] + down * r4 * g4_ref[...], 0.0).astype(BF)
    dy = jnp.where(valid, ct_ref[...].astype(F32), 0.0)
    dz = dy * down
    vrow_ref[0:1, :] = jnp.sum(dz * r4, axis=0, keepdims=True)
    inner = jnp.mean(dz * g4_ref[...], axis=-1, keepdims=True)
    dd = (r4 * g4_ref[...] * dy - down * (r4 * r4 * r4 * inner)).astype(BF)
    dd_ref[...] = dd
    vrow_ref[1:2, :] = jnp.sum(dd.astype(F32), axis=0, keepdims=True)
    send_ref[:, DD : DD + 512] = dd_ref[:, pl.ds(pl.multiple_of((1 - core) * 512, 512), 512)]
    keep_ref[:, 2048:2560] = dd_ref[:, pl.ds(pl.multiple_of(core * 512, 512), 512)]
    acc_ref[...] = jnp.zeros_like(acc_ref)
    for part in range(2):
        which = 1 - core if part == 0 else core
        for i in range(2048 // CHUNK):
            at = pl.ds(pl.multiple_of(which * 2048 + CHUNK * i, CHUNK), CHUNK)
            dact = dot_nt(dd, wdown_ref[at, :])
            dpre = (dact * slope_ref[:, at]).astype(BF)
            vup_ref[:, at] = jnp.sum(dpre.astype(F32), axis=0, keepdims=True)
            if part == 0:
                send_ref[:, DPRE + CHUNK * i : DPRE + CHUNK * (i + 1)] = dpre
            else:
                keep_ref[:, CHUNK * i : CHUNK * (i + 1)] = dpre
            acc_ref[...] += dot_nt(dpre, wup_ref[:, at])
    dm = acc_ref[...]
    middle = middle_ref[...]
    dz = dm * middle
    vrow_ref[2:3, :] = jnp.sum(dz * r3, axis=0, keepdims=True)
    inner = jnp.mean(dz * g3_ref[...], axis=-1, keepdims=True)
    dmid = dy + r3 * g3_ref[...] * dm - middle * (r3 * r3 * r3 * inner)
    dmid_ref[...] = dmid
    proj = proj_ref[...]
    dz = dmid * proj
    vrow_ref[3:4, :] = jnp.sum(dz * r2, axis=0, keepdims=True)
    inner = jnp.mean(dz * g2_ref[...], axis=-1, keepdims=True)
    dproj = (r2 * g2_ref[...] * dmid - proj * (r2 * r2 * r2 * inner)).astype(BF)
    dd_ref[...] = dproj
    send_ref[:, DPROJ : DPROJ + 512] = dd_ref[:, pl.ds(pl.multiple_of((1 - core) * 512, 512), 512)]
    keep_ref[:, 2560:3072] = dd_ref[:, pl.ds(pl.multiple_of(core * 512, 512), 512)]
    d_out = dot_nt(dproj, wo_ref[...]).astype(BF)
    for j in range(8):
        do_ref[j] = d_out[:, 128 * j : 128 * (j + 1)]


def mlp_call(*args):
    shape = jax.ShapeDtypeStruct
    return pl.pallas_call(
        mlp_kernel,
        in_specs=[SMEM] * 3 + [VMEM] * 3 + [HBM, HBM, VMEM, HBM] + [VMEM] * 4,
        out_specs=[VMEM] * 7,
        out_shape=[
            shape((128, 1024), BF), shape((128, 1024), F32), shape((8, 128, 128), BF), shape((128, SEND), BF),
            shape((128, 3072), BF), shape((1, 4096), F32), shape((4, 1024), F32),
        ],
        scratch_shapes=[
            pltpu.VMEM((128, 1024), F32), pltpu.VMEM((128, 1024), F32), pltpu.VMEM((128, 4096), F32),
            pltpu.VMEM((128, 1024), BF), pltpu.VMEM((128, 1024), F32),
            pltpu.VMEM((1024, 1024), BF), pltpu.VMEM((1024, 4096), BF), pltpu.VMEM((4096, 1024), BF),
            pltpu.SemaphoreType.DMA((2 * 4096 // CHUNK + 1,)),
        ],
        compiler_params=pltpu.CompilerParams(vmem_limit_bytes=60 * 2**20),
        cost_estimate=pl.CostEstimate(flops=4 * 128 * 9 * 2**20, bytes_accessed=20 * 2**20, transcendentals=2**19),
    )(*args)


def grad_parts(info_ref, relative, lefts, rights, outs, copies):
    b0, b1, b2 = info_ref[4], info_ref[2], info_ref[3]

    def left(at, n):
        return lefts[at : at + n, :]

    def cols(at, n):
        return rights[:, pl.ds(pl.multiple_of(at, 128), n)]

    eights = lambda g: [g[:, 128 * i : 128 * (i + 1)].reshape(128, 8, 128) for i in range(g.shape[1] // 128)]
    for k2 in range(2):
        block = 2 * (relative ^ b0) + k2
        rhs = jnp.concatenate([cols(u * 512 + block * 128, 128) for u in range(3)], axis=1)
        rows = eights(dot(left(M_AT, 1024), rhs))
        outs[0][k2 ^ b1] = jnp.concatenate(rows, axis=1).reshape(3072, 128).astype(BF)
    copies[0].start()
    rhs = cols(2048 + 256 * (relative ^ b1), 256)
    for half in range(2):
        g = dot(left(2048 * half, 2048), rhs)
        for k2 in range(2):
            part = g[:, 128 * k2 : 128 * (k2 + 1)].reshape(64, 32, 128)[:, 0:24]
            outs[1][k2 ^ b2, 1536 * half : 1536 * (half + 1), :] = part.reshape(1536, 128).astype(BF)
    copies[1].start()
    first = 256 * (relative ^ b2)
    g_up = eights(dot(left(M_AT, 1024), cols(3 * 512 + first, 256)))
    g_out = eights(dot(left(O_AT, 1024), cols(2560 + first, 256)))
    for half in range(2):
        g_down = dot(left(2048 * half, 2048), cols(2048 + first, 256))
        d = slice(64 * half, 64 * (half + 1))
        for k2 in range(2):
            tail = g_down[:, 128 * k2 : 128 * (k2 + 1)].reshape(64, 32, 128)[:, 24:32]
            rows = jnp.concatenate([g_up[k2][d], tail, g_out[k2][d]], axis=1)
            outs[2][k2 ^ b0, 1536 * half : 1536 * (half + 1), :] = rows.reshape(1536, 128).astype(BF)
    copies[2].start()


def turn(mine, theirs, lefts):
    for i in range(6144 // 512):
        at = slice(512 * i, 512 * (i + 1))
        lefts[at, 0:128] = mine[:, at].T
        lefts[at, 128:256] = theirs[:, at].T


def grads_kernel(relative, info_ref, mine_ref, keep_ref, theirs_ref, p_hbm, q_hbm, r_hbm, lefts, rights, p_ref, q_ref, r_ref, sems):
    turn(mine_ref, theirs_ref, lefts)
    rights[0:128, :] = keep_ref[...]
    rights[128:256, :] = theirs_ref[:, DPRE:SEND]
    copies = [
        pltpu.make_async_copy(ref, hbm, sems.at[i])
        for i, (ref, hbm) in enumerate(((p_ref, p_hbm), (q_ref, q_hbm), (r_ref, r_hbm)))
    ]
    grad_parts(info_ref, relative, lefts, rights, (p_ref, q_ref, r_ref), copies)
    for copy in copies:
        copy.wait()


PART_SHAPES = [jax.ShapeDtypeStruct((2, 128 * n, 128), BF) for n in PARTS]


def grads_call(relative, info, send, keep, got):
    return pl.pallas_call(
        functools.partial(grads_kernel, relative),
        in_specs=[SMEM, VMEM, VMEM, VMEM],
        out_specs=[HBM] * 3,
        out_shape=PART_SHAPES,
        scratch_shapes=[pltpu.VMEM((6144, 256), BF), pltpu.VMEM((256, 3072), BF)]
        + [pltpu.VMEM((2, 128 * n, 128), BF) for n in PARTS]
        + [pltpu.SemaphoreType.DMA((3,))],
        compiler_params=pltpu.CompilerParams(vmem_limit_bytes=60 * 2**20),
        cost_estimate=pl.CostEstimate(flops=1, bytes_accessed=1024, transcendentals=0),
    )(info, send, keep, got)


ROWS = 88


def add_kernel(*refs):
    for k, a, out in zip(refs[0:3], refs[3:6], refs[6:9]):
        out[...] = k[0] + a[0]


def add_call(kept, one):
    return pl.pallas_call(
        add_kernel,
        grid=(2,),
        in_specs=[pl.BlockSpec((1, 64 * n, 128), lambda j: (1, j, 0)) for n in PARTS] * 2,
        out_specs=[pl.BlockSpec((64 * n, 128), lambda j: (j, 0)) for n in PARTS],
        out_shape=[jax.ShapeDtypeStruct((128 * n, 128), BF) for n in PARTS],
        compiler_params=pltpu.CompilerParams(vmem_limit_bytes=60 * 2**20),
        cost_estimate=pl.CostEstimate(flops=1, bytes_accessed=1024, transcendentals=0),
    )(*kept, *one)


def pack_kernel(*refs):
    rows = []
    for k, a, b, n in zip(refs[0:3], refs[3:6], refs[6:9], PARTS):
        total = k[0].astype(F32) + a[0].astype(F32) + b[...].astype(F32)
        rows.append(total.reshape(64, n, 128))
    rows.append(refs[9][...].astype(F32) + refs[10][...].astype(F32))
    refs[11][...] = jnp.concatenate(rows, axis=1).astype(BF)


def pack_call(kept, one, two, qkv, qkv_two):
    half = [pl.BlockSpec((1, 64 * n, 128), lambda j: (0, j, 0)) for n in PARTS]
    tail = pl.BlockSpec((64, 16, 128), lambda j: (j, 0, 0))
    return pl.pallas_call(
        pack_kernel,
        grid=(2,),
        in_specs=half * 2 + [pl.BlockSpec((64 * n, 128), lambda j: (j, 0)) for n in PARTS] + [tail] * 2,
        out_specs=pl.BlockSpec((64, ROWS, 128), lambda j: (j, 0, 0)),
        out_shape=jax.ShapeDtypeStruct((128, ROWS, 128), BF),
        compiler_params=pltpu.CompilerParams(vmem_limit_bytes=60 * 2**20),
        cost_estimate=pl.CostEstimate(flops=1, bytes_accessed=1024, transcendentals=0),
    )(*kept, *one, *two, qkv, qkv_two)


def bits_of(s):
    return {n: (s >> i) & 1 for i, n in enumerate(("xh", "yl", "yh", "core", "xl", "zl", "zh"))}


def sum_kernel(got_ref, w_ref, g_ref, up_ref, down_ref, wo_ref, q_ref, k_ref, v_ref, gain_ref, *vec_refs):
    def total(keys, at, n):
        sums = {}
        for s in range(128):
            b = bits_of(s)
            k = tuple(b[name] for name in keys)
            v = got_ref[s].astype(F32)[at : at + n]
            sums[k] = sums[k] + v if k in sums else v
        return sums

    for (core, k1, k2), v in total(("core", "xl", "zl"), 0, 24).items():
        for u in range(3):
            at = core * 2048 + u * 512 + (2 * k1 + k2) * 128
            up_ref[:, at : at + 128] = v[8 * u : 8 * (u + 1)]
    for (core, k1, k2), v in total(("core", "zl", "yl"), 24, 24).items():
        at = core * 512 + (2 * k1 + k2) * 128
        down_ref[0:24, at : at + 128] = v
    for (core, k1, k2), v in total(("core", "yl", "xl"), 48, 24).items():
        at = (2 * k1 + k2) * 128
        up_ref[:, core * 2048 + 1536 + at : core * 2048 + 1536 + at + 128] = v[0:8]
        down_ref[24:32, core * 512 + at : core * 512 + at + 128] = v[8:16]
        wo_ref[:, core * 512 + at : core * 512 + at + 128] = v[16:24]
    weighted = jnp.zeros((8, 128), F32)
    vec = jnp.zeros((8, 128), F32)
    for (core, yh, yl, xh), v in total(("core", "yh", "yl", "xh"), 72, 16).items():
        b = 4 * yh + 2 * yl + xh
        at = slice(128 * b, 128 * (b + 1))
        for i, out in ((2, v_ref),) if core else ((0, q_ref), (1, k_ref)):
            part = v[8 * (i % 2) : 8 * (i % 2) + 8]
            out[:, at] = part
            weighted = weighted + part * w_ref[i, :, at]
        if core:
            vec = vec + v[8:16]
    gain_ref[...] = jnp.sum(weighted.T, axis=0, keepdims=True) / g_ref[...]
    at = 0
    for ref in vec_refs:
        n = ref.shape[1]
        ref[...] = vec[0:1, at : at + n]
        at += n


def sum_call(got, w_rows, gain_rows):
    shape = jax.ShapeDtypeStruct
    return pl.pallas_call(
        sum_kernel,
        in_specs=[VMEM] * 3,
        out_specs=[VMEM] * 12,
        out_shape=[shape((8, 4096), F32), shape((32, 1024), F32)]
        + [shape((8, 1024), F32)] * 4
        + [shape((1, n), F32) for n in (8, 32, 8, 8, 8, 8)],
        compiler_params=pltpu.CompilerParams(vmem_limit_bytes=16 * 2**20),
        cost_estimate=pl.CostEstimate(flops=10**7, bytes_accessed=3 * 2**20, transcendentals=0),
    )(got, w_rows, gain_rows)


def qkv_grads_kernel(info_ref, a0_ref, a1_ref, a2_ref, a3_ref, d_ref, vec_ref, keep_ref, send_ref):
    y, xh = info_ref[1] // 2, info_ref[1] % 2
    g = jnp.zeros((512, 384), F32)
    for back, ref in enumerate((a0_ref, a1_ref, a2_ref, a3_ref)):
        source = ((y + 4 - back) % 4) * 2
        d = jnp.concatenate([d_ref[source + xh], d_ref[source + 1 - xh]], axis=0)
        g = g + dot_tn(ref[...].reshape(256, 512), d)
    parts = [g[:, 128 * i : 128 * (i + 1)].reshape(64, 8, 128) for i in range(3)]
    first = lax.broadcasted_iota(jnp.int32, (64, 8, 128), 1) == 0
    parts.append(jnp.where(first, vec_ref[...].reshape(64, 1, 128), 0.0))
    one, two = (jnp.concatenate(parts[i : i + 2], axis=1) for i in (0, 2))
    mine = info_ref[0] == 0
    keep_ref[...] = jnp.where(mine, one, two).astype(BF)
    send_ref[...] = jnp.where(mine, two, one).astype(BF)


def qkv_grads_call(info, pairs, d_heads, vec):
    return pl.pallas_call(
        qkv_grads_kernel,
        grid=(2,),
        in_specs=[SMEM]
        + [pl.BlockSpec((2, 128, 512), lambda j: (0, 0, j))] * 4
        + [pl.BlockSpec((8, 128, 384), lambda j: (0, 0, 0)), pl.BlockSpec((64, 128), lambda j: (j, 0))],
        out_specs=[pl.BlockSpec((64, 16, 128), lambda j: (j, 0, 0))] * 2,
        out_shape=[jax.ShapeDtypeStruct((128, 16, 128), BF)] * 2,
        compiler_params=pltpu.CompilerParams(vmem_limit_bytes=63 * 2**20),
        cost_estimate=pl.CostEstimate(flops=1, bytes_accessed=1024, transcendentals=0),
    )(info, *pairs, d_heads, vec)


def input_kernel(d_ref, wq_ref, wk_ref, wv_ref, x_ref, g_ref, dmid_ref, out_ref):
    step = pl.program_id(0)
    acc = jnp.where(step == 0, 0.0, out_ref[...])
    for i, w_ref in enumerate((wq_ref, wk_ref, wv_ref)):
        d = jnp.concatenate([d_ref[j, :, 128 * i : 128 * (i + 1)] for j in range(2)], axis=1)
        acc = acc + dot_nt(d, w_ref[...])
    out_ref[...] = acc

    @pl.when(step == 3)
    def _():
        x = x_ref[...].astype(F32)
        r = lax.rsqrt(jnp.mean(x * x, axis=-1, keepdims=True) + EPSILON)
        dz = out_ref[...] * g_ref[...]
        inner = jnp.mean(dz * x, axis=-1, keepdims=True)
        out_ref[...] = dmid_ref[...] + r * dz - x * (r * r * r * inner)


def input_call(d_mine, wq, wk, wv, x, gain, dmid):
    whole = lambda shape: pl.BlockSpec(shape, lambda j: (0,) * len(shape))
    col = pl.BlockSpec((1024, 256), lambda j: (0, j))
    return pl.pallas_call(
        input_kernel,
        grid=(4,),
        in_specs=[pl.BlockSpec((2, 128, 384), lambda j: (j, 0, 0)), col, col, col, whole((128, 1024)), whole((1, 1024)), whole((128, 1024))],
        out_specs=whole((128, 1024)),
        out_shape=jax.ShapeDtypeStruct((128, 1024), F32),
        compiler_params=pltpu.CompilerParams(vmem_limit_bytes=16 * 2**20),
        cost_estimate=pl.CostEstimate(flops=2 * 128 * 1024 * 3072, bytes_accessed=7 * 2**20, transcendentals=0),
    )(d_mine, wq, wk, wv, x, gain, dmid)


def local(
    tokens, lengths, order, w_query, w_key, w_value, w_out, w_up, b_up, w_down, b_down,
    gain_attn_in, gain_attn_out, gain_mlp_in, gain_mlp_out, cotangent,
):
    z, xl, core, y, xh = (lax.axis_index(a) for a in ALL)
    my_blk = y * 2 + xh
    me = ((z * 2 + xl) * 2 + core) * 8 + my_blk
    info = jnp.stack([core, my_blk, z % 2, y % 2, xl]).astype(jnp.int32)
    row = lambda v: v.reshape(1, -1)
    order = order.T
    tie = lax.optimization_barrier

    qkv, attn_low = qkv_call(info, order, lengths, tokens, row(gain_attn_in), w_query, w_key, w_value)
    across = lax.ppermute(attn_low, ALL, ACROSS)
    qkv_heads = lax.all_to_all(qkv, BLK, 0, 0, tiled=True)

    late_lengths, across = tie((lengths, across))
    lengths_row = late_lengths[0]
    group_pos = jnp.arange(1024, dtype=jnp.int32)
    start = jnp.zeros((1024,), jnp.int32)
    end = jnp.int32(0)
    for e in range(6):
        end = end + lengths_row[e]
        start = jnp.where(group_pos >= end, end, start)
    cos_all, sin_all = rotary_tables(group_pos - start)

    qkv_heads, cos_all, sin_all, pair = tie((qkv_heads, cos_all, sin_all, jnp.stack([attn_low, across])))

    pairs = [pair] + [lax.ppermute(pair, ALL, to) for to in ALONG]
    out_heads, pos_qkv, lse = attend_call(order, lengths, qkv_heads)
    out_mine = lax.all_to_all(out_heads, BLK, 0, 0, tiled=True)
    out_mine, pairs[2] = tie((out_mine, pairs[2]))
    output, d_middle, d_out, send, keep, v_up, v_row = mlp_call(
        info, order, lengths, out_mine, tokens, cotangent, w_out, w_up, row(b_up), w_down, row(b_down),
        row(gain_attn_out), row(gain_mlp_in), row(gain_mlp_out),
    )
    send, keep, d_out, pairs = tie((send, keep, d_out, pairs))
    d_out_heads = lax.all_to_all(d_out, BLK, 0, 0, tiled=True)
    got = lax.ppermute(send, ALL, SWAP_CORES)
    sent = grads_call(1, info, send, keep, got)
    one = [lax.ppermute(p, ALL, to) for p, to in zip(sent, STEPS[0])]
    keep, _ = tie((keep, sent))
    kept = grads_call(0, info, send, keep, got)
    lse, kept = tie((lse, kept))
    d_heads = attend_back_call(order, lengths, pos_qkv, lse, cos_all, sin_all, d_out_heads)
    d_mine = lax.all_to_all(d_heads, BLK, 0, 0, tiled=True)
    v_up, v_row, _ = tie((v_up, v_row, d_heads))
    vectors = jnp.concatenate(
        [v_up.reshape(128, 32)] + [v_row[i].reshape(128, 8) for i in (1, 3, 2, 0)] + [jnp.zeros((128, 64), F32)], axis=1
    )
    one, vectors = tie((one, vectors))
    added = add_call(kept, one)
    two = [lax.ppermute(p, ALL, to) for p, to in zip(added, STEPS[1])]
    d_grads, d_mine, _ = tie((d_heads, d_mine, added))
    qkv_keep, qkv_send = qkv_grads_call(info, pairs, d_grads, vectors)
    packed = pack_call(kept, one, two, qkv_keep, lax.ppermute(qkv_send, ALL, SWAP_CORES))
    got_all = lax.all_to_all(packed, ALL, 0, 0, tiled=True)

    grad_tokens = input_call(d_mine, w_query, w_key, w_value, tokens, row(gain_attn_in), d_middle)
    my_rows = lambda w: lax.dynamic_slice_in_dim(w, me * 8, 8, 0).astype(F32)
    w_rows = jnp.stack([my_rows(w) for w in (w_query, w_key, w_value)])
    gain_rows = lax.dynamic_slice_in_dim(gain_attn_in, me * 8, 8, 0).reshape(1, 8)
    grad_w_up, grad_w_down, grad_w_out, grad_w_query, grad_w_key, grad_w_value, *vec = sum_call(got_all, w_rows, gain_rows)
    grad_gain_attn_in, grad_b_up, grad_b_down, grad_gain_attn_out, grad_gain_mlp_in, grad_gain_mlp_out = (
        v.reshape(-1) for v in vec
    )
    return (
        output, grad_tokens, grad_w_query, grad_w_key, grad_w_value, grad_w_out, grad_w_up, grad_b_up, grad_w_down,
        grad_b_down, grad_gain_attn_in, grad_gain_attn_out, grad_gain_mlp_in, grad_gain_mlp_out,
    )


def solution(mesh):
    split = Mesh(np.asarray(mesh.devices).reshape(4, 2, 2, 4, 2), ALL)
    every = P(ALL, None)
    flat = P(ALL)
    return jax.shard_map(
        local,
        mesh=split,
        in_specs=(every, P(("z", "xl", "core"), None)) + (P(),) * 13 + (every,),
        out_specs=(every,) * 7 + (flat, every) + (flat,) * 5,
        check_vma=False,
    )
```

```python
import functools
import math

import jax
import jax.numpy as jnp
import numpy as np
from jax import lax
from jax.experimental import pallas as pl
from jax.experimental.pallas import tpu as pltpu
from jax.sharding import Mesh
from jax.sharding import PartitionSpec as P

HEADS = 16
EPSILON = 1e-05
NEGATIVE = -1e30
ALL = ("z", "xl", "core", "y", "xh")
BLK = ("y", "xh")
BF = jnp.bfloat16
F32 = jnp.float32
TILES = ((0, 0, 256), (256, 0, 512), (512, 0, 768), (768, 512, 1024))


SMEM = pl.BlockSpec(memory_space=pltpu.SMEM)
VMEM = pl.BlockSpec(memory_space=pltpu.VMEM)
HBM = pl.BlockSpec(memory_space=pltpu.HBM)


def device_index(z, x, c, y):
    return (((z % 4) * 2 + (x % 4) % 2) * 2 + c) * 8 + (y % 4) * 2 + (x % 4) // 2


def pairs_of(f):
    return [
        (device_index(z, x, c, y), device_index(*f(z, x, c, y)))
        for z in range(4)
        for x in range(4)
        for c in range(2)
        for y in range(4)
    ]


def up(v):
    return v ^ 1


def down_pair(v):
    return ((v + 1) ^ 1) - 1


def flip(axis, by_core):
    way = (up, down_pair)

    def there(z, x, c, y):
        move = way[by_core[c]]
        return (
            move(z) if axis == "z" else z,
            move(x) if axis == "x" else x,
            c,
            move(y) if axis == "y" else y,
        )

    return pairs_of(there)


ACROSS = pairs_of(lambda z, x, c, y: (z, x + 2, c, y))
ALONG = [pairs_of(lambda z, x, c, y, by=by: (z, x, c, y + by)) for by in (1, 2, 3)]
SWAP_CORES = pairs_of(lambda z, x, c, y: (z, x, 1 - c, y))
PARTS = (24, 24, 24)
STEPS = (
    (flip("x", (0, 1)), flip("z", (0, 1)), flip("y", (0, 1))),
    (flip("z", (0, 1)), flip("y", (0, 1)), flip("x", (0, 1))),
)


def half_swap(x):
    n = x.shape[1]
    lane = lax.broadcasted_iota(jnp.int32, x.shape, 1) % 64
    return jnp.where(lane < 32, pltpu.roll(x, n - 32, 1), pltpu.roll(x, 32, 1))


def rotary_tables(relative):
    freqs = jnp.exp(jnp.arange(32, dtype=F32) * (-math.log(10000.0) / 32))
    angles = relative.astype(F32)[:, None] * freqs[None, :]
    c, s = jnp.cos(angles), jnp.sin(angles)
    return jnp.concatenate([c, c, c, c], axis=1), jnp.concatenate([-s, s, -s, s], axis=1)


def dot(a, b):
    return jnp.dot(a, b, preferred_element_type=F32)


def dot_nt(a, b):
    return lax.dot_general(a, b, (((1,), (1,)), ((), ())), preferred_element_type=F32)


def dot_tn(a, b):
    return lax.dot_general(a, b, (((0,), (0,)), ((), ())), preferred_element_type=F32)


def column_positions(info_ref, order_ref, len_ref):
    row = lax.broadcasted_iota(jnp.int32, (128, 1), 0)
    one, two = order_ref[0, info_ref[1]], order_ref[1, info_ref[1]]
    pos = jnp.where(row < 64, one * 64 + row, two * 64 + row - 64)
    start = jnp.zeros((128, 1), jnp.int32)
    end = jnp.int32(0)
    for e in range(6):
        end = end + len_ref[0, e]
        start = jnp.where(pos >= end, end, start)
    return pos, start, end


def qkv_kernel(info_ref, order_ref, len_ref, x_ref, g_ref, wq_hbm, wk_hbm, wv_hbm, out_ref, a_ref, wq, wk, wv, sems):
    copies = [
        pltpu.make_async_copy(hbm.at[:, 512 * h : 512 * (h + 1)], w.at[:, 512 * h : 512 * (h + 1)], sems.at[2 * i + h])
        for i, (hbm, w) in enumerate(((wq_hbm, wq), (wk_hbm, wk), (wv_hbm, wv)))
        for h in range(2)
    ]
    for copy in copies:
        copy.start()
    x = x_ref[...].astype(F32)
    factor = lax.rsqrt(jnp.mean(x * x, axis=-1, keepdims=True) + EPSILON)
    a = (x * factor * g_ref[...]).astype(BF)
    a_ref[...] = a
    pos, start, _ = column_positions(info_ref, order_ref, len_ref)
    lane = lax.broadcasted_iota(jnp.int32, (1, 128), 1)
    freqs = jnp.exp((lane % 32).astype(F32) * (-math.log(10000.0) / 32))
    angles = (pos - start).astype(F32) * freqs
    cos = jnp.cos(angles)
    sine = jnp.sin(angles)
    sin = jnp.where(lane % 64 < 32, -sine, sine)
    cos = jnp.concatenate([cos] * 4, axis=1)
    sin = jnp.concatenate([sin] * 4, axis=1)
    for i, w in enumerate((wq, wk, wv)):
        for h in range(2):
            copies[2 * i + h].wait()
            y = dot(a, w[:, 512 * h : 512 * (h + 1)])
            if i < 2:
                y = y * cos + half_swap(y) * sin
            y = y.astype(BF)
            for j in range(4):
                out_ref[4 * h + j, :, 128 * i : 128 * (i + 1)] = y[:, 128 * j : 128 * (j + 1)]


def qkv_call(info, order, lengths, x, gain, wq, wk, wv):
    return pl.pallas_call(
        qkv_kernel,
        in_specs=[SMEM, SMEM, SMEM, VMEM, VMEM, HBM, HBM, HBM],
        out_specs=[VMEM, VMEM],
        out_shape=[jax.ShapeDtypeStruct((8, 128, 384), BF), jax.ShapeDtypeStruct((128, 1024), BF)],
        scratch_shapes=[pltpu.VMEM((1024, 1024), BF)] * 3 + [pltpu.SemaphoreType.DMA((6,))],
        compiler_params=pltpu.CompilerParams(vmem_limit_bytes=60 * 2**20),
        cost_estimate=pl.CostEstimate(flops=2 * 128 * 1024 * 3072, bytes_accessed=7 * 2**20, transcendentals=0),
    )(info, order, lengths, x, gain, wq, wk, wv)


def allowed_mask(len_ref, q0, k0, k1):
    qpos = q0 + lax.broadcasted_iota(jnp.int32, (1, 256), 1)
    start = jnp.zeros((1, 256), jnp.int32)
    end = jnp.int32(0)
    for e in range(6):
        end = end + len_ref[0, e]
        start = jnp.where(qpos >= end, end, start)
    kpos = k0 + lax.broadcasted_iota(jnp.int32, (k1 - k0, 256), 0)
    return (kpos >= start) & (kpos <= qpos)


def attend_kernel(order_ref, len_ref, qkv_ref, out_ref, pos_ref, lse_ref, o_ref):
    for b in range(8):
        for j in range(2):
            at = pl.ds(pl.multiple_of(order_ref[j, b] * 64, 64), 64)
            pos_ref[at, :] = qkv_ref[b, 64 * j : 64 * (j + 1), :]
    first = lax.broadcasted_iota(jnp.int32, (1, 128), 1) < 64
    v_t = pos_ref[:, 256:384].T
    for q0, k0, k1 in TILES:
        q = pos_ref[q0 : q0 + 256, 0:128].astype(F32) * 0.125
        k = pos_ref[k0:k1, 128:256]
        mask = allowed_mask(len_ref, q0, k0, k1)
        outs = []
        for h in range(2):
            q_h = jnp.where(first if h == 0 else ~first, q, 0.0).astype(BF)
            s = jnp.where(mask, dot_nt(k, q_h), NEGATIVE)
            top = jnp.max(s, axis=0, keepdims=True)
            p = jnp.exp(s - top)
            total = jnp.sum(p, axis=0, keepdims=True)
            lse_ref[h : h + 1, q0 : q0 + 256] = top + jnp.log(total)
            p = (p * (1.0 / total)).astype(BF)
            outs.append(dot(v_t[64 * h : 64 * (h + 1), k0:k1], p))
        o_ref[q0 : q0 + 256, :] = jnp.concatenate(outs, axis=0).T.astype(BF)
    for b in range(8):
        for j in range(2):
            at = pl.ds(pl.multiple_of(order_ref[j, b] * 64, 64), 64)
            out_ref[b, 64 * j : 64 * (j + 1), :] = o_ref[at, :]


def attend_call(order, lengths, qkv):
    return pl.pallas_call(
        attend_kernel,
        in_specs=[SMEM, SMEM, VMEM],
        out_specs=[VMEM] * 3,
        out_shape=[
            jax.ShapeDtypeStruct((8, 128, 128), BF),
            jax.ShapeDtypeStruct((1024, 384), BF),
            jax.ShapeDtypeStruct((2, 1024), F32),
        ],
        scratch_shapes=[pltpu.VMEM((1024, 128), BF)],
        compiler_params=pltpu.CompilerParams(vmem_limit_bytes=24 * 2**20),
        cost_estimate=pl.CostEstimate(flops=2 * 10**9, bytes_accessed=3 * 2**20, transcendentals=2 * 10**6),
    )(order, lengths, qkv)


def attend_back_kernel(order_ref, len_ref, pos_ref, lse_ref, cos_ref, sin_ref, do_ref, out_ref, d_ref, dk_ref, dv_ref, dq_ref):
    for b in range(8):
        for j in range(2):
            at = pl.ds(pl.multiple_of(order_ref[j, b] * 64, 64), 64)
            d_ref[at, 0:128] = do_ref[b, 64 * j : 64 * (j + 1), :]
    first = lax.broadcasted_iota(jnp.int32, (1, 128), 1) < 64
    k_t = pos_ref[:, 128:256].T
    dk_ref[...] = jnp.zeros_like(dk_ref)
    dv_ref[...] = jnp.zeros_like(dv_ref)
    for q0, k0, k1 in TILES:
        q = pos_ref[q0 : q0 + 256, 0:128].astype(F32) * 0.125
        do = d_ref[q0 : q0 + 256, 0:128]
        k = pos_ref[k0:k1, 128:256]
        v = pos_ref[k0:k1, 256:384]
        mask = allowed_mask(len_ref, q0, k0, k1)
        outs = []
        for h in range(2):
            pick = first if h == 0 else ~first
            q_h = jnp.where(pick, q, 0.0).astype(BF)
            do_h = jnp.where(pick, do.astype(F32), 0.0).astype(BF)
            s = jnp.where(mask, dot_nt(k, q_h), NEGATIVE)
            p = jnp.exp(s - lse_ref[h : h + 1, q0 : q0 + 256])
            dp = dot_nt(v, do_h)
            delta = jnp.sum(p * dp, axis=0, keepdims=True)
            ds = (p * (dp - delta)).astype(BF)
            dv_ref[k0:k1, :] += dot(p.astype(BF), do_h)
            dk_ref[k0:k1, :] += dot(ds, q_h)
            outs.append(dot(k_t[64 * h : 64 * (h + 1), k0:k1], ds))
        dq_ref[q0 : q0 + 256, :] = jnp.concatenate(outs, axis=0).T * 0.125
    cos, sin = cos_ref[...], sin_ref[...]
    dq, dk = dq_ref[...], dk_ref[...]
    d_ref[:, 0:128] = (dq * cos - half_swap(dq) * sin).astype(BF)
    d_ref[:, 128:256] = (dk * cos - half_swap(dk) * sin).astype(BF)
    d_ref[:, 256:384] = dv_ref[...].astype(BF)
    for b in range(8):
        for j in range(2):
            at = pl.ds(pl.multiple_of(order_ref[j, b] * 64, 64), 64)
            out_ref[b, 64 * j : 64 * (j + 1), :] = d_ref[at, :]


def attend_back_call(order, lengths, pos, lse, cos, sin, d_out):
    return pl.pallas_call(
        attend_back_kernel,
        in_specs=[SMEM, SMEM, VMEM, VMEM, VMEM, VMEM, VMEM],
        out_specs=VMEM,
        out_shape=jax.ShapeDtypeStruct((8, 128, 384), BF),
        scratch_shapes=[
            pltpu.VMEM((1024, 384), BF),
            pltpu.VMEM((1024, 128), F32),
            pltpu.VMEM((1024, 128), F32),
            pltpu.VMEM((1024, 128), F32),
        ],
        compiler_params=pltpu.CompilerParams(vmem_limit_bytes=32 * 2**20),
        cost_estimate=pl.CostEstimate(flops=20000000000, bytes_accessed=1024, transcendentals=0),
    )(order, lengths, pos, lse, cos, sin, d_out)


ACT, M_AT, O_AT, DPRE, DD, DPROJ, SEND = 0, 4096, 5120, 6144, 8192, 8704, 9216
CHUNK = 1024


def mlp_kernel(info_ref, order_ref, len_ref, o_ref, x_ref, ct_ref, wo_hbm, wup_hbm, bup_ref, wdown_hbm, bdown_ref,
               g2_ref, g3_ref, g4_ref,
               out_ref, dmid_ref, do_ref, send_ref, keep_ref, vup_ref, vrow_ref,
               proj_ref, middle_ref, slope_ref, dd_ref, acc_ref, wo_ref, wup_ref, wdown_ref, sems):
    core = info_ref[0]
    count = 4096 // CHUNK
    copy_out = pltpu.make_async_copy(wo_hbm, wo_ref, sems.at[2 * count])
    copy_out.start()
    copies = []
    for i in range(count):
        at = slice(CHUNK * i, CHUNK * (i + 1))
        copies.append((
            pltpu.make_async_copy(wup_hbm.at[:, at], wup_ref.at[:, at], sems.at[2 * i]),
            pltpu.make_async_copy(wdown_hbm.at[at, :], wdown_ref.at[at, :], sems.at[2 * i + 1]),
        ))
        copies[-1][0].start()
        copies[-1][1].start()
    pos, _, end = column_positions(info_ref, order_ref, len_ref)
    valid = pos < end
    o = jnp.concatenate([o_ref[j] for j in range(8)], axis=1)
    send_ref[:, O_AT : O_AT + 1024] = o
    copy_out.wait()
    proj = dot(o, wo_ref[...])
    proj_ref[...] = proj
    r2 = lax.rsqrt(jnp.mean(proj * proj, axis=-1, keepdims=True) + EPSILON)
    middle = x_ref[...].astype(F32) + proj * r2 * g2_ref[...]
    middle_ref[...] = middle
    r3 = lax.rsqrt(jnp.mean(middle * middle, axis=-1, keepdims=True) + EPSILON)
    m = (middle * r3 * g3_ref[...]).astype(BF)
    send_ref[:, M_AT : M_AT + 1024] = m
    acc_ref[...] = jnp.zeros_like(acc_ref)
    root = math.sqrt(2.0 / math.pi)
    for i in range(4096 // CHUNK):
        at = slice(CHUNK * i, CHUNK * (i + 1))
        copies[i][0].wait()
        pre = dot(m, wup_ref[:, at]) + bup_ref[:, at]
        square = pre * pre
        t = jnp.tanh(root * (pre + 0.044715 * (square * pre)))
        half = 0.5 * (1.0 + t)
        act = (pre * half).astype(BF)
        slope_ref[:, at] = half + 0.5 * pre * (1.0 - t * t) * (root + (3.0 * 0.044715 * root) * square)
        send_ref[:, at] = act
        copies[i][1].wait()
        acc_ref[...] += dot(act, wdown_ref[at, :])
    down = acc_ref[...] + bdown_ref[...]
    r4 = lax.rsqrt(jnp.mean(down * down, axis=-1, keepdims=True) + EPSILON)
    out_ref[...] = jnp.where(valid, middle_ref[...] + down * r4 * g4_ref[...], 0.0).astype(BF)
    dy = jnp.where(valid, ct_ref[...].astype(F32), 0.0)
    dz = dy * down
    vrow_ref[0:1, :] = jnp.sum(dz * r4, axis=0, keepdims=True)
    inner = jnp.mean(dz * g4_ref[...], axis=-1, keepdims=True)
    dd = (r4 * g4_ref[...] * dy - down * (r4 * r4 * r4 * inner)).astype(BF)
    dd_ref[...] = dd
    vrow_ref[1:2, :] = jnp.sum(dd.astype(F32), axis=0, keepdims=True)
    send_ref[:, DD : DD + 512] = dd_ref[:, pl.ds(pl.multiple_of((1 - core) * 512, 512), 512)]
    keep_ref[:, 2048:2560] = dd_ref[:, pl.ds(pl.multiple_of(core * 512, 512), 512)]
    acc_ref[...] = jnp.zeros_like(acc_ref)
    for part in range(2):
        which = 1 - core if part == 0 else core
        for i in range(2048 // CHUNK):
            at = pl.ds(pl.multiple_of(which * 2048 + CHUNK * i, CHUNK), CHUNK)
            dact = dot_nt(dd, wdown_ref[at, :])
            dpre = (dact * slope_ref[:, at]).astype(BF)
            vup_ref[:, at] = jnp.sum(dpre.astype(F32), axis=0, keepdims=True)
            if part == 0:
                send_ref[:, DPRE + CHUNK * i : DPRE + CHUNK * (i + 1)] = dpre
            else:
                keep_ref[:, CHUNK * i : CHUNK * (i + 1)] = dpre
            acc_ref[...] += dot_nt(dpre, wup_ref[:, at])
    dm = acc_ref[...]
    middle = middle_ref[...]
    dz = dm * middle
    vrow_ref[2:3, :] = jnp.sum(dz * r3, axis=0, keepdims=True)
    inner = jnp.mean(dz * g3_ref[...], axis=-1, keepdims=True)
    dmid = dy + r3 * g3_ref[...] * dm - middle * (r3 * r3 * r3 * inner)
    dmid_ref[...] = dmid
    proj = proj_ref[...]
    dz = dmid * proj
    vrow_ref[3:4, :] = jnp.sum(dz * r2, axis=0, keepdims=True)
    inner = jnp.mean(dz * g2_ref[...], axis=-1, keepdims=True)
    dproj = (r2 * g2_ref[...] * dmid - proj * (r2 * r2 * r2 * inner)).astype(BF)
    dd_ref[...] = dproj
    send_ref[:, DPROJ : DPROJ + 512] = dd_ref[:, pl.ds(pl.multiple_of((1 - core) * 512, 512), 512)]
    keep_ref[:, 2560:3072] = dd_ref[:, pl.ds(pl.multiple_of(core * 512, 512), 512)]
    d_out = dot_nt(dproj, wo_ref[...]).astype(BF)
    for j in range(8):
        do_ref[j] = d_out[:, 128 * j : 128 * (j + 1)]


def mlp_call(*args):
    shape = jax.ShapeDtypeStruct
    return pl.pallas_call(
        mlp_kernel,
        in_specs=[SMEM] * 3 + [VMEM] * 3 + [HBM, HBM, VMEM, HBM] + [VMEM] * 4,
        out_specs=[VMEM] * 7,
        out_shape=[
            shape((128, 1024), BF), shape((128, 1024), F32), shape((8, 128, 128), BF), shape((128, SEND), BF),
            shape((128, 3072), BF), shape((1, 4096), F32), shape((4, 1024), F32),
        ],
        scratch_shapes=[
            pltpu.VMEM((128, 1024), F32), pltpu.VMEM((128, 1024), F32), pltpu.VMEM((128, 4096), F32),
            pltpu.VMEM((128, 1024), BF), pltpu.VMEM((128, 1024), F32),
            pltpu.VMEM((1024, 1024), BF), pltpu.VMEM((1024, 4096), BF), pltpu.VMEM((4096, 1024), BF),
            pltpu.SemaphoreType.DMA((2 * 4096 // CHUNK + 1,)),
        ],
        compiler_params=pltpu.CompilerParams(vmem_limit_bytes=60 * 2**20),
        cost_estimate=pl.CostEstimate(flops=4 * 128 * 9 * 2**20, bytes_accessed=20 * 2**20, transcendentals=2**19),
    )(*args)


def grad_parts(info_ref, relative, lefts, rights, outs, copies):
    b0, b1, b2 = info_ref[4], info_ref[2], info_ref[3]

    def left(at, n):
        return lefts[at : at + n, :]

    def cols(at, n):
        return rights[:, pl.ds(pl.multiple_of(at, 128), n)]

    eights = lambda g: [g[:, 128 * i : 128 * (i + 1)].reshape(128, 8, 128) for i in range(g.shape[1] // 128)]
    for k2 in range(2):
        block = 2 * (relative ^ b0) + k2
        rhs = jnp.concatenate([cols(u * 512 + block * 128, 128) for u in range(3)], axis=1)
        rows = eights(dot(left(M_AT, 1024), rhs))
        outs[0][k2 ^ b1] = jnp.concatenate(rows, axis=1).reshape(3072, 128).astype(BF)
    copies[0].start()
    rhs = cols(2048 + 256 * (relative ^ b1), 256)
    for half in range(2):
        g = dot(left(2048 * half, 2048), rhs)
        for k2 in range(2):
            part = g[:, 128 * k2 : 128 * (k2 + 1)].reshape(64, 32, 128)[:, 0:24]
            outs[1][k2 ^ b2, 1536 * half : 1536 * (half + 1), :] = part.reshape(1536, 128).astype(BF)
    copies[1].start()
    first = 256 * (relative ^ b2)
    g_up = eights(dot(left(M_AT, 1024), cols(3 * 512 + first, 256)))
    g_out = eights(dot(left(O_AT, 1024), cols(2560 + first, 256)))
    for half in range(2):
        g_down = dot(left(2048 * half, 2048), cols(2048 + first, 256))
        d = slice(64 * half, 64 * (half + 1))
        for k2 in range(2):
            tail = g_down[:, 128 * k2 : 128 * (k2 + 1)].reshape(64, 32, 128)[:, 24:32]
            rows = jnp.concatenate([g_up[k2][d], tail, g_out[k2][d]], axis=1)
            outs[2][k2 ^ b0, 1536 * half : 1536 * (half + 1), :] = rows.reshape(1536, 128).astype(BF)
    copies[2].start()


def turn(mine, theirs, lefts):
    for i in range(6144 // 512):
        at = slice(512 * i, 512 * (i + 1))
        lefts[at, 0:128] = mine[:, at].T
        lefts[at, 128:256] = theirs[:, at].T


def grads_kernel(relative, info_ref, mine_ref, keep_ref, theirs_ref, p_hbm, q_hbm, r_hbm, lefts, rights, p_ref, q_ref, r_ref, sems):
    turn(mine_ref, theirs_ref, lefts)
    rights[0:128, :] = keep_ref[...]
    rights[128:256, :] = theirs_ref[:, DPRE:SEND]
    copies = [
        pltpu.make_async_copy(ref, hbm, sems.at[i])
        for i, (ref, hbm) in enumerate(((p_ref, p_hbm), (q_ref, q_hbm), (r_ref, r_hbm)))
    ]
    grad_parts(info_ref, relative, lefts, rights, (p_ref, q_ref, r_ref), copies)
    for copy in copies:
        copy.wait()


PART_SHAPES = [jax.ShapeDtypeStruct((2, 128 * n, 128), BF) for n in PARTS]


def grads_call(relative, info, send, keep, got):
    return pl.pallas_call(
        functools.partial(grads_kernel, relative),
        in_specs=[SMEM, VMEM, VMEM, VMEM],
        out_specs=[HBM] * 3,
        out_shape=PART_SHAPES,
        scratch_shapes=[pltpu.VMEM((6144, 256), BF), pltpu.VMEM((256, 3072), BF)]
        + [pltpu.VMEM((2, 128 * n, 128), BF) for n in PARTS]
        + [pltpu.SemaphoreType.DMA((3,))],
        compiler_params=pltpu.CompilerParams(vmem_limit_bytes=60 * 2**20),
        cost_estimate=pl.CostEstimate(flops=1, bytes_accessed=1024, transcendentals=0),
    )(info, send, keep, got)


ROWS = 88


def add_kernel(*refs):
    for k, a, out in zip(refs[0:3], refs[3:6], refs[6:9]):
        out[...] = k[0] + a[0]


def add_call(kept, one):
    return pl.pallas_call(
        add_kernel,
        grid=(2,),
        in_specs=[pl.BlockSpec((1, 64 * n, 128), lambda j: (1, j, 0)) for n in PARTS] * 2,
        out_specs=[pl.BlockSpec((64 * n, 128), lambda j: (j, 0)) for n in PARTS],
        out_shape=[jax.ShapeDtypeStruct((128 * n, 128), BF) for n in PARTS],
        compiler_params=pltpu.CompilerParams(vmem_limit_bytes=60 * 2**20),
        cost_estimate=pl.CostEstimate(flops=1, bytes_accessed=1024, transcendentals=0),
    )(*kept, *one)


def pack_kernel(*refs):
    rows = []
    for k, a, b, n in zip(refs[0:3], refs[3:6], refs[6:9], PARTS):
        total = k[0].astype(F32) + a[0].astype(F32) + b[...].astype(F32)
        rows.append(total.reshape(64, n, 128))
    rows.append(refs[9][...].astype(F32) + refs[10][...].astype(F32))
    refs[11][...] = jnp.concatenate(rows, axis=1).astype(BF)


def pack_call(kept, one, two, qkv, qkv_two):
    half = [pl.BlockSpec((1, 64 * n, 128), lambda j: (0, j, 0)) for n in PARTS]
    tail = pl.BlockSpec((64, 16, 128), lambda j: (j, 0, 0))
    return pl.pallas_call(
        pack_kernel,
        grid=(2,),
        in_specs=half * 2 + [pl.BlockSpec((64 * n, 128), lambda j: (j, 0)) for n in PARTS] + [tail] * 2,
        out_specs=pl.BlockSpec((64, ROWS, 128), lambda j: (j, 0, 0)),
        out_shape=jax.ShapeDtypeStruct((128, ROWS, 128), BF),
        compiler_params=pltpu.CompilerParams(vmem_limit_bytes=60 * 2**20),
        cost_estimate=pl.CostEstimate(flops=1, bytes_accessed=1024, transcendentals=0),
    )(*kept, *one, *two, qkv, qkv_two)


def bits_of(s):
    return {n: (s >> i) & 1 for i, n in enumerate(("xh", "yl", "yh", "core", "xl", "zl", "zh"))}


def sum_kernel(got_ref, w_ref, g_ref, up_ref, down_ref, wo_ref, q_ref, k_ref, v_ref, gain_ref, *vec_refs):
    def total(keys, at, n):
        sums = {}
        for s in range(128):
            b = bits_of(s)
            k = tuple(b[name] for name in keys)
            v = got_ref[s].astype(F32)[at : at + n]
            sums[k] = sums[k] + v if k in sums else v
        return sums

    for (core, k1, k2), v in total(("core", "xl", "zl"), 0, 24).items():
        for u in range(3):
            at = core * 2048 + u * 512 + (2 * k1 + k2) * 128
            up_ref[:, at : at + 128] = v[8 * u : 8 * (u + 1)]
    for (core, k1, k2), v in total(("core", "zl", "yl"), 24, 24).items():
        at = core * 512 + (2 * k1 + k2) * 128
        down_ref[0:24, at : at + 128] = v
    for (core, k1, k2), v in total(("core", "yl", "xl"), 48, 24).items():
        at = (2 * k1 + k2) * 128
        up_ref[:, core * 2048 + 1536 + at : core * 2048 + 1536 + at + 128] = v[0:8]
        down_ref[24:32, core * 512 + at : core * 512 + at + 128] = v[8:16]
        wo_ref[:, core * 512 + at : core * 512 + at + 128] = v[16:24]
    weighted = jnp.zeros((8, 128), F32)
    vec = jnp.zeros((8, 128), F32)
    for (core, yh, yl, xh), v in total(("core", "yh", "yl", "xh"), 72, 16).items():
        b = 4 * yh + 2 * yl + xh
        at = slice(128 * b, 128 * (b + 1))
        for i, out in ((2, v_ref),) if core else ((0, q_ref), (1, k_ref)):
            part = v[8 * (i % 2) : 8 * (i % 2) + 8]
            out[:, at] = part
            weighted = weighted + part * w_ref[i, :, at]
        if core:
            vec = vec + v[8:16]
    gain_ref[...] = jnp.sum(weighted.T, axis=0, keepdims=True) / g_ref[...]
    at = 0
    for ref in vec_refs:
        n = ref.shape[1]
        ref[...] = vec[0:1, at : at + n]
        at += n


def sum_call(got, w_rows, gain_rows):
    shape = jax.ShapeDtypeStruct
    return pl.pallas_call(
        sum_kernel,
        in_specs=[VMEM] * 3,
        out_specs=[VMEM] * 12,
        out_shape=[shape((8, 4096), F32), shape((32, 1024), F32)]
        + [shape((8, 1024), F32)] * 4
        + [shape((1, n), F32) for n in (8, 32, 8, 8, 8, 8)],
        compiler_params=pltpu.CompilerParams(vmem_limit_bytes=16 * 2**20),
        cost_estimate=pl.CostEstimate(flops=10**7, bytes_accessed=3 * 2**20, transcendentals=0),
    )(got, w_rows, gain_rows)


def qkv_grads_kernel(info_ref, a0_ref, a1_ref, a2_ref, a3_ref, d_ref, vec_ref, keep_ref, send_ref):
    y, xh = info_ref[1] // 2, info_ref[1] % 2
    g = jnp.zeros((512, 384), F32)
    for back, ref in enumerate((a0_ref, a1_ref, a2_ref, a3_ref)):
        source = ((y + 4 - back) % 4) * 2
        d = jnp.concatenate([d_ref[source + xh], d_ref[source + 1 - xh]], axis=0)
        g = g + dot_tn(ref[...].reshape(256, 512), d)
    parts = [g[:, 128 * i : 128 * (i + 1)].reshape(64, 8, 128) for i in range(3)]
    first = lax.broadcasted_iota(jnp.int32, (64, 8, 128), 1) == 0
    parts.append(jnp.where(first, vec_ref[...].reshape(64, 1, 128), 0.0))
    one, two = (jnp.concatenate(parts[i : i + 2], axis=1) for i in (0, 2))
    mine = info_ref[0] == 0
    keep_ref[...] = jnp.where(mine, one, two).astype(BF)
    send_ref[...] = jnp.where(mine, two, one).astype(BF)


def qkv_grads_call(info, pairs, d_heads, vec):
    return pl.pallas_call(
        qkv_grads_kernel,
        grid=(2,),
        in_specs=[SMEM]
        + [pl.BlockSpec((2, 128, 512), lambda j: (0, 0, j))] * 4
        + [pl.BlockSpec((8, 128, 384), lambda j: (0, 0, 0)), pl.BlockSpec((64, 128), lambda j: (j, 0))],
        out_specs=[pl.BlockSpec((64, 16, 128), lambda j: (j, 0, 0))] * 2,
        out_shape=[jax.ShapeDtypeStruct((128, 16, 128), BF)] * 2,
        compiler_params=pltpu.CompilerParams(vmem_limit_bytes=63 * 2**20),
        cost_estimate=pl.CostEstimate(flops=1, bytes_accessed=1024, transcendentals=0),
    )(info, *pairs, d_heads, vec)


def input_kernel(d_ref, wq_ref, wk_ref, wv_ref, x_ref, g_ref, dmid_ref, out_ref):
    step = pl.program_id(0)
    acc = jnp.where(step == 0, 0.0, out_ref[...])
    for i, w_ref in enumerate((wq_ref, wk_ref, wv_ref)):
        d = jnp.concatenate([d_ref[j, :, 128 * i : 128 * (i + 1)] for j in range(2)], axis=1)
        acc = acc + dot_nt(d, w_ref[...])
    out_ref[...] = acc

    @pl.when(step == 3)
    def _():
        x = x_ref[...].astype(F32)
        r = lax.rsqrt(jnp.mean(x * x, axis=-1, keepdims=True) + EPSILON)
        dz = out_ref[...] * g_ref[...]
        inner = jnp.mean(dz * x, axis=-1, keepdims=True)
        out_ref[...] = dmid_ref[...] + r * dz - x * (r * r * r * inner)


def input_call(d_mine, wq, wk, wv, x, gain, dmid):
    whole = lambda shape: pl.BlockSpec(shape, lambda j: (0,) * len(shape))
    col = pl.BlockSpec((1024, 256), lambda j: (0, j))
    return pl.pallas_call(
        input_kernel,
        grid=(4,),
        in_specs=[pl.BlockSpec((2, 128, 384), lambda j: (j, 0, 0)), col, col, col, whole((128, 1024)), whole((1, 1024)), whole((128, 1024))],
        out_specs=whole((128, 1024)),
        out_shape=jax.ShapeDtypeStruct((128, 1024), F32),
        compiler_params=pltpu.CompilerParams(vmem_limit_bytes=16 * 2**20),
        cost_estimate=pl.CostEstimate(flops=2 * 128 * 1024 * 3072, bytes_accessed=7 * 2**20, transcendentals=0),
    )(d_mine, wq, wk, wv, x, gain, dmid)


def local(
    tokens, lengths, order, w_query, w_key, w_value, w_out, w_up, b_up, w_down, b_down,
    gain_attn_in, gain_attn_out, gain_mlp_in, gain_mlp_out, cotangent,
):
    z, xl, core, y, xh = (lax.axis_index(a) for a in ALL)
    my_blk = y * 2 + xh
    me = ((z * 2 + xl) * 2 + core) * 8 + my_blk
    info = jnp.stack([core, my_blk, z % 2, y % 2, xl]).astype(jnp.int32)
    row = lambda v: v.reshape(1, -1)
    order = order.T
    tie = lax.optimization_barrier

    qkv, attn_low = qkv_call(info, order, lengths, tokens, row(gain_attn_in), w_query, w_key, w_value)
    across = lax.ppermute(attn_low, ALL, ACROSS)
    qkv_heads = lax.all_to_all(qkv, BLK, 0, 0, tiled=True)

    late_lengths, across = tie((lengths, across))
    lengths_row = late_lengths[0]
    group_pos = jnp.arange(1024, dtype=jnp.int32)
    start = jnp.zeros((1024,), jnp.int32)
    end = jnp.int32(0)
    for e in range(6):
        end = end + lengths_row[e]
        start = jnp.where(group_pos >= end, end, start)
    cos_all, sin_all = rotary_tables(group_pos - start)

    qkv_heads, cos_all, sin_all, pair = tie((qkv_heads, cos_all, sin_all, jnp.stack([attn_low, across])))

    pairs = [pair] + [lax.ppermute(pair, ALL, to) for to in ALONG]
    out_heads, pos_qkv, lse = attend_call(order, lengths, qkv_heads)
    out_mine = lax.all_to_all(out_heads, BLK, 0, 0, tiled=True)
    out_mine, pairs[2] = tie((out_mine, pairs[2]))
    output, d_middle, d_out, send, keep, v_up, v_row = mlp_call(
        info, order, lengths, out_mine, tokens, cotangent, w_out, w_up, row(b_up), w_down, row(b_down),
        row(gain_attn_out), row(gain_mlp_in), row(gain_mlp_out),
    )
    send, keep, d_out, pairs = tie((send, keep, d_out, pairs))
    d_out_heads = lax.all_to_all(d_out, BLK, 0, 0, tiled=True)
    got = lax.ppermute(send, ALL, SWAP_CORES)
    sent = grads_call(1, info, send, keep, got)
    one = [lax.ppermute(p, ALL, to) for p, to in zip(sent, STEPS[0])]
    keep, _ = tie((keep, sent))
    kept = grads_call(0, info, send, keep, got)
    lse, kept = tie((lse, kept))
    d_heads = attend_back_call(order, lengths, pos_qkv, lse, cos_all, sin_all, d_out_heads)
    d_mine = lax.all_to_all(d_heads, BLK, 0, 0, tiled=True)
    added = add_call(kept, one)
    two = [lax.ppermute(p, ALL, to) for p, to in zip(added, STEPS[1])]
    v_up, v_row, _ = tie((v_up, v_row, added))
    vectors = jnp.concatenate(
        [v_up.reshape(128, 32)] + [v_row[i].reshape(128, 8) for i in (1, 3, 2, 0)] + [jnp.zeros((128, 64), F32)], axis=1
    )
    d_grads, _ = tie((d_heads, added))
    qkv_keep, qkv_send = qkv_grads_call(info, pairs, d_grads, vectors)
    qkv_send, d_mine = tie((qkv_send, d_mine))
    packed = pack_call(kept, one, two, qkv_keep, lax.ppermute(qkv_send, ALL, SWAP_CORES))
    got_all = lax.all_to_all(packed, ALL, 0, 0, tiled=True)

    grad_tokens = input_call(d_mine, w_query, w_key, w_value, tokens, row(gain_attn_in), d_middle)
    my_rows = lambda w: lax.dynamic_slice_in_dim(w, me * 8, 8, 0).astype(F32)
    w_rows = jnp.stack([my_rows(w) for w in (w_query, w_key, w_value)])
    gain_rows = lax.dynamic_slice_in_dim(gain_attn_in, me * 8, 8, 0).reshape(1, 8)
    grad_w_up, grad_w_down, grad_w_out, grad_w_query, grad_w_key, grad_w_value, *vec = sum_call(got_all, w_rows, gain_rows)
    grad_gain_attn_in, grad_b_up, grad_b_down, grad_gain_attn_out, grad_gain_mlp_in, grad_gain_mlp_out = (
        v.reshape(-1) for v in vec
    )
    return (
        output, grad_tokens, grad_w_query, grad_w_key, grad_w_value, grad_w_out, grad_w_up, grad_b_up, grad_w_down,
        grad_b_down, grad_gain_attn_in, grad_gain_attn_out, grad_gain_mlp_in, grad_gain_mlp_out,
    )


def solution(mesh):
    split = Mesh(np.asarray(mesh.devices).reshape(4, 2, 2, 4, 2), ALL)
    every = P(ALL, None)
    flat = P(ALL)
    return jax.shard_map(
        local,
        mesh=split,
        in_specs=(every, P(("z", "xl", "core"), None)) + (P(),) * 13 + (every,),
        out_specs=(every,) * 7 + (flat, every) + (flat,) * 5,
        check_vma=False,
    )
```

```python
import functools
import math

import jax
import jax.numpy as jnp
import numpy as np
from jax import lax
from jax.experimental import pallas as pl
from jax.experimental.pallas import tpu as pltpu
from jax.sharding import Mesh
from jax.sharding import PartitionSpec as P

HEADS = 16
EPSILON = 1e-05
NEGATIVE = -1e30
ALL = ("z", "xl", "core", "y", "xh")
BLK = ("y", "xh")
BF = jnp.bfloat16
F32 = jnp.float32
TILES = ((0, 0, 256), (256, 0, 512), (512, 0, 768), (768, 512, 1024))


SMEM = pl.BlockSpec(memory_space=pltpu.SMEM)
VMEM = pl.BlockSpec(memory_space=pltpu.VMEM)
HBM = pl.BlockSpec(memory_space=pltpu.HBM)


def device_index(z, x, c, y):
    return (((z % 4) * 2 + (x % 4) % 2) * 2 + c) * 8 + (y % 4) * 2 + (x % 4) // 2


def pairs_of(f):
    return [
        (device_index(z, x, c, y), device_index(*f(z, x, c, y)))
        for z in range(4)
        for x in range(4)
        for c in range(2)
        for y in range(4)
    ]


def up(v):
    return v ^ 1


def down_pair(v):
    return ((v + 1) ^ 1) - 1


def flip(axis, by_core):
    way = (up, down_pair)

    def there(z, x, c, y):
        move = way[by_core[c]]
        return (
            move(z) if axis == "z" else z,
            move(x) if axis == "x" else x,
            c,
            move(y) if axis == "y" else y,
        )

    return pairs_of(there)


ACROSS = pairs_of(lambda z, x, c, y: (z, x + 2, c, y))
ALONG = [pairs_of(lambda z, x, c, y, by=by: (z, x, c, y + by)) for by in (1, 2, 3)]
SWAP_CORES = pairs_of(lambda z, x, c, y: (z, x, 1 - c, y))
PARTS = (24, 24, 24)
STEPS = (
    (flip("x", (0, 1)), flip("z", (0, 1)), flip("y", (0, 1))),
    (flip("z", (0, 1)), flip("y", (0, 1)), flip("x", (0, 1))),
)


def half_swap(x):
    n = x.shape[1]
    lane = lax.broadcasted_iota(jnp.int32, x.shape, 1) % 64
    return jnp.where(lane < 32, pltpu.roll(x, n - 32, 1), pltpu.roll(x, 32, 1))


def rotary_tables(relative):
    freqs = jnp.exp(jnp.arange(32, dtype=F32) * (-math.log(10000.0) / 32))
    angles = relative.astype(F32)[:, None] * freqs[None, :]
    c, s = jnp.cos(angles), jnp.sin(angles)
    return jnp.concatenate([c, c, c, c], axis=1), jnp.concatenate([-s, s, -s, s], axis=1)


def dot(a, b):
    return jnp.dot(a, b, preferred_element_type=F32)


def dot_nt(a, b):
    return lax.dot_general(a, b, (((1,), (1,)), ((), ())), preferred_element_type=F32)


def dot_tn(a, b):
    return lax.dot_general(a, b, (((0,), (0,)), ((), ())), preferred_element_type=F32)


def column_positions(info_ref, order_ref, len_ref):
    row = lax.broadcasted_iota(jnp.int32, (128, 1), 0)
    one, two = order_ref[0, info_ref[1]], order_ref[1, info_ref[1]]
    pos = jnp.where(row < 64, one * 64 + row, two * 64 + row - 64)
    start = jnp.zeros((128, 1), jnp.int32)
    end = jnp.int32(0)
    for e in range(6):
        end = end + len_ref[0, e]
        start = jnp.where(pos >= end, end, start)
    return pos, start, end


def qkv_kernel(info_ref, order_ref, len_ref, x_ref, g_ref, wq_hbm, wk_hbm, wv_hbm, out_ref, a_ref, wq, wk, wv, sems):
    copies = [
        pltpu.make_async_copy(hbm.at[:, 512 * h : 512 * (h + 1)], w.at[:, 512 * h : 512 * (h + 1)], sems.at[2 * i + h])
        for i, (hbm, w) in enumerate(((wq_hbm, wq), (wk_hbm, wk), (wv_hbm, wv)))
        for h in range(2)
    ]
    for copy in copies:
        copy.start()
    x = x_ref[...].astype(F32)
    factor = lax.rsqrt(jnp.mean(x * x, axis=-1, keepdims=True) + EPSILON)
    a = (x * factor * g_ref[...]).astype(BF)
    a_ref[...] = a
    pos, start, _ = column_positions(info_ref, order_ref, len_ref)
    lane = lax.broadcasted_iota(jnp.int32, (1, 128), 1)
    freqs = jnp.exp((lane % 32).astype(F32) * (-math.log(10000.0) / 32))
    angles = (pos - start).astype(F32) * freqs
    cos = jnp.cos(angles)
    sine = jnp.sin(angles)
    sin = jnp.where(lane % 64 < 32, -sine, sine)
    cos = jnp.concatenate([cos] * 4, axis=1)
    sin = jnp.concatenate([sin] * 4, axis=1)
    for i, w in enumerate((wq, wk, wv)):
        for h in range(2):
            copies[2 * i + h].wait()
            y = dot(a, w[:, 512 * h : 512 * (h + 1)])
            if i < 2:
                y = y * cos + half_swap(y) * sin
            y = y.astype(BF)
            for j in range(4):
                out_ref[4 * h + j, :, 128 * i : 128 * (i + 1)] = y[:, 128 * j : 128 * (j + 1)]


def qkv_call(info, order, lengths, x, gain, wq, wk, wv):
    return pl.pallas_call(
        qkv_kernel,
        in_specs=[SMEM, SMEM, SMEM, VMEM, VMEM, HBM, HBM, HBM],
        out_specs=[VMEM, VMEM],
        out_shape=[jax.ShapeDtypeStruct((8, 128, 384), BF), jax.ShapeDtypeStruct((128, 1024), BF)],
        scratch_shapes=[pltpu.VMEM((1024, 1024), BF)] * 3 + [pltpu.SemaphoreType.DMA((6,))],
        compiler_params=pltpu.CompilerParams(vmem_limit_bytes=60 * 2**20),
        cost_estimate=pl.CostEstimate(flops=2 * 128 * 1024 * 3072, bytes_accessed=7 * 2**20, transcendentals=0),
    )(info, order, lengths, x, gain, wq, wk, wv)


def allowed_mask(len_ref, q0, k0, k1):
    qpos = q0 + lax.broadcasted_iota(jnp.int32, (1, 256), 1)
    start = jnp.zeros((1, 256), jnp.int32)
    end = jnp.int32(0)
    for e in range(6):
        end = end + len_ref[0, e]
        start = jnp.where(qpos >= end, end, start)
    kpos = k0 + lax.broadcasted_iota(jnp.int32, (k1 - k0, 256), 0)
    return (kpos >= start) & (kpos <= qpos)


def attend_kernel(order_ref, len_ref, qkv_ref, out_ref, pos_ref, lse_ref, o_ref):
    for b in range(8):
        for j in range(2):
            at = pl.ds(pl.multiple_of(order_ref[j, b] * 64, 64), 64)
            pos_ref[at, :] = qkv_ref[b, 64 * j : 64 * (j + 1), :]
    first = lax.broadcasted_iota(jnp.int32, (1, 128), 1) < 64
    v_t = pos_ref[:, 256:384].T
    for q0, k0, k1 in TILES:
        q = pos_ref[q0 : q0 + 256, 0:128].astype(F32) * 0.125
        k = pos_ref[k0:k1, 128:256]
        mask = allowed_mask(len_ref, q0, k0, k1)
        outs = []
        for h in range(2):
            q_h = jnp.where(first if h == 0 else ~first, q, 0.0).astype(BF)
            s = jnp.where(mask, dot_nt(k, q_h), NEGATIVE)
            top = jnp.max(s, axis=0, keepdims=True)
            p = jnp.exp(s - top)
            total = jnp.sum(p, axis=0, keepdims=True)
            lse_ref[h : h + 1, q0 : q0 + 256] = top + jnp.log(total)
            p = (p * (1.0 / total)).astype(BF)
            outs.append(dot(v_t[64 * h : 64 * (h + 1), k0:k1], p))
        o_ref[q0 : q0 + 256, :] = jnp.concatenate(outs, axis=0).T.astype(BF)
    for b in range(8):
        for j in range(2):
            at = pl.ds(pl.multiple_of(order_ref[j, b] * 64, 64), 64)
            out_ref[b, 64 * j : 64 * (j + 1), :] = o_ref[at, :]


def attend_call(order, lengths, qkv):
    return pl.pallas_call(
        attend_kernel,
        in_specs=[SMEM, SMEM, VMEM],
        out_specs=[VMEM] * 3,
        out_shape=[
            jax.ShapeDtypeStruct((8, 128, 128), BF),
            jax.ShapeDtypeStruct((1024, 384), BF),
            jax.ShapeDtypeStruct((2, 1024), F32),
        ],
        scratch_shapes=[pltpu.VMEM((1024, 128), BF)],
        compiler_params=pltpu.CompilerParams(vmem_limit_bytes=24 * 2**20),
        cost_estimate=pl.CostEstimate(flops=2 * 10**9, bytes_accessed=3 * 2**20, transcendentals=2 * 10**6),
    )(order, lengths, qkv)


def attend_back_kernel(order_ref, len_ref, pos_ref, lse_ref, cos_ref, sin_ref, do_ref, out_ref, d_ref, dk_ref, dv_ref, dq_ref):
    for b in range(8):
        for j in range(2):
            at = pl.ds(pl.multiple_of(order_ref[j, b] * 64, 64), 64)
            d_ref[at, 0:128] = do_ref[b, 64 * j : 64 * (j + 1), :]
    first = lax.broadcasted_iota(jnp.int32, (1, 128), 1) < 64
    k_t = pos_ref[:, 128:256].T
    dk_ref[...] = jnp.zeros_like(dk_ref)
    dv_ref[...] = jnp.zeros_like(dv_ref)
    for q0, k0, k1 in TILES:
        q = pos_ref[q0 : q0 + 256, 0:128].astype(F32) * 0.125
        do = d_ref[q0 : q0 + 256, 0:128]
        k = pos_ref[k0:k1, 128:256]
        v = pos_ref[k0:k1, 256:384]
        mask = allowed_mask(len_ref, q0, k0, k1)
        outs = []
        for h in range(2):
            pick = first if h == 0 else ~first
            q_h = jnp.where(pick, q, 0.0).astype(BF)
            do_h = jnp.where(pick, do.astype(F32), 0.0).astype(BF)
            s = jnp.where(mask, dot_nt(k, q_h), NEGATIVE)
            p = jnp.exp(s - lse_ref[h : h + 1, q0 : q0 + 256])
            dp = dot_nt(v, do_h)
            delta = jnp.sum(p * dp, axis=0, keepdims=True)
            ds = (p * (dp - delta)).astype(BF)
            dv_ref[k0:k1, :] += dot(p.astype(BF), do_h)
            dk_ref[k0:k1, :] += dot(ds, q_h)
            outs.append(dot(k_t[64 * h : 64 * (h + 1), k0:k1], ds))
        dq_ref[q0 : q0 + 256, :] = jnp.concatenate(outs, axis=0).T * 0.125
    cos, sin = cos_ref[...], sin_ref[...]
    dq, dk = dq_ref[...], dk_ref[...]
    d_ref[:, 0:128] = (dq * cos - half_swap(dq) * sin).astype(BF)
    d_ref[:, 128:256] = (dk * cos - half_swap(dk) * sin).astype(BF)
    d_ref[:, 256:384] = dv_ref[...].astype(BF)
    for b in range(8):
        for j in range(2):
            at = pl.ds(pl.multiple_of(order_ref[j, b] * 64, 64), 64)
            out_ref[b, 64 * j : 64 * (j + 1), :] = d_ref[at, :]


def attend_back_call(order, lengths, pos, lse, cos, sin, d_out):
    return pl.pallas_call(
        attend_back_kernel,
        in_specs=[SMEM, SMEM, VMEM, VMEM, VMEM, VMEM, VMEM],
        out_specs=VMEM,
        out_shape=jax.ShapeDtypeStruct((8, 128, 384), BF),
        scratch_shapes=[
            pltpu.VMEM((1024, 384), BF),
            pltpu.VMEM((1024, 128), F32),
            pltpu.VMEM((1024, 128), F32),
            pltpu.VMEM((1024, 128), F32),
        ],
        compiler_params=pltpu.CompilerParams(vmem_limit_bytes=32 * 2**20),
        cost_estimate=pl.CostEstimate(flops=20000000000, bytes_accessed=1024, transcendentals=0),
    )(order, lengths, pos, lse, cos, sin, d_out)


ACT, M_AT, O_AT, DPRE, DD, DPROJ, SEND = 0, 4096, 5120, 6144, 8192, 8704, 9216
CHUNK = 1024


def mlp_kernel(info_ref, order_ref, len_ref, o_ref, x_ref, ct_ref, wo_hbm, wup_hbm, bup_ref, wdown_hbm, bdown_ref,
               g2_ref, g3_ref, g4_ref,
               out_ref, dmid_ref, do_ref, send_ref, keep_ref, vup_ref, vrow_ref,
               proj_ref, middle_ref, slope_ref, dd_ref, acc_ref, wo_ref, wup_ref, wdown_ref, sems):
    core = info_ref[0]
    count = 4096 // CHUNK
    copy_out = pltpu.make_async_copy(wo_hbm, wo_ref, sems.at[2 * count])
    copy_out.start()
    copies = []
    for i in range(count):
        at = slice(CHUNK * i, CHUNK * (i + 1))
        copies.append((
            pltpu.make_async_copy(wup_hbm.at[:, at], wup_ref.at[:, at], sems.at[2 * i]),
            pltpu.make_async_copy(wdown_hbm.at[at, :], wdown_ref.at[at, :], sems.at[2 * i + 1]),
        ))
        copies[-1][0].start()
        copies[-1][1].start()
    pos, _, end = column_positions(info_ref, order_ref, len_ref)
    valid = pos < end
    o = jnp.concatenate([o_ref[j] for j in range(8)], axis=1)
    send_ref[:, O_AT : O_AT + 1024] = o
    copy_out.wait()
    proj = dot(o, wo_ref[...])
    proj_ref[...] = proj
    r2 = lax.rsqrt(jnp.mean(proj * proj, axis=-1, keepdims=True) + EPSILON)
    middle = x_ref[...].astype(F32) + proj * r2 * g2_ref[...]
    middle_ref[...] = middle
    r3 = lax.rsqrt(jnp.mean(middle * middle, axis=-1, keepdims=True) + EPSILON)
    m = (middle * r3 * g3_ref[...]).astype(BF)
    send_ref[:, M_AT : M_AT + 1024] = m
    acc_ref[...] = jnp.zeros_like(acc_ref)
    root = math.sqrt(2.0 / math.pi)
    for i in range(4096 // CHUNK):
        at = slice(CHUNK * i, CHUNK * (i + 1))
        copies[i][0].wait()
        pre = dot(m, wup_ref[:, at]) + bup_ref[:, at]
        square = pre * pre
        t = jnp.tanh(root * (pre + 0.044715 * (square * pre)))
        half = 0.5 * (1.0 + t)
        act = (pre * half).astype(BF)
        slope_ref[:, at] = half + 0.5 * pre * (1.0 - t * t) * (root + (3.0 * 0.044715 * root) * square)
        send_ref[:, at] = act
        copies[i][1].wait()
        acc_ref[...] += dot(act, wdown_ref[at, :])
    down = acc_ref[...] + bdown_ref[...]
    r4 = lax.rsqrt(jnp.mean(down * down, axis=-1, keepdims=True) + EPSILON)
    out_ref[...] = jnp.where(valid, middle_ref[...] + down * r4 * g4_ref[...], 0.0).astype(BF)
    dy = jnp.where(valid, ct_ref[...].astype(F32), 0.0)
    dz = dy * down
    vrow_ref[0:1, :] = jnp.sum(dz * r4, axis=0, keepdims=True)
    inner = jnp.mean(dz * g4_ref[...], axis=-1, keepdims=True)
    dd = (r4 * g4_ref[...] * dy - down * (r4 * r4 * r4 * inner)).astype(BF)
    dd_ref[...] = dd
    vrow_ref[1:2, :] = jnp.sum(dd.astype(F32), axis=0, keepdims=True)
    send_ref[:, DD : DD + 512] = dd_ref[:, pl.ds(pl.multiple_of((1 - core) * 512, 512), 512)]
    keep_ref[:, 2048:2560] = dd_ref[:, pl.ds(pl.multiple_of(core * 512, 512), 512)]
    acc_ref[...] = jnp.zeros_like(acc_ref)
    for part in range(2):
        which = 1 - core if part == 0 else core
        for i in range(2048 // CHUNK):
            at = pl.ds(pl.multiple_of(which * 2048 + CHUNK * i, CHUNK), CHUNK)
            dact = dot_nt(dd, wdown_ref[at, :])
            dpre = (dact * slope_ref[:, at]).astype(BF)
            vup_ref[:, at] = jnp.sum(dpre.astype(F32), axis=0, keepdims=True)
            if part == 0:
                send_ref[:, DPRE + CHUNK * i : DPRE + CHUNK * (i + 1)] = dpre
            else:
                keep_ref[:, CHUNK * i : CHUNK * (i + 1)] = dpre
            acc_ref[...] += dot_nt(dpre, wup_ref[:, at])
    dm = acc_ref[...]
    middle = middle_ref[...]
    dz = dm * middle
    vrow_ref[2:3, :] = jnp.sum(dz * r3, axis=0, keepdims=True)
    inner = jnp.mean(dz * g3_ref[...], axis=-1, keepdims=True)
    dmid = dy + r3 * g3_ref[...] * dm - middle * (r3 * r3 * r3 * inner)
    dmid_ref[...] = dmid
    proj = proj_ref[...]
    dz = dmid * proj
    vrow_ref[3:4, :] = jnp.sum(dz * r2, axis=0, keepdims=True)
    inner = jnp.mean(dz * g2_ref[...], axis=-1, keepdims=True)
    dproj = (r2 * g2_ref[...] * dmid - proj * (r2 * r2 * r2 * inner)).astype(BF)
    dd_ref[...] = dproj
    send_ref[:, DPROJ : DPROJ + 512] = dd_ref[:, pl.ds(pl.multiple_of((1 - core) * 512, 512), 512)]
    keep_ref[:, 2560:3072] = dd_ref[:, pl.ds(pl.multiple_of(core * 512, 512), 512)]
    d_out = dot_nt(dproj, wo_ref[...]).astype(BF)
    for j in range(8):
        do_ref[j] = d_out[:, 128 * j : 128 * (j + 1)]


def mlp_call(*args):
    shape = jax.ShapeDtypeStruct
    return pl.pallas_call(
        mlp_kernel,
        in_specs=[SMEM] * 3 + [VMEM] * 3 + [HBM, HBM, VMEM, HBM] + [VMEM] * 4,
        out_specs=[VMEM] * 7,
        out_shape=[
            shape((128, 1024), BF), shape((128, 1024), F32), shape((8, 128, 128), BF), shape((128, SEND), BF),
            shape((128, 3072), BF), shape((1, 4096), F32), shape((4, 1024), F32),
        ],
        scratch_shapes=[
            pltpu.VMEM((128, 1024), F32), pltpu.VMEM((128, 1024), F32), pltpu.VMEM((128, 4096), F32),
            pltpu.VMEM((128, 1024), BF), pltpu.VMEM((128, 1024), F32),
            pltpu.VMEM((1024, 1024), BF), pltpu.VMEM((1024, 4096), BF), pltpu.VMEM((4096, 1024), BF),
            pltpu.SemaphoreType.DMA((2 * 4096 // CHUNK + 1,)),
        ],
        compiler_params=pltpu.CompilerParams(vmem_limit_bytes=60 * 2**20),
        cost_estimate=pl.CostEstimate(flops=4 * 128 * 9 * 2**20, bytes_accessed=20 * 2**20, transcendentals=2**19),
    )(*args)


def grad_parts(info_ref, relative, lefts, rights, outs, copies):
    b0, b1, b2 = info_ref[4], info_ref[2], info_ref[3]

    def left(at, n):
        return lefts[at : at + n, :]

    def cols(at, n):
        return rights[:, pl.ds(pl.multiple_of(at, 128), n)]

    eights = lambda g: [g[:, 128 * i : 128 * (i + 1)].reshape(128, 8, 128) for i in range(g.shape[1] // 128)]
    for k2 in range(2):
        block = 2 * (relative ^ b0) + k2
        rhs = jnp.concatenate([cols(u * 512 + block * 128, 128) for u in range(3)], axis=1)
        rows = eights(dot(left(M_AT, 1024), rhs))
        outs[0][k2 ^ b1] = jnp.concatenate(rows, axis=1).reshape(3072, 128).astype(BF)
    copies[0].start()
    rhs = cols(2048 + 256 * (relative ^ b1), 256)
    for half in range(2):
        g = dot(left(2048 * half, 2048), rhs)
        for k2 in range(2):
            part = g[:, 128 * k2 : 128 * (k2 + 1)].reshape(64, 32, 128)[:, 0:24]
            outs[1][k2 ^ b2, 1536 * half : 1536 * (half + 1), :] = part.reshape(1536, 128).astype(BF)
    copies[1].start()
    first = 256 * (relative ^ b2)
    g_up = eights(dot(left(M_AT, 1024), cols(3 * 512 + first, 256)))
    g_out = eights(dot(left(O_AT, 1024), cols(2560 + first, 256)))
    for half in range(2):
        g_down = dot(left(2048 * half, 2048), cols(2048 + first, 256))
        d = slice(64 * half, 64 * (half + 1))
        for k2 in range(2):
            tail = g_down[:, 128 * k2 : 128 * (k2 + 1)].reshape(64, 32, 128)[:, 24:32]
            rows = jnp.concatenate([g_up[k2][d], tail, g_out[k2][d]], axis=1)
            outs[2][k2 ^ b0, 1536 * half : 1536 * (half + 1), :] = rows.reshape(1536, 128).astype(BF)
    copies[2].start()


def turn(mine, theirs, lefts):
    for i in range(6144 // 512):
        at = slice(512 * i, 512 * (i + 1))
        lefts[at, 0:128] = mine[:, at].T
        lefts[at, 128:256] = theirs[:, at].T


def grads_kernel(relative, info_ref, mine_ref, keep_ref, theirs_ref, p_hbm, q_hbm, r_hbm, lefts, rights, p_ref, q_ref, r_ref, sems):
    turn(mine_ref, theirs_ref, lefts)
    rights[0:128, :] = keep_ref[...]
    rights[128:256, :] = theirs_ref[:, DPRE:SEND]
    copies = [
        pltpu.make_async_copy(ref, hbm, sems.at[i])
        for i, (ref, hbm) in enumerate(((p_ref, p_hbm), (q_ref, q_hbm), (r_ref, r_hbm)))
    ]
    grad_parts(info_ref, relative, lefts, rights, (p_ref, q_ref, r_ref), copies)
    for copy in copies:
        copy.wait()


PART_SHAPES = [jax.ShapeDtypeStruct((2, 128 * n, 128), BF) for n in PARTS]


def grads_call(relative, info, send, keep, got):
    return pl.pallas_call(
        functools.partial(grads_kernel, relative),
        in_specs=[SMEM, VMEM, VMEM, VMEM],
        out_specs=[HBM] * 3,
        out_shape=PART_SHAPES,
        scratch_shapes=[pltpu.VMEM((6144, 256), BF), pltpu.VMEM((256, 3072), BF)]
        + [pltpu.VMEM((2, 128 * n, 128), BF) for n in PARTS]
        + [pltpu.SemaphoreType.DMA((3,))],
        compiler_params=pltpu.CompilerParams(vmem_limit_bytes=60 * 2**20),
        cost_estimate=pl.CostEstimate(flops=1, bytes_accessed=1024, transcendentals=0),
    )(info, send, keep, got)


ROWS = 88


def add_kernel(*refs):
    for k, a, out in zip(refs[0:3], refs[3:6], refs[6:9]):
        out[...] = k[0] + a[0]


def add_call(kept, one):
    return pl.pallas_call(
        add_kernel,
        grid=(2,),
        in_specs=[pl.BlockSpec((1, 64 * n, 128), lambda j: (1, j, 0)) for n in PARTS] * 2,
        out_specs=[pl.BlockSpec((64 * n, 128), lambda j: (j, 0)) for n in PARTS],
        out_shape=[jax.ShapeDtypeStruct((128 * n, 128), BF) for n in PARTS],
        compiler_params=pltpu.CompilerParams(vmem_limit_bytes=60 * 2**20),
        cost_estimate=pl.CostEstimate(flops=1, bytes_accessed=1024, transcendentals=0),
    )(*kept, *one)


def early_kernel(*refs):
    rows = []
    for k, a, n in zip(refs[0:3], refs[3:6], PARTS):
        rows.append((k[0].astype(F32) + a[0].astype(F32)).reshape(64, n, 128))
    rows.append(refs[6][...].astype(F32))
    refs[7][...] = jnp.concatenate(rows, axis=1).astype(BF)


def early_call(kept, one, qkv):
    half = [pl.BlockSpec((1, 64 * n, 128), lambda j: (0, j, 0)) for n in PARTS]
    whole = pl.BlockSpec((64, ROWS, 128), lambda j: (j, 0, 0))
    return pl.pallas_call(
        early_kernel,
        grid=(2,),
        in_specs=half * 2 + [pl.BlockSpec((64, 16, 128), lambda j: (j, 0, 0))],
        out_specs=whole,
        out_shape=jax.ShapeDtypeStruct((128, ROWS, 128), BF),
        compiler_params=pltpu.CompilerParams(vmem_limit_bytes=63 * 2**20),
        cost_estimate=pl.CostEstimate(flops=1, bytes_accessed=1024, transcendentals=0),
    )(*kept, *one, qkv)


def pack_kernel(early_ref, p_ref, q_ref, r_ref, qkv_ref, out_ref):
    rows = [ref[...].astype(F32).reshape(64, n, 128) for ref, n in zip((p_ref, q_ref, r_ref), PARTS)]
    rows.append(qkv_ref[...].astype(F32))
    out_ref[...] = (early_ref[...].astype(F32) + jnp.concatenate(rows, axis=1)).astype(BF)


def pack_call(early, two, qkv_two):
    whole = pl.BlockSpec((64, ROWS, 128), lambda j: (j, 0, 0))
    return pl.pallas_call(
        pack_kernel,
        grid=(2,),
        in_specs=[whole]
        + [pl.BlockSpec((64 * n, 128), lambda j: (j, 0)) for n in PARTS]
        + [pl.BlockSpec((64, 16, 128), lambda j: (j, 0, 0))],
        out_specs=whole,
        out_shape=jax.ShapeDtypeStruct((128, ROWS, 128), BF),
        compiler_params=pltpu.CompilerParams(vmem_limit_bytes=60 * 2**20),
        cost_estimate=pl.CostEstimate(flops=1, bytes_accessed=1024, transcendentals=0),
    )(early, *two, qkv_two)


def bits_of(s):
    return {n: (s >> i) & 1 for i, n in enumerate(("xh", "yl", "yh", "core", "xl", "zl", "zh"))}


def sum_kernel(got_ref, w_ref, g_ref, up_ref, down_ref, wo_ref, q_ref, k_ref, v_ref, gain_ref, *vec_refs):
    def total(keys, at, n):
        sums = {}
        for s in range(128):
            b = bits_of(s)
            k = tuple(b[name] for name in keys)
            v = got_ref[s].astype(F32)[at : at + n]
            sums[k] = sums[k] + v if k in sums else v
        return sums

    for (core, k1, k2), v in total(("core", "xl", "zl"), 0, 24).items():
        for u in range(3):
            at = core * 2048 + u * 512 + (2 * k1 + k2) * 128
            up_ref[:, at : at + 128] = v[8 * u : 8 * (u + 1)]
    for (core, k1, k2), v in total(("core", "zl", "yl"), 24, 24).items():
        at = core * 512 + (2 * k1 + k2) * 128
        down_ref[0:24, at : at + 128] = v
    for (core, k1, k2), v in total(("core", "yl", "xl"), 48, 24).items():
        at = (2 * k1 + k2) * 128
        up_ref[:, core * 2048 + 1536 + at : core * 2048 + 1536 + at + 128] = v[0:8]
        down_ref[24:32, core * 512 + at : core * 512 + at + 128] = v[8:16]
        wo_ref[:, core * 512 + at : core * 512 + at + 128] = v[16:24]
    weighted = jnp.zeros((8, 128), F32)
    vec = jnp.zeros((8, 128), F32)
    for (core, yh, yl, xh), v in total(("core", "yh", "yl", "xh"), 72, 16).items():
        b = 4 * yh + 2 * yl + xh
        at = slice(128 * b, 128 * (b + 1))
        for i, out in ((2, v_ref),) if core else ((0, q_ref), (1, k_ref)):
            part = v[8 * (i % 2) : 8 * (i % 2) + 8]
            out[:, at] = part
            weighted = weighted + part * w_ref[i, :, at]
        if core:
            vec = vec + v[8:16]
    gain_ref[...] = jnp.sum(weighted.T, axis=0, keepdims=True) / g_ref[...]
    at = 0
    for ref in vec_refs:
        n = ref.shape[1]
        ref[...] = vec[0:1, at : at + n]
        at += n


def sum_call(got, w_rows, gain_rows):
    shape = jax.ShapeDtypeStruct
    return pl.pallas_call(
        sum_kernel,
        in_specs=[VMEM] * 3,
        out_specs=[VMEM] * 12,
        out_shape=[shape((8, 4096), F32), shape((32, 1024), F32)]
        + [shape((8, 1024), F32)] * 4
        + [shape((1, n), F32) for n in (8, 32, 8, 8, 8, 8)],
        compiler_params=pltpu.CompilerParams(vmem_limit_bytes=16 * 2**20),
        cost_estimate=pl.CostEstimate(flops=10**7, bytes_accessed=3 * 2**20, transcendentals=0),
    )(got, w_rows, gain_rows)


def qkv_grads_kernel(info_ref, a0_ref, a1_ref, a2_ref, a3_ref, d_ref, vec_ref, keep_ref, send_ref):
    y, xh = info_ref[1] // 2, info_ref[1] % 2
    g = jnp.zeros((512, 384), F32)
    for back, ref in enumerate((a0_ref, a1_ref, a2_ref, a3_ref)):
        source = ((y + 4 - back) % 4) * 2
        d = jnp.concatenate([d_ref[source + xh], d_ref[source + 1 - xh]], axis=0)
        g = g + dot_tn(ref[...].reshape(256, 512), d)
    parts = [g[:, 128 * i : 128 * (i + 1)].reshape(64, 8, 128) for i in range(3)]
    first = lax.broadcasted_iota(jnp.int32, (64, 8, 128), 1) == 0
    parts.append(jnp.where(first, vec_ref[...].reshape(64, 1, 128), 0.0))
    one, two = (jnp.concatenate(parts[i : i + 2], axis=1) for i in (0, 2))
    mine = info_ref[0] == 0
    keep_ref[...] = jnp.where(mine, one, two).astype(BF)
    send_ref[...] = jnp.where(mine, two, one).astype(BF)


def qkv_grads_call(info, pairs, d_heads, vec):
    return pl.pallas_call(
        qkv_grads_kernel,
        grid=(2,),
        in_specs=[SMEM]
        + [pl.BlockSpec((2, 128, 512), lambda j: (0, 0, j))] * 4
        + [pl.BlockSpec((8, 128, 384), lambda j: (0, 0, 0)), pl.BlockSpec((64, 128), lambda j: (j, 0))],
        out_specs=[pl.BlockSpec((64, 16, 128), lambda j: (j, 0, 0))] * 2,
        out_shape=[jax.ShapeDtypeStruct((128, 16, 128), BF)] * 2,
        compiler_params=pltpu.CompilerParams(vmem_limit_bytes=63 * 2**20),
        cost_estimate=pl.CostEstimate(flops=1, bytes_accessed=1024, transcendentals=0),
    )(info, *pairs, d_heads, vec)


def input_kernel(d_ref, wq_ref, wk_ref, wv_ref, x_ref, g_ref, dmid_ref, out_ref):
    step = pl.program_id(0)
    acc = jnp.where(step == 0, 0.0, out_ref[...])
    for i, w_ref in enumerate((wq_ref, wk_ref, wv_ref)):
        d = jnp.concatenate([d_ref[j, :, 128 * i : 128 * (i + 1)] for j in range(2)], axis=1)
        acc = acc + dot_nt(d, w_ref[...])
    out_ref[...] = acc

    @pl.when(step == 3)
    def _():
        x = x_ref[...].astype(F32)
        r = lax.rsqrt(jnp.mean(x * x, axis=-1, keepdims=True) + EPSILON)
        dz = out_ref[...] * g_ref[...]
        inner = jnp.mean(dz * x, axis=-1, keepdims=True)
        out_ref[...] = dmid_ref[...] + r * dz - x * (r * r * r * inner)


def input_call(d_mine, wq, wk, wv, x, gain, dmid):
    whole = lambda shape: pl.BlockSpec(shape, lambda j: (0,) * len(shape))
    col = pl.BlockSpec((1024, 256), lambda j: (0, j))
    return pl.pallas_call(
        input_kernel,
        grid=(4,),
        in_specs=[pl.BlockSpec((2, 128, 384), lambda j: (j, 0, 0)), col, col, col, whole((128, 1024)), whole((1, 1024)), whole((128, 1024))],
        out_specs=whole((128, 1024)),
        out_shape=jax.ShapeDtypeStruct((128, 1024), F32),
        compiler_params=pltpu.CompilerParams(vmem_limit_bytes=16 * 2**20),
        cost_estimate=pl.CostEstimate(flops=2 * 128 * 1024 * 3072, bytes_accessed=7 * 2**20, transcendentals=0),
    )(d_mine, wq, wk, wv, x, gain, dmid)


def local(
    tokens, lengths, order, w_query, w_key, w_value, w_out, w_up, b_up, w_down, b_down,
    gain_attn_in, gain_attn_out, gain_mlp_in, gain_mlp_out, cotangent,
):
    z, xl, core, y, xh = (lax.axis_index(a) for a in ALL)
    my_blk = y * 2 + xh
    me = ((z * 2 + xl) * 2 + core) * 8 + my_blk
    info = jnp.stack([core, my_blk, z % 2, y % 2, xl]).astype(jnp.int32)
    row = lambda v: v.reshape(1, -1)
    order = order.T
    tie = lax.optimization_barrier

    qkv, attn_low = qkv_call(info, order, lengths, tokens, row(gain_attn_in), w_query, w_key, w_value)
    across = lax.ppermute(attn_low, ALL, ACROSS)
    qkv_heads = lax.all_to_all(qkv, BLK, 0, 0, tiled=True)

    late_lengths, across = tie((lengths, across))
    lengths_row = late_lengths[0]
    group_pos = jnp.arange(1024, dtype=jnp.int32)
    start = jnp.zeros((1024,), jnp.int32)
    end = jnp.int32(0)
    for e in range(6):
        end = end + lengths_row[e]
        start = jnp.where(group_pos >= end, end, start)
    cos_all, sin_all = rotary_tables(group_pos - start)

    qkv_heads, cos_all, sin_all, pair = tie((qkv_heads, cos_all, sin_all, jnp.stack([attn_low, across])))

    pairs = [pair] + [lax.ppermute(pair, ALL, to) for to in ALONG]
    out_heads, pos_qkv, lse = attend_call(order, lengths, qkv_heads)
    out_mine = lax.all_to_all(out_heads, BLK, 0, 0, tiled=True)
    out_mine, pairs[2] = tie((out_mine, pairs[2]))
    output, d_middle, d_out, send, keep, v_up, v_row = mlp_call(
        info, order, lengths, out_mine, tokens, cotangent, w_out, w_up, row(b_up), w_down, row(b_down),
        row(gain_attn_out), row(gain_mlp_in), row(gain_mlp_out),
    )
    send, keep, d_out, pairs = tie((send, keep, d_out, pairs))
    d_out_heads = lax.all_to_all(d_out, BLK, 0, 0, tiled=True)
    got = lax.ppermute(send, ALL, SWAP_CORES)
    sent = grads_call(1, info, send, keep, got)
    one = [lax.ppermute(p, ALL, to) for p, to in zip(sent, STEPS[0])]
    keep, _ = tie((keep, sent))
    kept = grads_call(0, info, send, keep, got)
    lse, kept = tie((lse, kept))
    d_heads = attend_back_call(order, lengths, pos_qkv, lse, cos_all, sin_all, d_out_heads)
    d_mine = lax.all_to_all(d_heads, BLK, 0, 0, tiled=True)
    added = add_call(kept, one)
    two = [lax.ppermute(p, ALL, to) for p, to in zip(added, STEPS[1])]
    v_up, v_row, _ = tie((v_up, v_row, added))
    vectors = jnp.concatenate(
        [v_up.reshape(128, 32)] + [v_row[i].reshape(128, 8) for i in (1, 3, 2, 0)] + [jnp.zeros((128, 64), F32)], axis=1
    )
    d_grads, _ = tie((d_heads, added))
    qkv_keep, qkv_send = qkv_grads_call(info, pairs, d_grads, vectors)
    qkv_send, d_mine = tie((qkv_send, d_mine))
    qkv_two = lax.ppermute(qkv_send, ALL, SWAP_CORES)
    qkv_keep, _ = tie((qkv_keep, d_mine))
    packed = pack_call(early_call(kept, one, qkv_keep), two, qkv_two)
    got_all = lax.all_to_all(packed, ALL, 0, 0, tiled=True)

    grad_tokens = input_call(d_mine, w_query, w_key, w_value, tokens, row(gain_attn_in), d_middle)
    my_rows = lambda w: lax.dynamic_slice_in_dim(w, me * 8, 8, 0).astype(F32)
    w_rows = jnp.stack([my_rows(w) for w in (w_query, w_key, w_value)])
    gain_rows = lax.dynamic_slice_in_dim(gain_attn_in, me * 8, 8, 0).reshape(1, 8)
    grad_w_up, grad_w_down, grad_w_out, grad_w_query, grad_w_key, grad_w_value, *vec = sum_call(got_all, w_rows, gain_rows)
    grad_gain_attn_in, grad_b_up, grad_b_down, grad_gain_attn_out, grad_gain_mlp_in, grad_gain_mlp_out = (
        v.reshape(-1) for v in vec
    )
    return (
        output, grad_tokens, grad_w_query, grad_w_key, grad_w_value, grad_w_out, grad_w_up, grad_b_up, grad_w_down,
        grad_b_down, grad_gain_attn_in, grad_gain_attn_out, grad_gain_mlp_in, grad_gain_mlp_out,
    )


def solution(mesh):
    split = Mesh(np.asarray(mesh.devices).reshape(4, 2, 2, 4, 2), ALL)
    every = P(ALL, None)
    flat = P(ALL)
    return jax.shard_map(
        local,
        mesh=split,
        in_specs=(every, P(("z", "xl", "core"), None)) + (P(),) * 13 + (every,),
        out_specs=(every,) * 7 + (flat, every) + (flat,) * 5,
        check_vma=False,
    )
```

```python
import functools
import math

import jax
import jax.numpy as jnp
import numpy as np
from jax import lax
from jax.experimental import pallas as pl
from jax.experimental.pallas import tpu as pltpu
from jax.sharding import Mesh
from jax.sharding import PartitionSpec as P

HEADS = 16
EPSILON = 1e-05
NEGATIVE = -1e30
ALL = ("z", "xl", "core", "y", "xh")
BLK = ("y", "xh")
BF = jnp.bfloat16
F32 = jnp.float32
TILES = ((0, 0, 256), (256, 0, 512), (512, 0, 768), (768, 512, 1024))


SMEM = pl.BlockSpec(memory_space=pltpu.SMEM)
VMEM = pl.BlockSpec(memory_space=pltpu.VMEM)
HBM = pl.BlockSpec(memory_space=pltpu.HBM)


def device_index(z, x, c, y):
    return (((z % 4) * 2 + (x % 4) % 2) * 2 + c) * 8 + (y % 4) * 2 + (x % 4) // 2


def pairs_of(f):
    return [
        (device_index(z, x, c, y), device_index(*f(z, x, c, y)))
        for z in range(4)
        for x in range(4)
        for c in range(2)
        for y in range(4)
    ]


def up(v):
    return v ^ 1


def down_pair(v):
    return ((v + 1) ^ 1) - 1


def flip(axis, by_core):
    way = (up, down_pair)

    def there(z, x, c, y):
        move = way[by_core[c]]
        return (
            move(z) if axis == "z" else z,
            move(x) if axis == "x" else x,
            c,
            move(y) if axis == "y" else y,
        )

    return pairs_of(there)


ACROSS = pairs_of(lambda z, x, c, y: (z, x + 2, c, y))
ALONG = [pairs_of(lambda z, x, c, y, by=by: (z, x, c, y + by)) for by in (1, 2, 3)]
SWAP_CORES = pairs_of(lambda z, x, c, y: (z, x, 1 - c, y))
PARTS = (24, 24, 24)
STEPS = (
    (flip("x", (0, 1)), flip("z", (0, 1)), flip("y", (0, 1))),
    (flip("z", (0, 1)), flip("y", (0, 1)), flip("x", (0, 1))),
)


def half_swap(x):
    n = x.shape[1]
    lane = lax.broadcasted_iota(jnp.int32, x.shape, 1) % 64
    return jnp.where(lane < 32, pltpu.roll(x, n - 32, 1), pltpu.roll(x, 32, 1))


def rotary_tables(relative):
    freqs = jnp.exp(jnp.arange(32, dtype=F32) * (-math.log(10000.0) / 32))
    angles = relative.astype(F32)[:, None] * freqs[None, :]
    c, s = jnp.cos(angles), jnp.sin(angles)
    return jnp.concatenate([c, c, c, c], axis=1), jnp.concatenate([-s, s, -s, s], axis=1)


def dot(a, b):
    return jnp.dot(a, b, preferred_element_type=F32)


def dot_nt(a, b):
    return lax.dot_general(a, b, (((1,), (1,)), ((), ())), preferred_element_type=F32)


def dot_tn(a, b):
    return lax.dot_general(a, b, (((0,), (0,)), ((), ())), preferred_element_type=F32)


def column_positions(blk, order_ref, len_ref):
    row = lax.broadcasted_iota(jnp.int32, (128, 1), 0)
    one, two = order_ref[0, blk], order_ref[1, blk]
    pos = jnp.where(row < 64, one * 64 + row, two * 64 + row - 64)
    start = jnp.zeros((128, 1), jnp.int32)
    end = jnp.int32(0)
    for e in range(6):
        end = end + len_ref[0, e]
        start = jnp.where(pos >= end, end, start)
    return pos, start, end


def qkv_kernel(order_ref, len_ref, x_ref, g_ref, wq_hbm, wk_hbm, wv_hbm, out_ref, a_ref, wq, wk, wv, sems):
    copies = [
        pltpu.make_async_copy(hbm.at[:, 512 * h : 512 * (h + 1)], w.at[:, 512 * h : 512 * (h + 1)], sems.at[2 * i + h])
        for i, (hbm, w) in enumerate(((wq_hbm, wq), (wk_hbm, wk), (wv_hbm, wv)))
        for h in range(2)
    ]
    for copy in copies:
        copy.start()
    x = x_ref[...].astype(F32)
    factor = lax.rsqrt(jnp.mean(x * x, axis=-1, keepdims=True) + EPSILON)
    a = (x * factor * g_ref[...]).astype(BF)
    a_ref[...] = a
    pos, start, _ = column_positions(lax.axis_index("y") * 2 + lax.axis_index("xh"), order_ref, len_ref)
    lane = lax.broadcasted_iota(jnp.int32, (1, 128), 1)
    freqs = jnp.exp((lane % 32).astype(F32) * (-math.log(10000.0) / 32))
    angles = (pos - start).astype(F32) * freqs
    cos = jnp.cos(angles)
    sine = jnp.sin(angles)
    sin = jnp.where(lane % 64 < 32, -sine, sine)
    cos = jnp.concatenate([cos] * 4, axis=1)
    sin = jnp.concatenate([sin] * 4, axis=1)
    for i, w in enumerate((wq, wk, wv)):
        for h in range(2):
            copies[2 * i + h].wait()
            y = dot(a, w[:, 512 * h : 512 * (h + 1)])
            if i < 2:
                y = y * cos + half_swap(y) * sin
            y = y.astype(BF)
            for j in range(4):
                out_ref[4 * h + j, :, 128 * i : 128 * (i + 1)] = y[:, 128 * j : 128 * (j + 1)]


def qkv_call(order, lengths, x, gain, wq, wk, wv):
    return pl.pallas_call(
        qkv_kernel,
        in_specs=[SMEM, SMEM, VMEM, VMEM, HBM, HBM, HBM],
        out_specs=[VMEM, VMEM],
        out_shape=[jax.ShapeDtypeStruct((8, 128, 384), BF), jax.ShapeDtypeStruct((128, 1024), BF)],
        scratch_shapes=[pltpu.VMEM((1024, 1024), BF)] * 3 + [pltpu.SemaphoreType.DMA((6,))],
        compiler_params=pltpu.CompilerParams(vmem_limit_bytes=60 * 2**20),
        cost_estimate=pl.CostEstimate(flops=2 * 128 * 1024 * 3072, bytes_accessed=7 * 2**20, transcendentals=0),
    )(order, lengths, x, gain, wq, wk, wv)


def allowed_mask(len_ref, q0, k0, k1):
    qpos = q0 + lax.broadcasted_iota(jnp.int32, (1, 256), 1)
    start = jnp.zeros((1, 256), jnp.int32)
    end = jnp.int32(0)
    for e in range(6):
        end = end + len_ref[0, e]
        start = jnp.where(qpos >= end, end, start)
    kpos = k0 + lax.broadcasted_iota(jnp.int32, (k1 - k0, 256), 0)
    return (kpos >= start) & (kpos <= qpos)


def attend_kernel(order_ref, len_ref, qkv_ref, out_ref, pos_ref, lse_ref, o_ref):
    for b in range(8):
        for j in range(2):
            at = pl.ds(pl.multiple_of(order_ref[j, b] * 64, 64), 64)
            pos_ref[at, :] = qkv_ref[b, 64 * j : 64 * (j + 1), :]
    first = lax.broadcasted_iota(jnp.int32, (1, 128), 1) < 64
    v_t = pos_ref[:, 256:384].T
    for q0, k0, k1 in TILES:
        q = pos_ref[q0 : q0 + 256, 0:128].astype(F32) * 0.125
        k = pos_ref[k0:k1, 128:256]
        mask = allowed_mask(len_ref, q0, k0, k1)
        outs = []
        for h in range(2):
            q_h = jnp.where(first if h == 0 else ~first, q, 0.0).astype(BF)
            s = jnp.where(mask, dot_nt(k, q_h), NEGATIVE)
            top = jnp.max(s, axis=0, keepdims=True)
            p = jnp.exp(s - top)
            total = jnp.sum(p, axis=0, keepdims=True)
            lse_ref[h : h + 1, q0 : q0 + 256] = top + jnp.log(total)
            p = (p * (1.0 / total)).astype(BF)
            outs.append(dot(v_t[64 * h : 64 * (h + 1), k0:k1], p))
        o_ref[q0 : q0 + 256, :] = jnp.concatenate(outs, axis=0).T.astype(BF)
    for b in range(8):
        for j in range(2):
            at = pl.ds(pl.multiple_of(order_ref[j, b] * 64, 64), 64)
            out_ref[b, 64 * j : 64 * (j + 1), :] = o_ref[at, :]


def attend_call(order, lengths, qkv):
    return pl.pallas_call(
        attend_kernel,
        in_specs=[SMEM, SMEM, VMEM],
        out_specs=[VMEM] * 3,
        out_shape=[
            jax.ShapeDtypeStruct((8, 128, 128), BF),
            jax.ShapeDtypeStruct((1024, 384), BF),
            jax.ShapeDtypeStruct((2, 1024), F32),
        ],
        scratch_shapes=[pltpu.VMEM((1024, 128), BF)],
        compiler_params=pltpu.CompilerParams(vmem_limit_bytes=24 * 2**20),
        cost_estimate=pl.CostEstimate(flops=2 * 10**9, bytes_accessed=3 * 2**20, transcendentals=2 * 10**6),
    )(order, lengths, qkv)


def attend_back_kernel(order_ref, len_ref, pos_ref, lse_ref, cos_ref, sin_ref, do_ref, out_ref, d_ref, dk_ref, dv_ref, dq_ref):
    for b in range(8):
        for j in range(2):
            at = pl.ds(pl.multiple_of(order_ref[j, b] * 64, 64), 64)
            d_ref[at, 0:128] = do_ref[b, 64 * j : 64 * (j + 1), :]
    first = lax.broadcasted_iota(jnp.int32, (1, 128), 1) < 64
    k_t = pos_ref[:, 128:256].T
    dk_ref[...] = jnp.zeros_like(dk_ref)
    dv_ref[...] = jnp.zeros_like(dv_ref)
    for q0, k0, k1 in TILES:
        q = pos_ref[q0 : q0 + 256, 0:128].astype(F32) * 0.125
        do = d_ref[q0 : q0 + 256, 0:128]
        k = pos_ref[k0:k1, 128:256]
        v = pos_ref[k0:k1, 256:384]
        mask = allowed_mask(len_ref, q0, k0, k1)
        outs = []
        for h in range(2):
            pick = first if h == 0 else ~first
            q_h = jnp.where(pick, q, 0.0).astype(BF)
            do_h = jnp.where(pick, do.astype(F32), 0.0).astype(BF)
            s = jnp.where(mask, dot_nt(k, q_h), NEGATIVE)
            p = jnp.exp(s - lse_ref[h : h + 1, q0 : q0 + 256])
            dp = dot_nt(v, do_h)
            delta = jnp.sum(p * dp, axis=0, keepdims=True)
            ds = (p * (dp - delta)).astype(BF)
            dv_ref[k0:k1, :] += dot(p.astype(BF), do_h)
            dk_ref[k0:k1, :] += dot(ds, q_h)
            outs.append(dot(k_t[64 * h : 64 * (h + 1), k0:k1], ds))
        dq_ref[q0 : q0 + 256, :] = jnp.concatenate(outs, axis=0).T * 0.125
    cos, sin = cos_ref[...], sin_ref[...]
    dq, dk = dq_ref[...], dk_ref[...]
    d_ref[:, 0:128] = (dq * cos - half_swap(dq) * sin).astype(BF)
    d_ref[:, 128:256] = (dk * cos - half_swap(dk) * sin).astype(BF)
    d_ref[:, 256:384] = dv_ref[...].astype(BF)
    for b in range(8):
        for j in range(2):
            at = pl.ds(pl.multiple_of(order_ref[j, b] * 64, 64), 64)
            out_ref[b, 64 * j : 64 * (j + 1), :] = d_ref[at, :]


def attend_back_call(order, lengths, pos, lse, cos, sin, d_out):
    return pl.pallas_call(
        attend_back_kernel,
        in_specs=[SMEM, SMEM, VMEM, VMEM, VMEM, VMEM, VMEM],
        out_specs=VMEM,
        out_shape=jax.ShapeDtypeStruct((8, 128, 384), BF),
        scratch_shapes=[
            pltpu.VMEM((1024, 384), BF),
            pltpu.VMEM((1024, 128), F32),
            pltpu.VMEM((1024, 128), F32),
            pltpu.VMEM((1024, 128), F32),
        ],
        compiler_params=pltpu.CompilerParams(vmem_limit_bytes=32 * 2**20),
        cost_estimate=pl.CostEstimate(flops=20000000000, bytes_accessed=1024, transcendentals=0),
    )(order, lengths, pos, lse, cos, sin, d_out)


ACT, M_AT, O_AT, DPRE, DD, DPROJ, SEND = 0, 4096, 5120, 6144, 8192, 8704, 9216
CHUNK = 1024


def mlp_kernel(info_ref, order_ref, len_ref, o_ref, x_ref, ct_ref, wo_hbm, wup_hbm, bup_ref, wdown_hbm, bdown_ref,
               g2_ref, g3_ref, g4_ref,
               out_ref, dmid_ref, do_ref, send_ref, keep_ref, vup_ref, vrow_ref,
               proj_ref, middle_ref, slope_ref, dd_ref, acc_ref, wo_ref, wup_ref, wdown_ref, sems):
    core = info_ref[0]
    count = 4096 // CHUNK
    copy_out = pltpu.make_async_copy(wo_hbm, wo_ref, sems.at[2 * count])
    copy_out.start()
    copies = []
    for i in range(count):
        at = slice(CHUNK * i, CHUNK * (i + 1))
        copies.append((
            pltpu.make_async_copy(wup_hbm.at[:, at], wup_ref.at[:, at], sems.at[2 * i]),
            pltpu.make_async_copy(wdown_hbm.at[at, :], wdown_ref.at[at, :], sems.at[2 * i + 1]),
        ))
        copies[-1][0].start()
        copies[-1][1].start()
    pos, _, end = column_positions(info_ref[1], order_ref, len_ref)
    valid = pos < end
    o = jnp.concatenate([o_ref[j] for j in range(8)], axis=1)
    send_ref[:, O_AT : O_AT + 1024] = o
    copy_out.wait()
    proj = dot(o, wo_ref[...])
    proj_ref[...] = proj
    r2 = lax.rsqrt(jnp.mean(proj * proj, axis=-1, keepdims=True) + EPSILON)
    middle = x_ref[...].astype(F32) + proj * r2 * g2_ref[...]
    middle_ref[...] = middle
    r3 = lax.rsqrt(jnp.mean(middle * middle, axis=-1, keepdims=True) + EPSILON)
    m = (middle * r3 * g3_ref[...]).astype(BF)
    send_ref[:, M_AT : M_AT + 1024] = m
    acc_ref[...] = jnp.zeros_like(acc_ref)
    root = math.sqrt(2.0 / math.pi)
    for i in range(4096 // CHUNK):
        at = slice(CHUNK * i, CHUNK * (i + 1))
        copies[i][0].wait()
        pre = dot(m, wup_ref[:, at]) + bup_ref[:, at]
        square = pre * pre
        t = jnp.tanh(root * (pre + 0.044715 * (square * pre)))
        half = 0.5 * (1.0 + t)
        act = (pre * half).astype(BF)
        slope_ref[:, at] = half + 0.5 * pre * (1.0 - t * t) * (root + (3.0 * 0.044715 * root) * square)
        send_ref[:, at] = act
        copies[i][1].wait()
        acc_ref[...] += dot(act, wdown_ref[at, :])
    down = acc_ref[...] + bdown_ref[...]
    r4 = lax.rsqrt(jnp.mean(down * down, axis=-1, keepdims=True) + EPSILON)
    out_ref[...] = jnp.where(valid, middle_ref[...] + down * r4 * g4_ref[...], 0.0).astype(BF)
    dy = jnp.where(valid, ct_ref[...].astype(F32), 0.0)
    dz = dy * down
    vrow_ref[0:1, :] = jnp.sum(dz * r4, axis=0, keepdims=True)
    inner = jnp.mean(dz * g4_ref[...], axis=-1, keepdims=True)
    dd = (r4 * g4_ref[...] * dy - down * (r4 * r4 * r4 * inner)).astype(BF)
    dd_ref[...] = dd
    vrow_ref[1:2, :] = jnp.sum(dd.astype(F32), axis=0, keepdims=True)
    send_ref[:, DD : DD + 512] = dd_ref[:, pl.ds(pl.multiple_of((1 - core) * 512, 512), 512)]
    keep_ref[:, 2048:2560] = dd_ref[:, pl.ds(pl.multiple_of(core * 512, 512), 512)]
    acc_ref[...] = jnp.zeros_like(acc_ref)
    for part in range(2):
        which = 1 - core if part == 0 else core
        for i in range(2048 // CHUNK):
            at = pl.ds(pl.multiple_of(which * 2048 + CHUNK * i, CHUNK), CHUNK)
            dact = dot_nt(dd, wdown_ref[at, :])
            dpre = (dact * slope_ref[:, at]).astype(BF)
            vup_ref[:, at] = jnp.sum(dpre.astype(F32), axis=0, keepdims=True)
            if part == 0:
                send_ref[:, DPRE + CHUNK * i : DPRE + CHUNK * (i + 1)] = dpre
            else:
                keep_ref[:, CHUNK * i : CHUNK * (i + 1)] = dpre
            acc_ref[...] += dot_nt(dpre, wup_ref[:, at])
    dm = acc_ref[...]
    middle = middle_ref[...]
    dz = dm * middle
    vrow_ref[2:3, :] = jnp.sum(dz * r3, axis=0, keepdims=True)
    inner = jnp.mean(dz * g3_ref[...], axis=-1, keepdims=True)
    dmid = dy + r3 * g3_ref[...] * dm - middle * (r3 * r3 * r3 * inner)
    dmid_ref[...] = dmid
    proj = proj_ref[...]
    dz = dmid * proj
    vrow_ref[3:4, :] = jnp.sum(dz * r2, axis=0, keepdims=True)
    inner = jnp.mean(dz * g2_ref[...], axis=-1, keepdims=True)
    dproj = (r2 * g2_ref[...] * dmid - proj * (r2 * r2 * r2 * inner)).astype(BF)
    dd_ref[...] = dproj
    send_ref[:, DPROJ : DPROJ + 512] = dd_ref[:, pl.ds(pl.multiple_of((1 - core) * 512, 512), 512)]
    keep_ref[:, 2560:3072] = dd_ref[:, pl.ds(pl.multiple_of(core * 512, 512), 512)]
    d_out = dot_nt(dproj, wo_ref[...]).astype(BF)
    for j in range(8):
        do_ref[j] = d_out[:, 128 * j : 128 * (j + 1)]


def mlp_call(*args):
    shape = jax.ShapeDtypeStruct
    return pl.pallas_call(
        mlp_kernel,
        in_specs=[SMEM] * 3 + [VMEM] * 3 + [HBM, HBM, VMEM, HBM] + [VMEM] * 4,
        out_specs=[VMEM] * 7,
        out_shape=[
            shape((128, 1024), BF), shape((128, 1024), F32), shape((8, 128, 128), BF), shape((128, SEND), BF),
            shape((128, 3072), BF), shape((1, 4096), F32), shape((4, 1024), F32),
        ],
        scratch_shapes=[
            pltpu.VMEM((128, 1024), F32), pltpu.VMEM((128, 1024), F32), pltpu.VMEM((128, 4096), F32),
            pltpu.VMEM((128, 1024), BF), pltpu.VMEM((128, 1024), F32),
            pltpu.VMEM((1024, 1024), BF), pltpu.VMEM((1024, 4096), BF), pltpu.VMEM((4096, 1024), BF),
            pltpu.SemaphoreType.DMA((2 * 4096 // CHUNK + 1,)),
        ],
        compiler_params=pltpu.CompilerParams(vmem_limit_bytes=60 * 2**20),
        cost_estimate=pl.CostEstimate(flops=4 * 128 * 9 * 2**20, bytes_accessed=20 * 2**20, transcendentals=2**19),
    )(*args)


def grad_parts(info_ref, relative, lefts, rights, outs, copies):
    b0, b1, b2 = info_ref[4], info_ref[2], info_ref[3]

    def left(at, n):
        return lefts[at : at + n, :]

    def cols(at, n):
        return rights[:, pl.ds(pl.multiple_of(at, 128), n)]

    eights = lambda g: [g[:, 128 * i : 128 * (i + 1)].reshape(128, 8, 128) for i in range(g.shape[1] // 128)]
    for k2 in range(2):
        block = 2 * (relative ^ b0) + k2
        rhs = jnp.concatenate([cols(u * 512 + block * 128, 128) for u in range(3)], axis=1)
        rows = eights(dot(left(M_AT, 1024), rhs))
        outs[0][k2 ^ b1] = jnp.concatenate(rows, axis=1).reshape(3072, 128).astype(BF)
    copies[0].start()
    rhs = cols(2048 + 256 * (relative ^ b1), 256)
    for half in range(2):
        g = dot(left(2048 * half, 2048), rhs)
        for k2 in range(2):
            part = g[:, 128 * k2 : 128 * (k2 + 1)].reshape(64, 32, 128)[:, 0:24]
            outs[1][k2 ^ b2, 1536 * half : 1536 * (half + 1), :] = part.reshape(1536, 128).astype(BF)
    copies[1].start()
    first = 256 * (relative ^ b2)
    g_up = eights(dot(left(M_AT, 1024), cols(3 * 512 + first, 256)))
    g_out = eights(dot(left(O_AT, 1024), cols(2560 + first, 256)))
    for half in range(2):
        g_down = dot(left(2048 * half, 2048), cols(2048 + first, 256))
        d = slice(64 * half, 64 * (half + 1))
        for k2 in range(2):
            tail = g_down[:, 128 * k2 : 128 * (k2 + 1)].reshape(64, 32, 128)[:, 24:32]
            rows = jnp.concatenate([g_up[k2][d], tail, g_out[k2][d]], axis=1)
            outs[2][k2 ^ b0, 1536 * half : 1536 * (half + 1), :] = rows.reshape(1536, 128).astype(BF)
    copies[2].start()


def turn(mine, theirs, lefts):
    for i in range(6144 // 512):
        at = slice(512 * i, 512 * (i + 1))
        lefts[at, 0:128] = mine[:, at].T
        lefts[at, 128:256] = theirs[:, at].T


def grads_kernel(relative, info_ref, mine_ref, keep_ref, theirs_ref, p_hbm, q_hbm, r_hbm, lefts, rights, p_ref, q_ref, r_ref, sems):
    turn(mine_ref, theirs_ref, lefts)
    rights[0:128, :] = keep_ref[...]
    rights[128:256, :] = theirs_ref[:, DPRE:SEND]
    copies = [
        pltpu.make_async_copy(ref, hbm, sems.at[i])
        for i, (ref, hbm) in enumerate(((p_ref, p_hbm), (q_ref, q_hbm), (r_ref, r_hbm)))
    ]
    grad_parts(info_ref, relative, lefts, rights, (p_ref, q_ref, r_ref), copies)
    for copy in copies:
        copy.wait()


PART_SHAPES = [jax.ShapeDtypeStruct((2, 128 * n, 128), BF) for n in PARTS]


def grads_call(relative, info, send, keep, got):
    return pl.pallas_call(
        functools.partial(grads_kernel, relative),
        in_specs=[SMEM, pl.BlockSpec((128, DPRE), lambda j: (0, 0)), VMEM, VMEM],
        grid=(1,),
        out_specs=[HBM] * 3,
        out_shape=PART_SHAPES,
        scratch_shapes=[pltpu.VMEM((6144, 256), BF), pltpu.VMEM((256, 3072), BF)]
        + [pltpu.VMEM((2, 128 * n, 128), BF) for n in PARTS]
        + [pltpu.SemaphoreType.DMA((3,))],
        compiler_params=pltpu.CompilerParams(vmem_limit_bytes=60 * 2**20),
        cost_estimate=pl.CostEstimate(flops=1, bytes_accessed=1024, transcendentals=0),
    )(info, send, keep, got)


ROWS = 88


def add_kernel(*refs):
    for k, a, out in zip(refs[0:3], refs[3:6], refs[6:9]):
        out[...] = k[0] + a[0]


def add_call(kept, one):
    return pl.pallas_call(
        add_kernel,
        grid=(2,),
        in_specs=[pl.BlockSpec((1, 64 * n, 128), lambda j: (1, j, 0)) for n in PARTS] * 2,
        out_specs=[pl.BlockSpec((64 * n, 128), lambda j: (j, 0)) for n in PARTS],
        out_shape=[jax.ShapeDtypeStruct((128 * n, 128), BF) for n in PARTS],
        compiler_params=pltpu.CompilerParams(vmem_limit_bytes=60 * 2**20),
        cost_estimate=pl.CostEstimate(flops=1, bytes_accessed=1024, transcendentals=0),
    )(*kept, *one)


def early_kernel(*refs):
    rows = []
    for k, a, n in zip(refs[0:3], refs[3:6], PARTS):
        rows.append((k[0].astype(F32) + a[0].astype(F32)).reshape(64, n, 128))
    rows.append(refs[6][...].astype(F32))
    refs[7][...] = jnp.concatenate(rows, axis=1).astype(BF)


def early_call(kept, one, qkv):
    half = [pl.BlockSpec((1, 64 * n, 128), lambda j: (0, j, 0)) for n in PARTS]
    whole = pl.BlockSpec((64, ROWS, 128), lambda j: (j, 0, 0))
    return pl.pallas_call(
        early_kernel,
        grid=(2,),
        in_specs=half * 2 + [pl.BlockSpec((64, 16, 128), lambda j: (j, 0, 0))],
        out_specs=whole,
        out_shape=jax.ShapeDtypeStruct((128, ROWS, 128), BF),
        compiler_params=pltpu.CompilerParams(vmem_limit_bytes=63 * 2**20),
        cost_estimate=pl.CostEstimate(flops=1, bytes_accessed=1024, transcendentals=0),
    )(*kept, *one, qkv)


def pack_kernel(early_ref, p_ref, q_ref, r_ref, qkv_ref, out_ref):
    rows = [ref[...].astype(F32).reshape(64, n, 128) for ref, n in zip((p_ref, q_ref, r_ref), PARTS)]
    rows.append(qkv_ref[...].astype(F32))
    out_ref[...] = (early_ref[...].astype(F32) + jnp.concatenate(rows, axis=1)).astype(BF)


def pack_call(early, two, qkv_two):
    whole = pl.BlockSpec((64, ROWS, 128), lambda j: (j, 0, 0))
    return pl.pallas_call(
        pack_kernel,
        grid=(2,),
        in_specs=[whole]
        + [pl.BlockSpec((64 * n, 128), lambda j: (j, 0)) for n in PARTS]
        + [pl.BlockSpec((64, 16, 128), lambda j: (j, 0, 0))],
        out_specs=whole,
        out_shape=jax.ShapeDtypeStruct((128, ROWS, 128), BF),
        compiler_params=pltpu.CompilerParams(vmem_limit_bytes=60 * 2**20),
        cost_estimate=pl.CostEstimate(flops=1, bytes_accessed=1024, transcendentals=0),
    )(early, *two, qkv_two)


def bits_of(s):
    return {n: (s >> i) & 1 for i, n in enumerate(("xh", "yl", "yh", "core", "xl", "zl", "zh"))}


def sum_kernel(got_ref, w_ref, g_ref, up_ref, down_ref, wo_ref, q_ref, k_ref, v_ref, gain_ref, *vec_refs):
    def total(keys, at, n):
        sums = {}
        for s in range(128):
            b = bits_of(s)
            k = tuple(b[name] for name in keys)
            v = got_ref[s].astype(F32)[at : at + n]
            sums[k] = sums[k] + v if k in sums else v
        return sums

    for (core, k1, k2), v in total(("core", "xl", "zl"), 0, 24).items():
        for u in range(3):
            at = core * 2048 + u * 512 + (2 * k1 + k2) * 128
            up_ref[:, at : at + 128] = v[8 * u : 8 * (u + 1)]
    for (core, k1, k2), v in total(("core", "zl", "yl"), 24, 24).items():
        at = core * 512 + (2 * k1 + k2) * 128
        down_ref[0:24, at : at + 128] = v
    for (core, k1, k2), v in total(("core", "yl", "xl"), 48, 24).items():
        at = (2 * k1 + k2) * 128
        up_ref[:, core * 2048 + 1536 + at : core * 2048 + 1536 + at + 128] = v[0:8]
        down_ref[24:32, core * 512 + at : core * 512 + at + 128] = v[8:16]
        wo_ref[:, core * 512 + at : core * 512 + at + 128] = v[16:24]
    weighted = jnp.zeros((8, 128), F32)
    vec = jnp.zeros((8, 128), F32)
    for (core, yh, yl, xh), v in total(("core", "yh", "yl", "xh"), 72, 16).items():
        b = 4 * yh + 2 * yl + xh
        at = slice(128 * b, 128 * (b + 1))
        for i, out in ((2, v_ref),) if core else ((0, q_ref), (1, k_ref)):
            part = v[8 * (i % 2) : 8 * (i % 2) + 8]
            out[:, at] = part
            weighted = weighted + part * w_ref[i, :, at]
        if core:
            vec = vec + v[8:16]
    gain_ref[...] = jnp.sum(weighted.T, axis=0, keepdims=True) / g_ref[...]
    at = 0
    for ref in vec_refs:
        n = ref.shape[1]
        ref[...] = vec[0:1, at : at + n]
        at += n


def sum_call(got, w_rows, gain_rows):
    shape = jax.ShapeDtypeStruct
    return pl.pallas_call(
        sum_kernel,
        in_specs=[VMEM] * 3,
        out_specs=[VMEM] * 12,
        out_shape=[shape((8, 4096), F32), shape((32, 1024), F32)]
        + [shape((8, 1024), F32)] * 4
        + [shape((1, n), F32) for n in (8, 32, 8, 8, 8, 8)],
        compiler_params=pltpu.CompilerParams(vmem_limit_bytes=16 * 2**20),
        cost_estimate=pl.CostEstimate(flops=10**7, bytes_accessed=3 * 2**20, transcendentals=0),
    )(got, w_rows, gain_rows)


def qkv_grads_kernel(info_ref, a0_ref, a1_ref, a2_ref, a3_ref, d_ref, vec_ref, keep_ref, send_ref):
    y, xh = info_ref[1] // 2, info_ref[1] % 2
    g = jnp.zeros((512, 384), F32)
    for back, ref in enumerate((a0_ref, a1_ref, a2_ref, a3_ref)):
        source = ((y + 4 - back) % 4) * 2
        d = jnp.concatenate([d_ref[source + xh], d_ref[source + 1 - xh]], axis=0)
        g = g + dot_tn(ref[...].reshape(256, 512), d)
    parts = [g[:, 128 * i : 128 * (i + 1)].reshape(64, 8, 128) for i in range(3)]
    first = lax.broadcasted_iota(jnp.int32, (64, 8, 128), 1) == 0
    parts.append(jnp.where(first, vec_ref[...].reshape(64, 1, 128), 0.0))
    one, two = (jnp.concatenate(parts[i : i + 2], axis=1) for i in (0, 2))
    mine = info_ref[0] == 0
    keep_ref[...] = jnp.where(mine, one, two).astype(BF)
    send_ref[...] = jnp.where(mine, two, one).astype(BF)


def qkv_grads_call(info, pairs, d_heads, vec):
    return pl.pallas_call(
        qkv_grads_kernel,
        grid=(2,),
        in_specs=[SMEM]
        + [pl.BlockSpec((2, 128, 512), lambda j: (0, 0, j))] * 4
        + [pl.BlockSpec((8, 128, 384), lambda j: (0, 0, 0)), pl.BlockSpec((64, 128), lambda j: (j, 0))],
        out_specs=[pl.BlockSpec((64, 16, 128), lambda j: (j, 0, 0))] * 2,
        out_shape=[jax.ShapeDtypeStruct((128, 16, 128), BF)] * 2,
        compiler_params=pltpu.CompilerParams(vmem_limit_bytes=63 * 2**20),
        cost_estimate=pl.CostEstimate(flops=1, bytes_accessed=1024, transcendentals=0),
    )(info, *pairs, d_heads, vec)


def input_kernel(d_ref, wq_ref, wk_ref, wv_ref, x_ref, g_ref, dmid_ref, out_ref):
    step = pl.program_id(0)
    acc = jnp.where(step == 0, 0.0, out_ref[...])
    for i, w_ref in enumerate((wq_ref, wk_ref, wv_ref)):
        d = jnp.concatenate([d_ref[j, :, 128 * i : 128 * (i + 1)] for j in range(2)], axis=1)
        acc = acc + dot_nt(d, w_ref[...])
    out_ref[...] = acc

    @pl.when(step == 3)
    def _():
        x = x_ref[...].astype(F32)
        r = lax.rsqrt(jnp.mean(x * x, axis=-1, keepdims=True) + EPSILON)
        dz = out_ref[...] * g_ref[...]
        inner = jnp.mean(dz * x, axis=-1, keepdims=True)
        out_ref[...] = dmid_ref[...] + r * dz - x * (r * r * r * inner)


def input_call(d_mine, wq, wk, wv, x, gain, dmid):
    whole = lambda shape: pl.BlockSpec(shape, lambda j: (0,) * len(shape))
    col = pl.BlockSpec((1024, 256), lambda j: (0, j))
    return pl.pallas_call(
        input_kernel,
        grid=(4,),
        in_specs=[pl.BlockSpec((2, 128, 384), lambda j: (j, 0, 0)), col, col, col, whole((128, 1024)), whole((1, 1024)), whole((128, 1024))],
        out_specs=whole((128, 1024)),
        out_shape=jax.ShapeDtypeStruct((128, 1024), F32),
        compiler_params=pltpu.CompilerParams(vmem_limit_bytes=16 * 2**20),
        cost_estimate=pl.CostEstimate(flops=2 * 128 * 1024 * 3072, bytes_accessed=7 * 2**20, transcendentals=0),
    )(d_mine, wq, wk, wv, x, gain, dmid)


def local(
    tokens, lengths, order, w_query, w_key, w_value, w_out, w_up, b_up, w_down, b_down,
    gain_attn_in, gain_attn_out, gain_mlp_in, gain_mlp_out, cotangent,
):
    z, xl, core, y, xh = (lax.axis_index(a) for a in ALL)
    my_blk = y * 2 + xh
    me = ((z * 2 + xl) * 2 + core) * 8 + my_blk
    info = jnp.stack([core, my_blk, z % 2, y % 2, xl]).astype(jnp.int32)
    row = lambda v: v.reshape(1, -1)
    order = order.T
    tie = lax.optimization_barrier

    qkv, attn_low = qkv_call(order, lengths, tokens, row(gain_attn_in), w_query, w_key, w_value)
    across = lax.ppermute(attn_low, ALL, ACROSS)
    qkv_heads = lax.all_to_all(qkv, BLK, 0, 0, tiled=True)

    late_lengths, across = tie((lengths, across))
    lengths_row = late_lengths[0]
    group_pos = jnp.arange(1024, dtype=jnp.int32)
    start = jnp.zeros((1024,), jnp.int32)
    end = jnp.int32(0)
    for e in range(6):
        end = end + lengths_row[e]
        start = jnp.where(group_pos >= end, end, start)
    cos_all, sin_all = rotary_tables(group_pos - start)

    qkv_heads, cos_all, sin_all, pair = tie((qkv_heads, cos_all, sin_all, jnp.stack([attn_low, across])))

    pairs = [pair] + [lax.ppermute(pair, ALL, to) for to in ALONG]
    out_heads, pos_qkv, lse = attend_call(order, lengths, qkv_heads)
    out_mine = lax.all_to_all(out_heads, BLK, 0, 0, tiled=True)
    out_mine, pairs[2] = tie((out_mine, pairs[2]))
    output, d_middle, d_out, send, keep, v_up, v_row = mlp_call(
        info, order, lengths, out_mine, tokens, cotangent, w_out, w_up, row(b_up), w_down, row(b_down),
        row(gain_attn_out), row(gain_mlp_in), row(gain_mlp_out),
    )
    send, keep, d_out, pairs = tie((send, keep, d_out, pairs))
    d_out_heads = lax.all_to_all(d_out, BLK, 0, 0, tiled=True)
    got = lax.ppermute(send, ALL, SWAP_CORES)
    sent = grads_call(1, info, send, keep, got)
    one = [lax.ppermute(p, ALL, to) for p, to in zip(sent, STEPS[0])]
    keep, _ = tie((keep, sent))
    kept = grads_call(0, info, send, keep, got)
    lse, kept = tie((lse, kept))
    d_heads = attend_back_call(order, lengths, pos_qkv, lse, cos_all, sin_all, d_out_heads)
    d_mine = lax.all_to_all(d_heads, BLK, 0, 0, tiled=True)
    added = add_call(kept, one)
    two = [lax.ppermute(p, ALL, to) for p, to in zip(added, STEPS[1])]
    v_up, v_row, _ = tie((v_up, v_row, added))
    vectors = jnp.concatenate(
        [v_up.reshape(128, 32)] + [v_row[i].reshape(128, 8) for i in (1, 3, 2, 0)] + [jnp.zeros((128, 64), F32)], axis=1
    )
    d_grads, _ = tie((d_heads, added))
    qkv_keep, qkv_send = qkv_grads_call(info, pairs, d_grads, vectors)
    qkv_send, d_mine = tie((qkv_send, d_mine))
    qkv_two = lax.ppermute(qkv_send, ALL, SWAP_CORES)
    qkv_keep, _ = tie((qkv_keep, d_mine))
    packed = pack_call(early_call(kept, one, qkv_keep), two, qkv_two)
    got_all = lax.all_to_all(packed, ALL, 0, 0, tiled=True)

    grad_tokens = input_call(d_mine, w_query, w_key, w_value, tokens, row(gain_attn_in), d_middle)
    my_rows = lambda w: lax.dynamic_slice_in_dim(w, me * 8, 8, 0).astype(F32)
    w_rows = jnp.stack([my_rows(w) for w in (w_query, w_key, w_value)])
    gain_rows = lax.dynamic_slice_in_dim(gain_attn_in, me * 8, 8, 0).reshape(1, 8)
    grad_w_up, grad_w_down, grad_w_out, grad_w_query, grad_w_key, grad_w_value, *vec = sum_call(got_all, w_rows, gain_rows)
    grad_gain_attn_in, grad_b_up, grad_b_down, grad_gain_attn_out, grad_gain_mlp_in, grad_gain_mlp_out = (
        v.reshape(-1) for v in vec
    )
    return (
        output, grad_tokens, grad_w_query, grad_w_key, grad_w_value, grad_w_out, grad_w_up, grad_b_up, grad_w_down,
        grad_b_down, grad_gain_attn_in, grad_gain_attn_out, grad_gain_mlp_in, grad_gain_mlp_out,
    )


def solution(mesh):
    split = Mesh(np.asarray(mesh.devices).reshape(4, 2, 2, 4, 2), ALL)
    every = P(ALL, None)
    flat = P(ALL)
    return jax.shard_map(
        local,
        mesh=split,
        in_specs=(every, P(("z", "xl", "core"), None)) + (P(),) * 13 + (every,),
        out_specs=(every,) * 7 + (flat, every) + (flat,) * 5,
        check_vma=False,
    )
```
